128 devices in a mesh: gx: 16 (over x_hi, z, core), gy: 8 (over y, x_lo).
Axes of the slice: x: 4 (x_hi: 2, x_lo: 2; x = x_hi * 2 + x_lo), y: 4, z: 4, core: 2. Of those that a mesh axis runs over, the one named last changes fastest.
Arguments:
- populations: float32 [19, 128, 128, 128], P(None, 'gx', 'gy'), may hold values from 0 to 1.25, as said below
- solid_mask: int32 [128, 128, 128], P('gx', 'gy'), may hold values 0 or 1
- wall_class: int32 [128, 128, 128], P('gx', 'gy'), may hold values from 0 to 7
- wall_table: float32 [8], replicated, may hold values from 0.2 to 0.9
- relax_rates: float32 [19], replicated, may hold values from 0.7 to 1.6
- pop_cotangent: float32 [19, 128, 128, 128], P(None, 'gx', 'gy'), may hold values from -6 to 6
Outputs:
- pop_adjoint: float32 [19, 128, 128, 128], P(None, 'gx', 'gy')
- density_adjoint: float32 [2, 128, 128, 128], P(None, 'gx', 'gy')
- wet_gradient: float32 [128, 128, 128], P('gx', 'gy')
The draws below stay inside these ranges and needn't reach their ends.
Inputs may be any that keep to these rules, and one draw needn't show every extreme that they name: `populations`: every population is positive.
All inputs are finite; a program needn't handle non-finite values. No bound on the sum of `solid_mask` on one device may be relied on, other than what follows from the above.
Results may differ from the reference program's by a relative error of at most 0.00014.
Values sent between devices are 32-bit elements; how exact they have to be, the bound alone decides.
A program may use at most 64 MiB of HBM per device.

```python
import math
import jax
import jax.numpy as jnp
import numpy as np
from jax import lax

WALL_CLASSES = 8
NX = 128
NY = 128
NZ = 128


WEIGHT_TABLE = [1.0 / 3.0] + [1.0 / 18.0] * 6 + [1.0 / 36.0] * 12


def draw_populations(key, part):
    key = jax.random.fold_in(key, 7)
    key_density, key_ripple = jax.random.split(key)
    density = jnp.exp(jax.random.uniform(key_density, (NX, NY, NZ), jnp.float32, math.log(0.4), math.log(2.5)))
    ripple = jax.random.uniform(key_ripple, (19, NX, NY, NZ), jnp.float32, -0.3, 0.3)
    return jnp.asarray(WEIGHT_TABLE, jnp.float32)[:, None, None, None] * density[None] * (1.0 + ripple)


def with_ends(drawn, rng, smallest, top_value):
    longest = drawn.shape.index(max(drawn.shape))
    spots = []
    for shift in (0, 1):
        where = [jax.random.randint(jax.random.fold_in(rng, axis), (), 0, length) for axis, length in enumerate(drawn.shape)]
        where[longest] = (where[longest] + shift) % drawn.shape[longest]
        spots.append(tuple(where))
    return drawn.at[spots[0]].set(smallest).at[spots[1]].set(top_value)


def shard_levels(stream_key, dims, shards, low, largest):
    loudness, own = 1.0, jax.random.fold_in(stream_key, 6)
    for dim, shards_of in shards:
        steps = jnp.exp(jax.random.uniform(jax.random.fold_in(own, dim), (shards_of,), jnp.float32, low / len(shards), largest / len(shards)))
        loudness = loudness * jnp.repeat(steps, dims[dim] // shards_of).reshape([-1 if axis == dim else 1 for axis in range(len(dims))])
    return loudness


def normal_values(rng, extent, deviation, most, shards=(), kind=jnp.bfloat16):
    entries = deviation * jax.random.normal(rng, extent, jnp.float32)
    if shards:
        entries = entries * shard_levels(rng, extent, shards, -0.22, 0.18)
    return jnp.clip(entries, -most, most).astype(kind)


def setup_inputs(seed: int = 0) -> dict:
    splits = jax.random.split(jax.random.key(seed), 7)
    return {
        "populations": draw_populations(jax.random.fold_in(splits[6], 71), 0),
        "solid_mask": with_ends((jax.random.randint(splits[1], (NX, NY, NZ), 0, 4) < 1).astype(jnp.int32), jax.random.fold_in(splits[1], 1), 0, 1),
        "wall_class": with_ends(jax.random.randint(splits[2], (NX, NY, NZ), 0, WALL_CLASSES), jax.random.fold_in(splits[2], 1), 0, WALL_CLASSES - 1).astype(jnp.int32),
        "wall_table": jnp.clip(jax.random.uniform(splits[3], (WALL_CLASSES,), jnp.float32, 0.2, 0.9), 0.2, 0.9),
        "relax_rates": jnp.clip(jnp.exp(jax.random.uniform(splits[4], (19,), jnp.float32, math.log(0.7), math.log(1.6))), 0.7, 1.6),
        "pop_cotangent": normal_values(splits[5], (19, NX, NY, NZ), 1.0, 6.0, ((1, 16), (2, 8)), jnp.float32),
    }


VELOCITY = np.array([[0, 0, 0], [1, 0, 0], [-1, 0, 0], [0, 1, 0], [0, -1, 0], [0, 0, 1], [0, 0, -1], [1, 1, 0], [-1, -1, 0], [1, -1, 0], [-1, 1, 0], [1, 0, 1], [-1, 0, -1], [1, 0, -1], [-1, 0, 1], [0, 1, 1], [0, -1, -1], [0, 1, -1], [0, -1, 1]])
OPPOSITE = np.array([0, 2, 1, 4, 3, 6, 5, 8, 7, 10, 9, 12, 11, 14, 13, 16, 15, 18, 17])
WEIGHTS = [1.0 / 3.0] + [1.0 / 18.0] * 6 + [1.0 / 36.0] * 12
COUPLING = -5.0

def moment_rows():
    columns = []
    for entry in VELOCITY:
        first, second, third = (int(entry[0]), int(entry[1]), int(entry[2]))
        columns.append([1, first, second, third, first * second, first * third, second * third, first * first, second * second, third * third, first * second * second, first * third * third, second * first * first, second * third * third, third * first * first, third * second * second, first * first * second * second, first * first * third * third, second * second * third * third])
    return [[float(columns[column][row]) for column in range(19)] for row in range(19)]

def invert_table(matrix):
    count = len(matrix)
    table = [list(matrix[row]) + [1.0 if other == row else 0.0 for other in range(count)] for row in range(count)]
    for column in range(count):
        pivot = column
        for candidate in range(column + 1, count):
            if abs(table[candidate][column]) > abs(table[pivot][column]):
                pivot = candidate
        table[column], table[pivot] = (table[pivot], table[column])
        leader = table[column][column]
        table[column] = [value / leader for value in table[column]]
        for target in range(count):
            if target != column:
                factor = table[target][column]
                if factor != 0.0:
                    table[target] = [left - factor * right for left, right in zip(table[target], table[column])]
    return [row_values[count:] for row_values in table]

def collide(populations_now, density, potential, pulling, solid_mask, relax_rates):
    highest = lax.Precision.HIGHEST
    lattice = jnp.asarray(VELOCITY, jnp.float32)
    weight = jnp.asarray(WEIGHTS, jnp.float32)[:, None, None, None]
    forcing = -COUPLING * potential[None] * pulling
    momentum = jnp.einsum('ia,ixyz->axyz', lattice, populations_now, precision=highest)
    velocity = (momentum + 0.5 * forcing) / density[None]
    projected = jnp.einsum('ia,axyz->ixyz', lattice, velocity, precision=highest)
    kinetic = lax.optimization_barrier(jnp.sum(velocity * velocity, axis=0))
    equilibrium = weight * density[None] * (1.0 + 3.0 * projected + 4.5 * projected * projected - 1.5 * kinetic[None])
    pushed = jnp.einsum('ia,axyz->ixyz', lattice, forcing, precision=highest)
    power_term = lax.optimization_barrier(jnp.sum(velocity * forcing, axis=0))
    source = weight * (3.0 * (pushed - power_term[None]) + 9.0 * projected * pushed)
    moment_list = moment_rows()
    moment = jnp.asarray(moment_list, jnp.float32)
    inverse = jnp.asarray(invert_table(moment_list), jnp.float32)
    kernel = jnp.dot(inverse * relax_rates[None, :], moment, precision=highest)
    collided = populations_now + source - jnp.einsum('ij,jxyz->ixyz', kernel, populations_now - equilibrium + 0.5 * source, precision=highest)
    bounced = populations_now[OPPOSITE]
    return jnp.where(solid_mask[None] == 1, bounced, collided)

def neighbour_pull(padded, height, breadth):
    components = [0.0, 0.0, 0.0]
    for direction in range(1, 19):
        move_first, move_second, move_third = (int(entry) for entry in VELOCITY[direction])
        portion = padded[1 + move_first:1 + move_first + height, 1 + move_second:1 + move_second + breadth]
        portion = jnp.roll(portion, -move_third, axis=2)
        for axis_number, entry in enumerate((move_first, move_second, move_third)):
            if entry != 0:
                components[axis_number] = components[axis_number] + float(WEIGHTS[direction] * entry) * portion
    return jnp.stack(components)

def advance(populations_now, shift_density, wall_value, solid_mask, relax_rates):
    density = lax.optimization_barrier(jnp.sum(populations_now, axis=0)) + shift_density
    potential = jnp.where(solid_mask == 1, wall_value, 1.0 - jnp.exp(-density))
    padded = jnp.pad(potential, ((1, 1), (1, 1), (0, 0)), mode='wrap')
    pulling = neighbour_pull(padded, potential.shape[0], potential.shape[1])
    post = collide(populations_now, density, potential, pulling, solid_mask, relax_rates)
    shifted = []
    for direction in range(19):
        move_first, move_second, move_third = (int(entry) for entry in VELOCITY[direction])
        shifted.append(jnp.roll(post[direction], (move_first, move_second, move_third), axis=(0, 1, 2)))
    return jnp.stack(shifted)

def reference(populations, solid_mask, wall_class, wall_table, relax_rates, pop_cotangent):
    wall_value = wall_table[wall_class]
    zero_shift = jnp.zeros(populations.shape[1:], jnp.float32)
    states = [populations]
    states.append(advance(populations, zero_shift, wall_value, solid_mask, relax_rates))
    adjoint = pop_cotangent
    densities = [zero_shift, zero_shift]
    wet_total = jnp.zeros(populations.shape[1:], jnp.float32)
    for sweep in (1, 0):

        def local_step(first_arg, second_arg, third_arg):
            return advance(first_arg, second_arg, third_arg, solid_mask, relax_rates)
        unused, pullback = jax.vjp(local_step, states[sweep], zero_shift, wall_value)
        adjoint, density_bar, wall_bar = pullback(adjoint)
        densities[sweep] = density_bar
        wet_total = wet_total + wall_bar
    return (adjoint, jnp.stack(densities), wet_total)
```

```python
import functools

import jax
import jax.numpy as jnp
from jax import lax
from jax.experimental import pallas as pl
from jax.experimental.pallas import tpu as pltpu
from jax.sharding import PartitionSpec as P

MESH = pl.DeviceIdType.MESH
VELOCITY = [
    (0, 0, 0),
    (1, 0, 0), (-1, 0, 0), (0, 1, 0), (0, -1, 0), (0, 0, 1), (0, 0, -1),
    (1, 1, 0), (-1, -1, 0), (1, -1, 0), (-1, 1, 0),
    (1, 0, 1), (-1, 0, -1), (1, 0, -1), (-1, 0, 1),
    (0, 1, 1), (0, -1, -1), (0, 1, -1), (0, -1, 1),
]
FACE_W, EDGE_W = 1.0 / 18.0, 1.0 / 36.0
AXES = (0, 1, 2)
PAIRS = ((0, 1), (0, 2), (1, 2))
CROSS = {(0, 1): 4, (0, 2): 5, (1, 2): 6}
QUAD = {(0, 1): 16, (0, 2): 17, (1, 2): 18}
CUBIC = {(0, 1): 10, (0, 2): 11, (1, 0): 12, (1, 2): 13, (2, 0): 14, (2, 1): 15}
EDGE = {(0, 1): 7, (0, 2): 11, (1, 2): 15}
ODD = (1, 2, 3, 10, 11, 12, 13, 14, 15)
OTHERS = {0: (1, 2), 1: (0, 2), 2: (0, 1)}
DIRS = ((-1, -1), (-1, 1), (1, -1), (1, 1), (-1, 0), (1, 0), (0, -1), (0, 1))
CLASSES = [(a, b) for a in (-1, 0, 1) for b in (-1, 0, 1)]
SLOT = {c: n for n, c in enumerate(CLASSES)}
MEMBERS = {c: [i for i, v in enumerate(VELOCITY) if v[:2] == c] for c in CLASSES}
H, B, Z = 8, 16, 128
Y0, Y1 = 8, 24
MID = slice(Y0, Y1)
ROWS = (16, 112, 104, 152, 48)


def quad(a, b):
    return QUAD[(min(a, b), max(a, b))]


def cross(a, b):
    return CROSS[(min(a, b), max(a, b))]


def roll_z(v, shift):
    return v if shift == 0 else pltpu.roll(v, shift % Z, v.ndim - 1)


def moments(f):
    m = [None] * 19
    s = [f[1 + 2 * a] + f[2 + 2 * a] for a in AXES]
    d = [f[1 + 2 * a] - f[2 + 2 * a] for a in AXES]
    for a, b in PAIRS:
        e = EDGE[a, b]
        al, ad = f[e] + f[e + 1], f[e] - f[e + 1]
        be, bd = f[e + 2] + f[e + 3], f[e + 2] - f[e + 3]
        m[CROSS[a, b]] = al - be
        m[QUAD[a, b]] = al + be
        m[CUBIC[a, b]] = ad + bd
        m[CUBIC[b, a]] = ad - bd
    for a in AXES:
        b, c = OTHERS[a]
        m[1 + a] = d[a] + (m[CUBIC[a, b]] + m[CUBIC[a, c]])
        m[7 + a] = s[a] + (m[quad(a, b)] + m[quad(a, c)])
    m[0] = (f[0] + s[0]) + (s[1] + s[2]) + (m[16] + m[17] + m[18])
    return m


def from_moments(p):
    f = [None] * 19
    for a in AXES:
        b, c = OTHERS[a]
        s = 0.5 * (p[7 + a] - (p[quad(a, b)] + p[quad(a, c)]))
        d = 0.5 * (p[1 + a] - (p[CUBIC[a, b]] + p[CUBIC[a, c]]))
        f[1 + 2 * a], f[2 + 2 * a] = s + d, s - d
    for a, b in PAIRS:
        e = EDGE[a, b]
        q, r = 0.25 * p[QUAD[a, b]], 0.25 * p[CROSS[a, b]]
        t, w = 0.25 * p[CUBIC[a, b]], 0.25 * p[CUBIC[b, a]]
        up, down, plus, minus = q + r, q - r, t + w, t - w
        f[e], f[e + 1], f[e + 2], f[e + 3] = up + plus, up - plus, down + minus, down - minus
    f[0] = p[0] - (p[7] + p[8] + p[9]) + (p[16] + p[17] + p[18])
    return f


def from_moments_t(lam):
    mu = [None] * 19
    mu[0] = lam[0]
    s = [0.5 * (lam[1 + 2 * a] + lam[2 + 2 * a]) for a in AXES]
    d = [0.5 * (lam[1 + 2 * a] - lam[2 + 2 * a]) for a in AXES]
    for a in AXES:
        mu[1 + a] = d[a]
        mu[7 + a] = s[a] - lam[0]
    for a, b in PAIRS:
        e = EDGE[a, b]
        al, ad = lam[e] + lam[e + 1], lam[e] - lam[e + 1]
        be, bd = lam[e + 2] + lam[e + 3], lam[e + 2] - lam[e + 3]
        mu[QUAD[a, b]] = 0.25 * (al + be) - s[a] - mu[7 + b]
        mu[CROSS[a, b]] = 0.25 * (al - be)
        mu[CUBIC[a, b]] = 0.25 * (ad + bd) - d[a]
        mu[CUBIC[b, a]] = 0.25 * (ad - bd) - d[b]
    return mu


def moments_t(nu):
    f = [None] * 19
    f[0] = nu[0]
    for a in AXES:
        s = nu[0] + nu[7 + a]
        f[1 + 2 * a], f[2 + 2 * a] = s + nu[1 + a], s - nu[1 + a]
    for a, b in PAIRS:
        e = EDGE[a, b]
        even = (nu[0] + nu[7 + a]) + (nu[7 + b] + nu[QUAD[a, b]])
        up, down = even + nu[CROSS[a, b]], even - nu[CROSS[a, b]]
        p, q = nu[1 + a] + nu[CUBIC[a, b]], nu[1 + b] + nu[CUBIC[b, a]]
        f[e], f[e + 1], f[e + 2], f[e + 3] = up + (p + q), up - (p + q), down + (p - q), down - (p - q)
    return f


def collide(f, psi, pull, inv, solid, rate):
    m = moments(f)
    rho = m[0]
    force = [5.0 * psi * g for g in pull]
    u = [(m[1 + a] + 0.5 * force[a]) * inv for a in AXES]
    n = [m[1 + a] - 0.5 * force[a] for a in AXES]
    p = [None] * 19
    p[0] = rho
    w = [u[a] * n[a] for a in AXES]
    t = [u[a] * force[a] for a in AXES]
    third = rho * (1.0 / 3.0)
    ninth = rho * (1.0 / 9.0)
    for a in AXES:
        p[1 + a] = m[1 + a] + force[a]
        k = 7 + a
        p[k] = m[k] + rate[k] * (third + w[a] - m[k]) + 2.0 * t[a]
    m3 = [m[1 + a] * (1.0 / 3.0) for a in AXES]
    f3 = [force[a] * (1.0 / 3.0) for a in AXES]
    for (a, b), k in CUBIC.items():
        p[k] = m[k] + rate[k] * (m3[a] - m[k]) + f3[a]
    w3 = [(1.0 / 3.0) * v for v in w]
    t3 = [(1.0 / 3.0) * v for v in t]
    for a, b in PAIRS:
        c = 3 - a - b
        k = CROSS[a, b]
        p[k] = m[k] + rate[k] * (0.5 * (u[b] * n[a] + u[a] * n[b]) - m[k]) + (u[a] * force[b] + u[b] * force[a])
        k = QUAD[a, b]
        p[k] = (
            m[k]
            + rate[k] * (ninth + (w3[a] + w3[b]) - 0.5 * w3[c] - m[k])
            + (2.0 * (t3[a] + t3[b]) - t3[c])
        )
    for k in range(1, 19):
        p[k] = jnp.where(solid, -m[k] if k in ODD else m[k], p[k])
    return from_moments(p), u, force


def collide_adjoint(lam, u, force, inv, solid, rate):
    mu = from_moments_t(lam)
    e, nu, g = [None] * 19, [None] * 19, [None] * 19
    for k in (0,) + tuple(range(4, 19)):
        e[k] = rate[k] * mu[k]
        nu[k] = mu[k] - e[k]
        g[k] = mu[k] - 0.5 * e[k]

    def diagonal(v):
        out = []
        for a in AXES:
            b, c = OTHERS[a]
            out.append(2.0 * v[7 + a] + (2.0 / 3.0) * (v[quad(a, b)] + v[quad(a, c)]) - (1.0 / 3.0) * v[quad(b, c)])
        return out

    def times(diag, v, x):
        out = []
        for a in AXES:
            b, c = OTHERS[a]
            out.append(diag[a] * x[a] + v[cross(a, b)] * x[b] + v[cross(a, c)] * x[c])
        return out

    ed, gd = diagonal(e), diagonal(g)
    eu, gu, gf = times(ed, e, u), times(gd, g, u), times(gd, g, force)
    fbar = []
    for a in AXES:
        b, c = OTHERS[a]
        jbar = (1.0 / 3.0) * (e[CUBIC[a, b]] + e[CUBIC[a, c]]) + eu[a] + gf[a] * inv
        cbar = mu[1 + a] + (1.0 / 3.0) * (g[CUBIC[a, b]] + g[CUBIC[a, c]]) + gu[a]
        nu[1 + a] = mu[1 + a] + jbar
        fbar.append(jnp.where(solid, 0.0, cbar + 0.5 * jbar))
    rho_bar = (
        e[0]
        + (1.0 / 3.0) * (e[7] + e[8] + e[9])
        + (1.0 / 9.0) * (e[16] + e[17] + e[18])
        - 0.5 * (u[0] * eu[0] + u[1] * eu[1] + u[2] * eu[2])
        - (force[0] * gu[0] + force[1] * gu[1] + force[2] * gu[2]) * inv
    )
    for k in range(19):
        nu[k] = jnp.where(solid, -mu[k] if k in ODD else mu[k], nu[k])
    return nu, fbar, jnp.where(solid, 0.0, rho_bar)


def neighbour_pull(ext, x):
    at = {(a, b): ext[x + 1 + a, Y0 + b : Y1 + b, :] for a, b in CLASSES}
    dx, dy = at[1, 0] - at[-1, 0], at[0, 1] - at[0, -1]
    main, other = at[1, 1] - at[-1, -1], at[1, -1] - at[-1, 1]
    total = FACE_W * at[0, 0] + EDGE_W * ((at[1, 0] + at[-1, 0]) + (at[0, 1] + at[0, -1]))
    gx = FACE_W * dx + EDGE_W * (main + other + (roll_z(dx, 1) + roll_z(dx, -1)))
    gy = FACE_W * dy + EDGE_W * (main - other + (roll_z(dy, 1) + roll_z(dy, -1)))
    return [gx, gy, roll_z(total, -1) - roll_z(total, 1)]


def spread_classes(p):
    px, py, pz = p
    up, down = roll_z(pz, 1), roll_z(pz, -1)
    side = {0: px, 1: py}
    turned = {a: EDGE_W * (roll_z(v, 1) + roll_z(v, -1)) + FACE_W * v for a, v in side.items()}
    lift = EDGE_W * (up - down)
    both, apart = EDGE_W * (px + py), EDGE_W * (px - py)
    return {
        (0, 0): FACE_W * (up - down),
        (1, 0): turned[0] + lift, (-1, 0): lift - turned[0],
        (0, 1): turned[1] + lift, (0, -1): lift - turned[1],
        (1, 1): both, (-1, -1): -both, (1, -1): apart, (-1, 1): -apart,
    }


def gather(ext, i, x, orient):
    cx, cy, _ = VELOCITY[i]
    return ext[i, x + 1 - orient * cx, Y0 - orient * cy : Y1 - orient * cy, :]


def class_sum(q, x):
    total = None
    for c in CLASSES:
        v = q[SLOT[c], x + 1 - c[0], Y0 - c[1] : Y1 - c[1], :]
        total = v if total is None else total + v
    return total


def chosen(d, orient):
    return [i for i, v in enumerate(VELOCITY) if all(d[n] == 0 or v[n] == orient * d[n] for n in (0, 1))]


def chosen_classes(d):
    return [c for c in CLASSES if all(d[n] == 0 or c[n] == d[n] for n in (0, 1))]


def edge_of(d):
    return (1 if d[0] < 0 else H), (Y0 if d[1] < 0 else Y1 - 1)


def halo_of(d):
    return (0 if d[0] > 0 else H + 1), (Y0 - 1 if d[1] > 0 else Y1)


def column(ext, y, shift=0):
    return jnp.concatenate([ext[1 + x + shift, y : y + 1, :] for x in range(H)], axis=0)


def pack(sb, k, place, ext):
    d = DIRS[k]
    ex, ey = edge_of(d)
    if d[1] == 0:
        sb[k, place * B : (place + 1) * B, :] = ext[ex, MID, :]
    elif d[0] == 0:
        for x in range(H):
            sb[k, place * H + x : place * H + x + 1, :] = ext[1 + x, ey : ey + 1, :]
    else:
        sb[k, place : place + 1, :] = ext[ex, ey : ey + 1, :]


def unpack(rb, k, place, ext):
    d = DIRS[k]
    hx, hy = halo_of(d)
    if d[1] == 0:
        ext[hx, MID, :] = rb[k, place * B : (place + 1) * B, :]
    elif d[0] == 0:
        for x in range(H):
            ext[1 + x, hy : hy + 1, :] = rb[k, place * H + x : place * H + x + 1, :]
    else:
        ext[hx, hy : hy + 1, :] = rb[k, place : place + 1, :]


def shifted(v, step):
    rows = v.shape[0]
    index = lax.broadcasted_iota(jnp.int32, v.shape, 0)
    return jnp.where(index == (0 if step > 0 else rows - 1), 0.0, pltpu.roll(v, step % rows, 0))


def pack_partial(sb, k, place, q):
    d = DIRS[k]
    ex, ey = edge_of(d)
    if d[1] == 0:
        t = {c: q[SLOT[0, c], ex, MID, :] + q[SLOT[d[0], c], ex - d[0], MID, :] for c in (-1, 0, 1)}
        at, size = place * B, B
    elif d[0] == 0:
        t = {c: column(q.at[SLOT[c, 0]], ey) + column(q.at[SLOT[c, d[1]]], ey - d[1]) for c in (-1, 0, 1)}
        at, size = place * H, H
    else:
        def one(c, x, y):
            return q[SLOT[c], x, y : y + 1, :]

        dx, dy = d
        sb[k, place : place + 1, :] = (
            one((0, 0), ex, ey) + one((dx, 0), ex - dx, ey) + one((0, dy), ex, ey - dy) + one(d, ex - dx, ey - dy)
        )
        sb[k, place + 1 : place + 2, :] = one((dx, 0), ex, ey) + one(d, ex, ey - dy)
        sb[k, place + 2 : place + 3, :] = one((0, dy), ex, ey) + one(d, ex - dx, ey)
        return
    sb[k, at : at + size, :] = t[0] + shifted(t[1], 1) + shifted(t[-1], -1)
    sb[k, at + size : at + size + 1, :] = t[-1][0:1, :]
    sb[k, at + size + 1 : at + size + 2, :] = t[1][size - 1 : size, :]


def border_sum(rb, places, q, out):
    at = {d: n for n, d in enumerate(DIRS)}
    for dx in (-1, 1):
        hx, _ = halo_of((dx, 0))
        ex, _ = edge_of((-dx, 0))
        k = at[dx, 0]
        n = places[k] * B
        total = rb[k, n : n + B, :]
        for c in (-1, 0, 1):
            total = total + q[SLOT[-dx, c], ex, Y0 - c : Y1 - c, :]
        out[hx, MID, :] = total
        for dy in (-1, 1):
            kc = at[dx, dy]
            _, ey = edge_of((0, -dy))
            out[hx, ey : ey + 1, :] += rb[kc, places[kc] + 2 : places[kc] + 3, :]
    for dy in (-1, 1):
        _, hy = halo_of((0, dy))
        _, ey = edge_of((0, -dy))
        k = at[0, dy]
        n = places[k] * H
        for x in range(H):
            total = rb[k, n + x : n + x + 1, :]
            for c in (-1, 0, 1):
                total = total + q[SLOT[c, -dy], x + 1 - c, ey : ey + 1, :]
            for dx in (-1, 1):
                if x == (0 if dx > 0 else H - 1):
                    kc = at[dx, dy]
                    total = total + rb[kc, places[kc] + 1 : places[kc] + 2, :]
            out[1 + x, hy : hy + 1, :] = total
    for dx in (-1, 1):
        for dy in (-1, 1):
            kc, kx, ky = at[dx, dy], at[dx, 0], at[0, dy]
            hx, hy = halo_of((dx, dy))
            ex, ey = edge_of((-dx, -dy))
            nx = places[kx] * B + B + (0 if dy > 0 else 1)
            ny = places[ky] * H + H + (0 if dx > 0 else 1)
            out[hx, hy : hy + 1, :] = (
                rb[kc, places[kc] : places[kc] + 1, :]
                + q[SLOT[-dx, -dy], ex, ey : ey + 1, :]
                + rb[kx, nx : nx + 1, :]
                + rb[ky, ny : ny + 1, :]
            )


def rows_of(k, fields, ends):
    d = DIRS[k]
    if d[1] == 0:
        return fields * B + (B + 8 if ends else 0)
    if d[0] == 0:
        return fields * H + (H + 8 if ends else 0)
    return 8


def kernel(
    nx, ny,
    table, rates, pops_hbm, mask_hbm, class_hbm, cot_hbm, base_hbm, extra_hbm,
    pops, cot, mask, wall_class, state, base_out, extra,
    psi_ext, solid_ext, wall_ext, e2_ext, sum_ext, d_ext, q_ext, cot_ext, post_ext, base_ext,
    s0, s1, s2, s3, s4, r0, r1, r2, r3, r4,
    send_sem, recv_sem, local_sem,
):
    gx, gy = lax.axis_index("gx"), lax.axis_index("gy")
    sends, recvs = (s0, s1, s2, s3, s4), (r0, r1, r2, r3, r4)

    def device(d):
        return (lax.rem(gx + (d[0] + nx), nx), lax.rem(gy + (d[1] + ny), ny))

    barrier = pltpu.get_barrier_semaphore()
    for d in DIRS:
        pl.semaphore_signal(barrier, inc=1, device_id=device(d), device_id_type=MESH)

    loads = [
        pltpu.make_async_copy(src, dst, local_sem.at[n])
        for n, (src, dst) in enumerate(
            ((pops_hbm, pops), (mask_hbm, mask), (class_hbm, wall_class), (cot_hbm, cot))
        )
    ]
    for c in loads:
        c.start()

    def start(r, fields, ends=False):
        copies = []
        for k, d in enumerate(DIRS):
            rows = pl.ds(0, rows_of(k, fields, ends))
            c = pltpu.make_async_remote_copy(
                src_ref=sends[r].at[k, rows], dst_ref=recvs[r].at[k, rows],
                send_sem=send_sem.at[r, k], recv_sem=recv_sem.at[r, k],
                device_id=device(d), device_id_type=MESH,
            )
            c.start()
            copies.append(c)
        return copies

    def finish(copies):
        for c in copies:
            c.wait()

    def each_row(body):
        def step(x, carry):
            body(x)
            return carry

        lax.fori_loop(0, H, step, 0)

    rate = [rates[k] for k in range(19)]

    for c in loads[:3]:
        c.wait()

    def prepare(x):
        f = [pops[i, x] for i in range(19)]
        rho = f[0]
        for i in range(1, 19):
            rho = rho + f[i]
        solid = mask[x] == 1
        kind = wall_class[x]
        wall = jnp.full(rho.shape, table[0], jnp.float32)
        for n in range(1, 8):
            wall = jnp.where(kind == n, table[n], wall)
        fade = jnp.exp(-rho)
        psi_ext[x + 1, MID, :] = jnp.where(solid, wall, 1.0 - fade)
        solid_ext[x + 1, MID, :] = jnp.where(solid, 1.0, 0.0)
        wall_ext[x + 1, MID, :] = wall
        state[0, x] = 1.0 / rho
        state[11, x] = jnp.where(solid, 0.0, fade)

    each_row(prepare)
    for k in range(8):
        pack(s0, k, 0, psi_ext)

    loads[3].wait()

    def turn(x):
        for i, c in enumerate(VELOCITY):
            cot_ext[i, x + 1, MID, :] = roll_z(cot[i, x], -c[2])

    each_row(turn)
    for k, d in enumerate(DIRS):
        ids = chosen(d, -1)
        for n, i in enumerate(ids):
            pack(s1, k, n, cot_ext.at[i])
        pack(s1, k, len(ids), solid_ext)
        pack(s1, k, len(ids) + 1, wall_ext)

    pl.semaphore_wait(barrier, len(DIRS))
    first = start(0, 1)
    early = start(1, 7)
    finish(first)
    for k in range(8):
        unpack(r0, k, 0, psi_ext)

    def forward(x):
        psi = psi_ext[x + 1, MID, :]
        pull = neighbour_pull(psi_ext, x)
        post, u, force = collide([pops[i, x] for i in range(19)], psi, pull, state[0, x], mask[x] == 1, rate)
        post = [roll_z(v, c[2]) for v, c in zip(post, VELOCITY)]
        for i in range(19):
            post_ext[i, x + 1, MID, :] = post[i]
        for c in CLASSES:
            total = post[MEMBERS[c][0]]
            for i in MEMBERS[c][1:]:
                total = total + post[i]
            q_ext[SLOT[c], x + 1, MID, :] = total
        for a in AXES:
            state[1 + a, x] = u[a]
            state[4 + a, x] = force[a]
            state[7 + a, x] = pull[a]
        state[10, x] = psi

    each_row(forward)
    places = []
    for k, d in enumerate(DIRS):
        ids = chosen(d, 1)
        for n, i in enumerate(ids):
            pack(s2, k, n, post_ext.at[i])
        pack_partial(s2, k, len(ids), q_ext)
        places.append(len(ids))
    second = start(2, 5, True)
    finish(early)
    for k, d in enumerate(DIRS):
        ids = chosen(d, -1)
        for n, i in enumerate(ids):
            unpack(r1, k, n, cot_ext.at[i])
        unpack(r1, k, len(ids), solid_ext)
        unpack(r1, k, len(ids) + 1, wall_ext)
    finish(second)

    for k, d in enumerate(DIRS):
        for n, i in enumerate(chosen(d, 1)):
            unpack(r2, k, n, post_ext.at[i])
    for d in DIRS:
        hx, hy = halo_of(d)
        for c in chosen_classes(d):
            if d[1] == 0:
                where = [(hx, MID)]
            elif d[0] == 0:
                where = [(1 + x, slice(hy, hy + 1)) for x in range(H)]
            else:
                where = [(hx, slice(hy, hy + 1))]
            for x, y in where:
                total = post_ext[MEMBERS[c][0], x, y, :]
                for i in MEMBERS[c][1:]:
                    total = total + post_ext[i, x, y, :]
                q_ext[SLOT[c], x, y, :] = total
    border_sum(r2, places, q_ext, sum_ext)

    def density(x):
        sum_ext[x + 1, MID, :] = class_sum(q_ext, x)

    each_row(density)

    def potential(x, carry):
        solid = solid_ext[x] > 0.5
        fade = jnp.exp(-sum_ext[x])
        psi_ext[x] = jnp.where(solid, wall_ext[x], 1.0 - fade)
        e2_ext[x] = jnp.where(solid, 0.0, fade)
        return carry

    lax.fori_loop(0, H + 2, potential, 0)

    def spread_out(fbar, psi, x):
        p = [5.0 * psi * v for v in fbar]
        for c, v in spread_classes(p).items():
            q_ext[SLOT[c], x + 1, MID, :] = v

    def backward_second(x):
        rho = sum_ext[x + 1, MID, :]
        inv = 1.0 / rho
        psi = psi_ext[x + 1, MID, :]
        solid = mask[x] == 1
        pull = neighbour_pull(psi_ext, x)
        force = [5.0 * psi * g for g in pull]
        f = [gather(post_ext, i, x, 1) for i in range(19)]
        u = []
        for a in AXES:
            m = None
            for i, c in enumerate(VELOCITY):
                if c[a] == 1:
                    m = f[i] if m is None else m + f[i]
            for i, c in enumerate(VELOCITY):
                if c[a] == -1:
                    m = m - f[i]
            u.append((m + 0.5 * force[a]) * inv)
        lam = [gather(cot_ext, i, x, -1) for i in range(19)]
        nu, fbar, rho_bar = collide_adjoint(lam, u, force, inv, solid, rate)
        local = rho_bar + e2_ext[x + 1, MID, :] * (
            5.0 * (pull[0] * fbar[0] + pull[1] * fbar[1] + pull[2] * fbar[2])
        )
        extra[2, x] = local
        nu[0] = nu[0] + local
        for i, v in enumerate(moments_t(nu)):
            base_ext[i, x + 1, MID, :] = roll_z(v, -VELOCITY[i][2])
        spread_out(fbar, psi, x)

    each_row(backward_second)
    places = []
    for k, d in enumerate(DIRS):
        ids, cs = chosen(d, -1), chosen_classes(d)
        for n, i in enumerate(ids):
            pack(s3, k, n, base_ext.at[i])
        for n, c in enumerate(cs):
            pack(s3, k, len(ids) + n, q_ext.at[SLOT[c]])
        pack_partial(s3, k, len(ids) + len(cs), q_ext)
        places.append(len(ids) + len(cs))
    finish(start(3, 8, True))
    for k, d in enumerate(DIRS):
        ids, cs = chosen(d, -1), chosen_classes(d)
        for n, i in enumerate(ids):
            unpack(r3, k, n, base_ext.at[i])
        for n, c in enumerate(cs):
            unpack(r3, k, len(ids) + n, q_ext.at[SLOT[c]])
    border_sum(r3, places, q_ext, sum_ext)

    def spread_second(x):
        total = class_sum(q_ext, x)
        sum_ext[x + 1, MID, :] = total
        extra[2, x] += e2_ext[x + 1, MID, :] * total
        extra[3, x] = jnp.where(mask[x] == 1, total, 0.0)

    each_row(spread_second)

    def shift_second(x, carry):
        v = e2_ext[x] * sum_ext[x]
        for c in (-1, 0, 1):
            d_ext[c + 1, x] = roll_z(v, -c)
        return carry

    lax.fori_loop(0, H + 2, shift_second, 0)

    def backward_first(x):
        solid = mask[x] == 1
        inv, psi = state[0, x], state[10, x]
        u = [state[1 + a, x] for a in AXES]
        force = [state[4 + a, x] for a in AXES]
        lam = []
        for i, c in enumerate(VELOCITY):
            more = d_ext[c[2] + 1, x + 1 + c[0], Y0 + c[1] : Y1 + c[1], :]
            lam.append(gather(base_ext, i, x, -1) + more)
        nu, fbar, rho_bar = collide_adjoint(lam, u, force, inv, solid, rate)
        local = rho_bar + state[11, x] * (
            5.0 * (state[7, x] * fbar[0] + state[8, x] * fbar[1] + state[9, x] * fbar[2])
        )
        extra[1, x] = local
        nu[0] = nu[0] + local
        for i, v in enumerate(moments_t(nu)):
            base_out[i, x] = v
        spread_out(fbar, psi, x)

    each_row(backward_first)
    for k, d in enumerate(DIRS):
        for n, c in enumerate(chosen_classes(d)):
            pack(s4, k, n, q_ext.at[SLOT[c]])
    last = start(4, 3)
    store = pltpu.make_async_copy(base_out, base_hbm, local_sem.at[4])
    store.start()
    finish(last)
    for k, d in enumerate(DIRS):
        for n, c in enumerate(chosen_classes(d)):
            unpack(r4, k, n, q_ext.at[SLOT[c]])

    def spread_first(x):
        total = class_sum(q_ext, x)
        change = state[11, x] * total
        extra[0, x] = change
        extra[1, x] += change
        extra[3, x] += jnp.where(mask[x] == 1, total, 0.0)

    each_row(spread_first)
    rest = pltpu.make_async_copy(extra, extra_hbm, local_sem.at[5])
    rest.start()
    rest.wait()
    store.wait()


def body(populations, solid_mask, wall_class, wall_table, relax_rates, pop_cotangent):
    f32 = jnp.float32
    nx, ny = lax.axis_size("gx"), lax.axis_size("gy")
    block = (H, B, Z)
    ext = (H + 2, 32, Z)
    anywhere = pl.BlockSpec(memory_space=pl.ANY)
    scalars = pl.BlockSpec(memory_space=pltpu.SMEM)
    vmem = pltpu.VMEM
    base, extra = pl.pallas_call(
        functools.partial(kernel, nx, ny),
        out_shape=(
            jax.ShapeDtypeStruct((19,) + block, f32),
            jax.ShapeDtypeStruct((4,) + block, f32),
        ),
        in_specs=[scalars, scalars] + [anywhere] * 4,
        out_specs=(anywhere, anywhere),
        scratch_shapes=[
            vmem((19,) + block, f32),
            vmem((19,) + block, f32),
            vmem(block, jnp.int32),
            vmem(block, jnp.int32),
            vmem((12,) + block, f32),
            vmem((19,) + block, f32),
            vmem((4,) + block, f32),
            vmem(ext, f32), vmem(ext, f32), vmem(ext, f32), vmem(ext, f32), vmem(ext, f32),
            vmem((3,) + ext, f32),
            vmem((9,) + ext, f32),
            vmem((19,) + ext, f32),
            vmem((19,) + ext, f32),
            vmem((19,) + ext, f32),
        ]
        + [vmem((8, n, Z), f32) for n in ROWS] * 2
        + [
            pltpu.SemaphoreType.DMA((5, 8)),
            pltpu.SemaphoreType.DMA((5, 8)),
            pltpu.SemaphoreType.DMA((6,)),
        ],
        compiler_params=pltpu.CompilerParams(
            collective_id=0, has_side_effects=True, vmem_limit_bytes=48 * 2**20
        ),
    )(wall_table, relax_rates, populations, solid_mask, wall_class, pop_cotangent)
    return base + extra[0][None], extra[1:3], extra[3]


def solution(mesh):
    in_specs = (
        P(None, "gx", "gy", None),
        P("gx", "gy", None),
        P("gx", "gy", None),
        P(),
        P(),
        P(None, "gx", "gy", None),
    )
    out_specs = (P(None, "gx", "gy", None), P(None, "gx", "gy", None), P("gx", "gy", None))
    return jax.shard_map(body, mesh=mesh, in_specs=in_specs, out_specs=out_specs, check_vma=False)
```

```python
import functools

import jax
import jax.numpy as jnp
from jax import lax
from jax.experimental import pallas as pl
from jax.experimental.pallas import tpu as pltpu
from jax.sharding import PartitionSpec as P

MESH = pl.DeviceIdType.MESH
VELOCITY = [
    (0, 0, 0),
    (1, 0, 0), (-1, 0, 0), (0, 1, 0), (0, -1, 0), (0, 0, 1), (0, 0, -1),
    (1, 1, 0), (-1, -1, 0), (1, -1, 0), (-1, 1, 0),
    (1, 0, 1), (-1, 0, -1), (1, 0, -1), (-1, 0, 1),
    (0, 1, 1), (0, -1, -1), (0, 1, -1), (0, -1, 1),
]
FACE_W, EDGE_W = 1.0 / 18.0, 1.0 / 36.0
AXES = (0, 1, 2)
PAIRS = ((0, 1), (0, 2), (1, 2))
CROSS = {(0, 1): 4, (0, 2): 5, (1, 2): 6}
QUAD = {(0, 1): 16, (0, 2): 17, (1, 2): 18}
CUBIC = {(0, 1): 10, (0, 2): 11, (1, 0): 12, (1, 2): 13, (2, 0): 14, (2, 1): 15}
EDGE = {(0, 1): 7, (0, 2): 11, (1, 2): 15}
ODD = (1, 2, 3, 10, 11, 12, 13, 14, 15)
OTHERS = {0: (1, 2), 1: (0, 2), 2: (0, 1)}
DIRS = ((-1, -1), (-1, 1), (1, -1), (1, 1), (-1, 0), (1, 0), (0, -1), (0, 1))
CLASSES = [(a, b) for a in (-1, 0, 1) for b in (-1, 0, 1)]
SLOT = {c: n for n, c in enumerate(CLASSES)}
MEMBERS = {c: [i for i, v in enumerate(VELOCITY) if v[:2] == c] for c in CLASSES}
H, B, Z = 8, 16, 128
Y0, Y1 = 8, 24
MID = slice(Y0, Y1)
ROWS = (16, 112, 104, 152, 48)


def quad(a, b):
    return QUAD[(min(a, b), max(a, b))]


def cross(a, b):
    return CROSS[(min(a, b), max(a, b))]


def roll_z(v, shift):
    return v if shift == 0 else pltpu.roll(v, shift % Z, v.ndim - 1)


def moments(f):
    m = [None] * 19
    s = [f[1 + 2 * a] + f[2 + 2 * a] for a in AXES]
    d = [f[1 + 2 * a] - f[2 + 2 * a] for a in AXES]
    for a, b in PAIRS:
        e = EDGE[a, b]
        al, ad = f[e] + f[e + 1], f[e] - f[e + 1]
        be, bd = f[e + 2] + f[e + 3], f[e + 2] - f[e + 3]
        m[CROSS[a, b]] = al - be
        m[QUAD[a, b]] = al + be
        m[CUBIC[a, b]] = ad + bd
        m[CUBIC[b, a]] = ad - bd
    for a in AXES:
        b, c = OTHERS[a]
        m[1 + a] = d[a] + (m[CUBIC[a, b]] + m[CUBIC[a, c]])
        m[7 + a] = s[a] + (m[quad(a, b)] + m[quad(a, c)])
    m[0] = (f[0] + s[0]) + (s[1] + s[2]) + (m[16] + m[17] + m[18])
    return m


def from_moments(p):
    f = [None] * 19
    for a in AXES:
        b, c = OTHERS[a]
        s = 0.5 * (p[7 + a] - (p[quad(a, b)] + p[quad(a, c)]))
        d = 0.5 * (p[1 + a] - (p[CUBIC[a, b]] + p[CUBIC[a, c]]))
        f[1 + 2 * a], f[2 + 2 * a] = s + d, s - d
    for a, b in PAIRS:
        e = EDGE[a, b]
        q, r = 0.25 * p[QUAD[a, b]], 0.25 * p[CROSS[a, b]]
        t, w = 0.25 * p[CUBIC[a, b]], 0.25 * p[CUBIC[b, a]]
        up, down, plus, minus = q + r, q - r, t + w, t - w
        f[e], f[e + 1], f[e + 2], f[e + 3] = up + plus, up - plus, down + minus, down - minus
    f[0] = p[0] - (p[7] + p[8] + p[9]) + (p[16] + p[17] + p[18])
    return f


def from_moments_t(lam):
    mu = [None] * 19
    mu[0] = lam[0]
    s = [0.5 * (lam[1 + 2 * a] + lam[2 + 2 * a]) for a in AXES]
    d = [0.5 * (lam[1 + 2 * a] - lam[2 + 2 * a]) for a in AXES]
    for a in AXES:
        mu[1 + a] = d[a]
        mu[7 + a] = s[a] - lam[0]
    for a, b in PAIRS:
        e = EDGE[a, b]
        al, ad = lam[e] + lam[e + 1], lam[e] - lam[e + 1]
        be, bd = lam[e + 2] + lam[e + 3], lam[e + 2] - lam[e + 3]
        mu[QUAD[a, b]] = 0.25 * (al + be) - s[a] - mu[7 + b]
        mu[CROSS[a, b]] = 0.25 * (al - be)
        mu[CUBIC[a, b]] = 0.25 * (ad + bd) - d[a]
        mu[CUBIC[b, a]] = 0.25 * (ad - bd) - d[b]
    return mu


def moments_t(nu):
    f = [None] * 19
    f[0] = nu[0]
    for a in AXES:
        s = nu[0] + nu[7 + a]
        f[1 + 2 * a], f[2 + 2 * a] = s + nu[1 + a], s - nu[1 + a]
    for a, b in PAIRS:
        e = EDGE[a, b]
        even = (nu[0] + nu[7 + a]) + (nu[7 + b] + nu[QUAD[a, b]])
        up, down = even + nu[CROSS[a, b]], even - nu[CROSS[a, b]]
        p, q = nu[1 + a] + nu[CUBIC[a, b]], nu[1 + b] + nu[CUBIC[b, a]]
        f[e], f[e + 1], f[e + 2], f[e + 3] = up + (p + q), up - (p + q), down + (p - q), down - (p - q)
    return f


def collide(f, psi, pull, inv, solid, rate):
    m = moments(f)
    rho = m[0]
    force = [5.0 * psi * g for g in pull]
    u = [(m[1 + a] + 0.5 * force[a]) * inv for a in AXES]
    n = [m[1 + a] - 0.5 * force[a] for a in AXES]
    p = [None] * 19
    p[0] = rho
    w = [u[a] * n[a] for a in AXES]
    t = [u[a] * force[a] for a in AXES]
    third = rho * (1.0 / 3.0)
    ninth = rho * (1.0 / 9.0)
    for a in AXES:
        p[1 + a] = m[1 + a] + force[a]
        k = 7 + a
        p[k] = m[k] + rate[k] * (third + w[a] - m[k]) + 2.0 * t[a]
    m3 = [m[1 + a] * (1.0 / 3.0) for a in AXES]
    f3 = [force[a] * (1.0 / 3.0) for a in AXES]
    for (a, b), k in CUBIC.items():
        p[k] = m[k] + rate[k] * (m3[a] - m[k]) + f3[a]
    w3 = [(1.0 / 3.0) * v for v in w]
    t3 = [(1.0 / 3.0) * v for v in t]
    for a, b in PAIRS:
        c = 3 - a - b
        k = CROSS[a, b]
        p[k] = m[k] + rate[k] * (0.5 * (u[b] * n[a] + u[a] * n[b]) - m[k]) + (u[a] * force[b] + u[b] * force[a])
        k = QUAD[a, b]
        p[k] = (
            m[k]
            + rate[k] * (ninth + (w3[a] + w3[b]) - 0.5 * w3[c] - m[k])
            + (2.0 * (t3[a] + t3[b]) - t3[c])
        )
    for k in range(1, 19):
        p[k] = jnp.where(solid, -m[k] if k in ODD else m[k], p[k])
    return from_moments(p), u, force


def collide_adjoint(lam, u, force, inv, solid, rate):
    mu = from_moments_t(lam)
    e, nu, g = [None] * 19, [None] * 19, [None] * 19
    for k in (0,) + tuple(range(4, 19)):
        e[k] = rate[k] * mu[k]
        nu[k] = mu[k] - e[k]
        g[k] = mu[k] - 0.5 * e[k]

    def diagonal(v):
        out = []
        for a in AXES:
            b, c = OTHERS[a]
            out.append(2.0 * v[7 + a] + (2.0 / 3.0) * (v[quad(a, b)] + v[quad(a, c)]) - (1.0 / 3.0) * v[quad(b, c)])
        return out

    def times(diag, v, x):
        out = []
        for a in AXES:
            b, c = OTHERS[a]
            out.append(diag[a] * x[a] + v[cross(a, b)] * x[b] + v[cross(a, c)] * x[c])
        return out

    ed, gd = diagonal(e), diagonal(g)
    eu, gu, gf = times(ed, e, u), times(gd, g, u), times(gd, g, force)
    fbar = []
    for a in AXES:
        b, c = OTHERS[a]
        jbar = (1.0 / 3.0) * (e[CUBIC[a, b]] + e[CUBIC[a, c]]) + eu[a] + gf[a] * inv
        cbar = mu[1 + a] + (1.0 / 3.0) * (g[CUBIC[a, b]] + g[CUBIC[a, c]]) + gu[a]
        nu[1 + a] = mu[1 + a] + jbar
        fbar.append(jnp.where(solid, 0.0, cbar + 0.5 * jbar))
    rho_bar = (
        e[0]
        + (1.0 / 3.0) * (e[7] + e[8] + e[9])
        + (1.0 / 9.0) * (e[16] + e[17] + e[18])
        - 0.5 * (u[0] * eu[0] + u[1] * eu[1] + u[2] * eu[2])
        - (force[0] * gu[0] + force[1] * gu[1] + force[2] * gu[2]) * inv
    )
    for k in range(19):
        nu[k] = jnp.where(solid, -mu[k] if k in ODD else mu[k], nu[k])
    return nu, fbar, jnp.where(solid, 0.0, rho_bar)


def neighbour_pull(ext, x):
    at = {(a, b): ext[x + 1 + a, Y0 + b : Y1 + b, :] for a, b in CLASSES}
    dx, dy = at[1, 0] - at[-1, 0], at[0, 1] - at[0, -1]
    main, other = at[1, 1] - at[-1, -1], at[1, -1] - at[-1, 1]
    total = FACE_W * at[0, 0] + EDGE_W * ((at[1, 0] + at[-1, 0]) + (at[0, 1] + at[0, -1]))
    gx = FACE_W * dx + EDGE_W * (main + other + (roll_z(dx, 1) + roll_z(dx, -1)))
    gy = FACE_W * dy + EDGE_W * (main - other + (roll_z(dy, 1) + roll_z(dy, -1)))
    return [gx, gy, roll_z(total, -1) - roll_z(total, 1)]


def spread_classes(p):
    px, py, pz = p
    up, down = roll_z(pz, 1), roll_z(pz, -1)
    side = {0: px, 1: py}
    turned = {a: EDGE_W * (roll_z(v, 1) + roll_z(v, -1)) + FACE_W * v for a, v in side.items()}
    lift = EDGE_W * (up - down)
    both, apart = EDGE_W * (px + py), EDGE_W * (px - py)
    return {
        (0, 0): FACE_W * (up - down),
        (1, 0): turned[0] + lift, (-1, 0): lift - turned[0],
        (0, 1): turned[1] + lift, (0, -1): lift - turned[1],
        (1, 1): both, (-1, -1): -both, (1, -1): apart, (-1, 1): -apart,
    }


def gather(ext, i, x, orient):
    cx, cy, _ = VELOCITY[i]
    return ext[i, x + 1 - orient * cx, Y0 - orient * cy : Y1 - orient * cy, :]


def class_sum(q, x):
    total = None
    for c in CLASSES:
        v = q[SLOT[c], x + 1 - c[0], Y0 - c[1] : Y1 - c[1], :]
        total = v if total is None else total + v
    return total


def chosen(d, orient):
    return [i for i, v in enumerate(VELOCITY) if all(d[n] == 0 or v[n] == orient * d[n] for n in (0, 1))]


def chosen_classes(d):
    return [c for c in CLASSES if all(d[n] == 0 or c[n] == d[n] for n in (0, 1))]


def edge_of(d):
    return (1 if d[0] < 0 else H), (Y0 if d[1] < 0 else Y1 - 1)


def halo_of(d):
    return (0 if d[0] > 0 else H + 1), (Y0 - 1 if d[1] > 0 else Y1)


def strip(y, shift=0):
    return pl.ds((1 + shift) * 32 + y, H, stride=32)


def flat(ext):
    return ext.reshape((H + 2) * 32, Z)


def column(ext, y, shift=0):
    return flat(ext)[strip(y, shift), :]


def pack(sb, k, place, ext):
    d = DIRS[k]
    ex, ey = edge_of(d)
    if d[1] == 0:
        sb[k, place * B : (place + 1) * B, :] = ext[ex, MID, :]
    elif d[0] == 0:
        sb[k, place * H : (place + 1) * H, :] = column(ext, ey)
    else:
        sb[k, place : place + 1, :] = ext[ex, ey : ey + 1, :]


def unpack(rb, k, place, ext):
    d = DIRS[k]
    hx, hy = halo_of(d)
    if d[1] == 0:
        ext[hx, MID, :] = rb[k, place * B : (place + 1) * B, :]
    elif d[0] == 0:
        flat(ext)[strip(hy), :] = rb[k, place * H : (place + 1) * H, :]
    else:
        ext[hx, hy : hy + 1, :] = rb[k, place : place + 1, :]


def shifted(v, step):
    rows = v.shape[0]
    index = lax.broadcasted_iota(jnp.int32, v.shape, 0)
    return jnp.where(index == (0 if step > 0 else rows - 1), 0.0, pltpu.roll(v, step % rows, 0))


def pack_partial(sb, k, place, q):
    d = DIRS[k]
    ex, ey = edge_of(d)
    if d[1] == 0:
        t = {c: q[SLOT[0, c], ex, MID, :] + q[SLOT[d[0], c], ex - d[0], MID, :] for c in (-1, 0, 1)}
        at, size = place * B, B
    elif d[0] == 0:
        t = {c: column(q.at[SLOT[c, 0]], ey) + column(q.at[SLOT[c, d[1]]], ey - d[1]) for c in (-1, 0, 1)}
        at, size = place * H, H
    else:
        def one(c, x, y):
            return q[SLOT[c], x, y : y + 1, :]

        dx, dy = d
        sb[k, place : place + 1, :] = (
            one((0, 0), ex, ey) + one((dx, 0), ex - dx, ey) + one((0, dy), ex, ey - dy) + one(d, ex - dx, ey - dy)
        )
        sb[k, place + 1 : place + 2, :] = one((dx, 0), ex, ey) + one(d, ex, ey - dy)
        sb[k, place + 2 : place + 3, :] = one((0, dy), ex, ey) + one(d, ex - dx, ey)
        return
    sb[k, at : at + size, :] = t[0] + shifted(t[1], 1) + shifted(t[-1], -1)
    sb[k, at + size : at + size + 1, :] = t[-1][0:1, :]
    sb[k, at + size + 1 : at + size + 2, :] = t[1][size - 1 : size, :]


def border_sum(rb, places, q, out):
    at = {d: n for n, d in enumerate(DIRS)}
    for dx in (-1, 1):
        hx, _ = halo_of((dx, 0))
        ex, _ = edge_of((-dx, 0))
        k = at[dx, 0]
        n = places[k] * B
        total = rb[k, n : n + B, :]
        for c in (-1, 0, 1):
            total = total + q[SLOT[-dx, c], ex, Y0 - c : Y1 - c, :]
        out[hx, MID, :] = total
        for dy in (-1, 1):
            kc = at[dx, dy]
            _, ey = edge_of((0, -dy))
            out[hx, ey : ey + 1, :] += rb[kc, places[kc] + 2 : places[kc] + 3, :]
    for dy in (-1, 1):
        _, hy = halo_of((0, dy))
        _, ey = edge_of((0, -dy))
        k = at[0, dy]
        n = places[k] * H
        total = rb[k, n : n + H, :]
        for c in (-1, 0, 1):
            total = total + column(q.at[SLOT[c, -dy]], ey, -c)
        flat(out)[strip(hy), :] = total
        for dx in (-1, 1):
            kc = at[dx, dy]
            ex, _ = edge_of((-dx, 0))
            out[ex, hy : hy + 1, :] += rb[kc, places[kc] + 1 : places[kc] + 2, :]
    for dx in (-1, 1):
        for dy in (-1, 1):
            kc, kx, ky = at[dx, dy], at[dx, 0], at[0, dy]
            hx, hy = halo_of((dx, dy))
            ex, ey = edge_of((-dx, -dy))
            nx = places[kx] * B + B + (0 if dy > 0 else 1)
            ny = places[ky] * H + H + (0 if dx > 0 else 1)
            out[hx, hy : hy + 1, :] = (
                rb[kc, places[kc] : places[kc] + 1, :]
                + q[SLOT[-dx, -dy], ex, ey : ey + 1, :]
                + rb[kx, nx : nx + 1, :]
                + rb[ky, ny : ny + 1, :]
            )


def rows_of(k, fields, ends):
    d = DIRS[k]
    if d[1] == 0:
        return fields * B + (B + 8 if ends else 0)
    if d[0] == 0:
        return fields * H + (H + 8 if ends else 0)
    return 8


def kernel(
    nx, ny,
    table_hbm, rates_hbm, pops_hbm, mask_hbm, class_hbm, cot_hbm, base_out, extra,
    table, rates, pops, cot, mask, wall_class, state,
    psi_ext, solid_ext, wall_ext, e2_ext, sum_ext, d_ext, q_ext, cot_ext, post_ext, base_ext,
    s0, s1, s2, s3, s4, r0, r1, r2, r3, r4,
    send_sem, recv_sem, local_sem,
):
    gx, gy = lax.axis_index("gx"), lax.axis_index("gy")
    sends, recvs = (s0, s1, s2, s3, s4), (r0, r1, r2, r3, r4)

    def device(d):
        return (lax.rem(gx + (d[0] + nx), nx), lax.rem(gy + (d[1] + ny), ny))

    barrier = pltpu.get_barrier_semaphore()
    for d in DIRS:
        pl.semaphore_signal(barrier, inc=1, device_id=device(d), device_id_type=MESH)

    loads = [
        pltpu.make_async_copy(src, dst, local_sem.at[n])
        for n, (src, dst) in enumerate(
            ((pops_hbm, pops), (mask_hbm, mask), (class_hbm, wall_class), (table_hbm, table), (rates_hbm, rates), (cot_hbm, cot))
        )
    ]
    for c in loads:
        c.start()

    def start(r, fields, ends=False):
        copies = []
        for k, d in enumerate(DIRS):
            rows = pl.ds(0, rows_of(k, fields, ends))
            c = pltpu.make_async_remote_copy(
                src_ref=sends[r].at[k, rows], dst_ref=recvs[r].at[k, rows],
                send_sem=send_sem.at[r, k], recv_sem=recv_sem.at[r, k],
                device_id=device(d), device_id_type=MESH,
            )
            c.start()
            copies.append(c)
        return copies

    def finish(copies):
        for c in copies:
            c.wait()

    def each_row(body):
        def step(x, carry):
            body(x)
            return carry

        lax.fori_loop(0, H, step, 0, unroll=8)

    for c in loads[:5]:
        c.wait()
    rate = [rates[k] for k in range(19)]

    def prepare(x):
        f = [pops[i, x] for i in range(19)]
        rho = f[0]
        for i in range(1, 19):
            rho = rho + f[i]
        solid = mask[x] == 1
        kind = wall_class[x]
        wall = jnp.full(rho.shape, table[0], jnp.float32)
        for n in range(1, 8):
            wall = jnp.where(kind == n, table[n], wall)
        fade = jnp.exp(-rho)
        psi_ext[x + 1, MID, :] = jnp.where(solid, wall, 1.0 - fade)
        solid_ext[x + 1, MID, :] = jnp.where(solid, 1.0, 0.0)
        wall_ext[x + 1, MID, :] = wall
        state[0, x] = 1.0 / rho
        state[11, x] = jnp.where(solid, 0.0, fade)

    each_row(prepare)
    for k in range(8):
        pack(s0, k, 0, psi_ext)

    loads[5].wait()

    def turn(x):
        for i, c in enumerate(VELOCITY):
            cot_ext[i, x + 1, MID, :] = roll_z(cot[i, x], -c[2])

    each_row(turn)
    for k, d in enumerate(DIRS):
        ids = chosen(d, -1)
        for n, i in enumerate(ids):
            pack(s1, k, n, cot_ext.at[i])
        pack(s1, k, len(ids), solid_ext)
        pack(s1, k, len(ids) + 1, wall_ext)

    pl.semaphore_wait(barrier, len(DIRS))
    first = start(0, 1)
    early = start(1, 7)
    finish(first)
    for k in range(8):
        unpack(r0, k, 0, psi_ext)

    def forward(x):
        psi = psi_ext[x + 1, MID, :]
        pull = neighbour_pull(psi_ext, x)
        post, u, force = collide([pops[i, x] for i in range(19)], psi, pull, state[0, x], mask[x] == 1, rate)
        post = [roll_z(v, c[2]) for v, c in zip(post, VELOCITY)]
        for i in range(19):
            post_ext[i, x + 1, MID, :] = post[i]
        for c in CLASSES:
            total = post[MEMBERS[c][0]]
            for i in MEMBERS[c][1:]:
                total = total + post[i]
            q_ext[SLOT[c], x + 1, MID, :] = total
        for a in AXES:
            state[1 + a, x] = u[a]
            state[4 + a, x] = force[a]
            state[7 + a, x] = pull[a]
        state[10, x] = psi

    each_row(forward)
    places = []
    for k, d in enumerate(DIRS):
        ids = chosen(d, 1)
        for n, i in enumerate(ids):
            pack(s2, k, n, post_ext.at[i])
        pack_partial(s2, k, len(ids), q_ext)
        places.append(len(ids))
    second = start(2, 5, True)
    finish(early)
    for k, d in enumerate(DIRS):
        ids = chosen(d, -1)
        for n, i in enumerate(ids):
            unpack(r1, k, n, cot_ext.at[i])
        unpack(r1, k, len(ids), solid_ext)
        unpack(r1, k, len(ids) + 1, wall_ext)
    finish(second)

    for k, d in enumerate(DIRS):
        for n, i in enumerate(chosen(d, 1)):
            unpack(r2, k, n, post_ext.at[i])
    for d in DIRS:
        hx, hy = halo_of(d)
        for c in chosen_classes(d):
            if d[1] == 0:
                where = [(hx, MID)]
            elif d[0] == 0:
                total = column(post_ext.at[MEMBERS[c][0]], hy)
                for i in MEMBERS[c][1:]:
                    total = total + column(post_ext.at[i], hy)
                flat(q_ext.at[SLOT[c]])[strip(hy), :] = total
                continue
            else:
                where = [(hx, slice(hy, hy + 1))]
            for x, y in where:
                total = post_ext[MEMBERS[c][0], x, y, :]
                for i in MEMBERS[c][1:]:
                    total = total + post_ext[i, x, y, :]
                q_ext[SLOT[c], x, y, :] = total
    border_sum(r2, places, q_ext, sum_ext)

    def density(x):
        sum_ext[x + 1, MID, :] = class_sum(q_ext, x)

    each_row(density)

    def potential(x, carry):
        solid = solid_ext[x] > 0.5
        fade = jnp.exp(-sum_ext[x])
        psi_ext[x] = jnp.where(solid, wall_ext[x], 1.0 - fade)
        e2_ext[x] = jnp.where(solid, 0.0, fade)
        return carry

    lax.fori_loop(0, H + 2, potential, 0, unroll=10)

    def spread_out(fbar, psi, x):
        p = [5.0 * psi * v for v in fbar]
        for c, v in spread_classes(p).items():
            q_ext[SLOT[c], x + 1, MID, :] = v

    def backward_second(x):
        rho = sum_ext[x + 1, MID, :]
        inv = 1.0 / rho
        psi = psi_ext[x + 1, MID, :]
        solid = mask[x] == 1
        pull = neighbour_pull(psi_ext, x)
        force = [5.0 * psi * g for g in pull]
        f = [gather(post_ext, i, x, 1) for i in range(19)]
        u = []
        for a in AXES:
            m = None
            for i, c in enumerate(VELOCITY):
                if c[a] == 1:
                    m = f[i] if m is None else m + f[i]
            for i, c in enumerate(VELOCITY):
                if c[a] == -1:
                    m = m - f[i]
            u.append((m + 0.5 * force[a]) * inv)
        lam = [gather(cot_ext, i, x, -1) for i in range(19)]
        nu, fbar, rho_bar = collide_adjoint(lam, u, force, inv, solid, rate)
        local = rho_bar + e2_ext[x + 1, MID, :] * (
            5.0 * (pull[0] * fbar[0] + pull[1] * fbar[1] + pull[2] * fbar[2])
        )
        extra[2, x] = local
        nu[0] = nu[0] + local
        for i, v in enumerate(moments_t(nu)):
            base_ext[i, x + 1, MID, :] = roll_z(v, -VELOCITY[i][2])
        spread_out(fbar, psi, x)

    each_row(backward_second)
    places = []
    for k, d in enumerate(DIRS):
        ids, cs = chosen(d, -1), chosen_classes(d)
        for n, i in enumerate(ids):
            pack(s3, k, n, base_ext.at[i])
        for n, c in enumerate(cs):
            pack(s3, k, len(ids) + n, q_ext.at[SLOT[c]])
        pack_partial(s3, k, len(ids) + len(cs), q_ext)
        places.append(len(ids) + len(cs))
    finish(start(3, 8, True))
    for k, d in enumerate(DIRS):
        ids, cs = chosen(d, -1), chosen_classes(d)
        for n, i in enumerate(ids):
            unpack(r3, k, n, base_ext.at[i])
        for n, c in enumerate(cs):
            unpack(r3, k, len(ids) + n, q_ext.at[SLOT[c]])
    border_sum(r3, places, q_ext, sum_ext)

    def spread_second(x):
        total = class_sum(q_ext, x)
        sum_ext[x + 1, MID, :] = total
        extra[2, x] += e2_ext[x + 1, MID, :] * total
        extra[3, x] = jnp.where(mask[x] == 1, total, 0.0)

    each_row(spread_second)

    def shift_second(x, carry):
        v = e2_ext[x] * sum_ext[x]
        for c in (-1, 0, 1):
            d_ext[c + 1, x] = roll_z(v, -c)
        return carry

    lax.fori_loop(0, H + 2, shift_second, 0, unroll=10)

    def backward_first(x):
        solid = mask[x] == 1
        inv, psi = state[0, x], state[10, x]
        u = [state[1 + a, x] for a in AXES]
        force = [state[4 + a, x] for a in AXES]
        lam = []
        for i, c in enumerate(VELOCITY):
            more = d_ext[c[2] + 1, x + 1 + c[0], Y0 + c[1] : Y1 + c[1], :]
            lam.append(gather(base_ext, i, x, -1) + more)
        nu, fbar, rho_bar = collide_adjoint(lam, u, force, inv, solid, rate)
        local = rho_bar + state[11, x] * (
            5.0 * (state[7, x] * fbar[0] + state[8, x] * fbar[1] + state[9, x] * fbar[2])
        )
        extra[1, x] = local
        nu[0] = nu[0] + local
        for i, v in enumerate(moments_t(nu)):
            base_out[i, x] = v
        spread_out(fbar, psi, x)

    each_row(backward_first)
    for k, d in enumerate(DIRS):
        for n, c in enumerate(chosen_classes(d)):
            pack(s4, k, n, q_ext.at[SLOT[c]])
    last = start(4, 3)
    finish(last)
    for k, d in enumerate(DIRS):
        for n, c in enumerate(chosen_classes(d)):
            unpack(r4, k, n, q_ext.at[SLOT[c]])

    def spread_first(x):
        total = class_sum(q_ext, x)
        change = state[11, x] * total
        extra[0, x] = change
        extra[1, x] += change
        extra[3, x] += jnp.where(mask[x] == 1, total, 0.0)

    each_row(spread_first)


def closing(base, extra, adjoint_hbm, density_hbm, wet_hbm, adjoint, sems):
    copies = [
        pltpu.make_async_copy(extra.at[pl.ds(1, 2)], density_hbm, sems.at[19]),
        pltpu.make_async_copy(extra.at[3], wet_hbm, sems.at[20]),
    ]
    for c in copies:
        c.start()
    for i in range(19):
        adjoint[i] = base[i] + extra[0]
        c = pltpu.make_async_copy(adjoint.at[i], adjoint_hbm.at[i], sems.at[i])
        c.start()
        copies.append(c)
    for c in copies:
        c.wait()


def body(populations, solid_mask, wall_class, wall_table, relax_rates, pop_cotangent):
    f32 = jnp.float32
    nx, ny = lax.axis_size("gx"), lax.axis_size("gy")
    block = (H, B, Z)
    ext = (H + 2, 32, Z)
    anywhere = pl.BlockSpec(memory_space=pl.ANY)
    vmem = pltpu.VMEM
    far = [
        pltpu.with_memory_space_constraint(v, pltpu.HBM)
        for v in (wall_table, relax_rates, populations, solid_mask, wall_class, pop_cotangent)
    ]
    base, extra = pl.pallas_call(
        functools.partial(kernel, nx, ny),
        out_shape=(
            vmem((19,) + block, f32),
            vmem((4,) + block, f32),
        ),
        in_specs=[anywhere] * 6,
        out_specs=(pl.BlockSpec(memory_space=vmem),) * 2,
        scratch_shapes=[
            pltpu.SMEM((8,), f32),
            pltpu.SMEM((19,), f32),
            vmem((19,) + block, f32),
            vmem((19,) + block, f32),
            vmem(block, jnp.int32),
            vmem(block, jnp.int32),
            vmem((12,) + block, f32),
            vmem(ext, f32), vmem(ext, f32), vmem(ext, f32), vmem(ext, f32), vmem(ext, f32),
            vmem((3,) + ext, f32),
            vmem((9,) + ext, f32),
            vmem((19,) + ext, f32),
            vmem((19,) + ext, f32),
            vmem((19,) + ext, f32),
        ]
        + [vmem((8, n, Z), f32) for n in ROWS] * 2
        + [
            pltpu.SemaphoreType.DMA((5, 8)),
            pltpu.SemaphoreType.DMA((5, 8)),
            pltpu.SemaphoreType.DMA((6,)),
        ],
        compiler_params=pltpu.CompilerParams(
            collective_id=0, has_side_effects=True, vmem_limit_bytes=40 * 2**20
        ),
    )(*far)
    return pl.pallas_call(
        closing,
        out_shape=(
            jax.ShapeDtypeStruct((19,) + block, f32),
            jax.ShapeDtypeStruct((2,) + block, f32),
            jax.ShapeDtypeStruct(block, f32),
        ),
        in_specs=[pl.BlockSpec(memory_space=vmem)] * 2,
        out_specs=(anywhere,) * 3,
        scratch_shapes=[vmem((19,) + block, f32), pltpu.SemaphoreType.DMA((21,))],
        compiler_params=pltpu.CompilerParams(vmem_limit_bytes=8 * 2**20),
    )(base, extra)


def solution(mesh):
    in_specs = (
        P(None, "gx", "gy", None),
        P("gx", "gy", None),
        P("gx", "gy", None),
        P(),
        P(),
        P(None, "gx", "gy", None),
    )
    out_specs = (P(None, "gx", "gy", None), P(None, "gx", "gy", None), P("gx", "gy", None))
    return jax.shard_map(body, mesh=mesh, in_specs=in_specs, out_specs=out_specs, check_vma=False)
```

```python
import functools

import jax
import jax.numpy as jnp
from jax import lax
from jax.experimental import pallas as pl
from jax.experimental.pallas import tpu as pltpu
from jax.sharding import PartitionSpec as P

MESH = pl.DeviceIdType.MESH
VELOCITY = [
    (0, 0, 0),
    (1, 0, 0), (-1, 0, 0), (0, 1, 0), (0, -1, 0), (0, 0, 1), (0, 0, -1),
    (1, 1, 0), (-1, -1, 0), (1, -1, 0), (-1, 1, 0),
    (1, 0, 1), (-1, 0, -1), (1, 0, -1), (-1, 0, 1),
    (0, 1, 1), (0, -1, -1), (0, 1, -1), (0, -1, 1),
]
FACE_W, EDGE_W = 1.0 / 18.0, 1.0 / 36.0
AXES = (0, 1, 2)
PAIRS = ((0, 1), (0, 2), (1, 2))
CROSS = {(0, 1): 4, (0, 2): 5, (1, 2): 6}
QUAD = {(0, 1): 16, (0, 2): 17, (1, 2): 18}
CUBIC = {(0, 1): 10, (0, 2): 11, (1, 0): 12, (1, 2): 13, (2, 0): 14, (2, 1): 15}
EDGE = {(0, 1): 7, (0, 2): 11, (1, 2): 15}
ODD = (1, 2, 3, 10, 11, 12, 13, 14, 15)
OTHERS = {0: (1, 2), 1: (0, 2), 2: (0, 1)}
DIRS = ((-1, -1), (-1, 1), (1, -1), (1, 1), (-1, 0), (1, 0), (0, -1), (0, 1))
CLASSES = [(a, b) for a in (-1, 0, 1) for b in (-1, 0, 1)]
ACROSS, BESIDE = range(4), range(4, 8)
SLOT = {c: n for n, c in enumerate(CLASSES)}
MEMBERS = {c: [i for i, v in enumerate(VELOCITY) if v[:2] == c] for c in CLASSES}
H, B, Z = 8, 16, 128
Y0, Y1 = 8, 24
MID = slice(Y0, Y1)
ROWS = (16, 112, 104, 120, 16)


def quad(a, b):
    return QUAD[(min(a, b), max(a, b))]


def cross(a, b):
    return CROSS[(min(a, b), max(a, b))]


def roll_z(v, shift):
    return v if shift == 0 else pltpu.roll(v, shift % Z, v.ndim - 1)


def moments(f):
    m = [None] * 19
    s = [f[1 + 2 * a] + f[2 + 2 * a] for a in AXES]
    d = [f[1 + 2 * a] - f[2 + 2 * a] for a in AXES]
    for a, b in PAIRS:
        e = EDGE[a, b]
        al, ad = f[e] + f[e + 1], f[e] - f[e + 1]
        be, bd = f[e + 2] + f[e + 3], f[e + 2] - f[e + 3]
        m[CROSS[a, b]] = al - be
        m[QUAD[a, b]] = al + be
        m[CUBIC[a, b]] = ad + bd
        m[CUBIC[b, a]] = ad - bd
    for a in AXES:
        b, c = OTHERS[a]
        m[1 + a] = d[a] + (m[CUBIC[a, b]] + m[CUBIC[a, c]])
        m[7 + a] = s[a] + (m[quad(a, b)] + m[quad(a, c)])
    m[0] = (f[0] + s[0]) + (s[1] + s[2]) + (m[16] + m[17] + m[18])
    return m


def from_moments(p):
    f = [None] * 19
    for a in AXES:
        b, c = OTHERS[a]
        s = 0.5 * (p[7 + a] - (p[quad(a, b)] + p[quad(a, c)]))
        d = 0.5 * (p[1 + a] - (p[CUBIC[a, b]] + p[CUBIC[a, c]]))
        f[1 + 2 * a], f[2 + 2 * a] = s + d, s - d
    for a, b in PAIRS:
        e = EDGE[a, b]
        q, r = 0.25 * p[QUAD[a, b]], 0.25 * p[CROSS[a, b]]
        t, w = 0.25 * p[CUBIC[a, b]], 0.25 * p[CUBIC[b, a]]
        up, down, plus, minus = q + r, q - r, t + w, t - w
        f[e], f[e + 1], f[e + 2], f[e + 3] = up + plus, up - plus, down + minus, down - minus
    f[0] = p[0] - (p[7] + p[8] + p[9]) + (p[16] + p[17] + p[18])
    return f


def from_moments_t(lam):
    mu = [None] * 19
    mu[0] = lam[0]
    s = [0.5 * (lam[1 + 2 * a] + lam[2 + 2 * a]) for a in AXES]
    d = [0.5 * (lam[1 + 2 * a] - lam[2 + 2 * a]) for a in AXES]
    for a in AXES:
        mu[1 + a] = d[a]
        mu[7 + a] = s[a] - lam[0]
    for a, b in PAIRS:
        e = EDGE[a, b]
        al, ad = lam[e] + lam[e + 1], lam[e] - lam[e + 1]
        be, bd = lam[e + 2] + lam[e + 3], lam[e + 2] - lam[e + 3]
        mu[QUAD[a, b]] = 0.25 * (al + be) - s[a] - mu[7 + b]
        mu[CROSS[a, b]] = 0.25 * (al - be)
        mu[CUBIC[a, b]] = 0.25 * (ad + bd) - d[a]
        mu[CUBIC[b, a]] = 0.25 * (ad - bd) - d[b]
    return mu


def moments_t(nu):
    f = [None] * 19
    f[0] = nu[0]
    for a in AXES:
        s = nu[0] + nu[7 + a]
        f[1 + 2 * a], f[2 + 2 * a] = s + nu[1 + a], s - nu[1 + a]
    for a, b in PAIRS:
        e = EDGE[a, b]
        even = (nu[0] + nu[7 + a]) + (nu[7 + b] + nu[QUAD[a, b]])
        up, down = even + nu[CROSS[a, b]], even - nu[CROSS[a, b]]
        p, q = nu[1 + a] + nu[CUBIC[a, b]], nu[1 + b] + nu[CUBIC[b, a]]
        f[e], f[e + 1], f[e + 2], f[e + 3] = up + (p + q), up - (p + q), down + (p - q), down - (p - q)
    return f


def collide(f, psi, pull, inv, solid, rate):
    m = moments(f)
    rho = m[0]
    force = [5.0 * psi * g for g in pull]
    u = [(m[1 + a] + 0.5 * force[a]) * inv for a in AXES]
    n = [m[1 + a] - 0.5 * force[a] for a in AXES]
    p = [None] * 19
    p[0] = rho
    w = [u[a] * n[a] for a in AXES]
    t = [u[a] * force[a] for a in AXES]
    third = rho * (1.0 / 3.0)
    ninth = rho * (1.0 / 9.0)
    for a in AXES:
        p[1 + a] = m[1 + a] + force[a]
        k = 7 + a
        p[k] = m[k] + rate[k] * (third + w[a] - m[k]) + 2.0 * t[a]
    m3 = [m[1 + a] * (1.0 / 3.0) for a in AXES]
    f3 = [force[a] * (1.0 / 3.0) for a in AXES]
    for (a, b), k in CUBIC.items():
        p[k] = m[k] + rate[k] * (m3[a] - m[k]) + f3[a]
    w3 = [(1.0 / 3.0) * v for v in w]
    t3 = [(1.0 / 3.0) * v for v in t]
    for a, b in PAIRS:
        c = 3 - a - b
        k = CROSS[a, b]
        p[k] = m[k] + rate[k] * (0.5 * (u[b] * n[a] + u[a] * n[b]) - m[k]) + (u[a] * force[b] + u[b] * force[a])
        k = QUAD[a, b]
        p[k] = (
            m[k]
            + rate[k] * (ninth + (w3[a] + w3[b]) - 0.5 * w3[c] - m[k])
            + (2.0 * (t3[a] + t3[b]) - t3[c])
        )
    for k in range(1, 19):
        p[k] = jnp.where(solid, -m[k] if k in ODD else m[k], p[k])
    return from_moments(p), u, force


def adjoint_setup(lam, solid, rate):
    mu = from_moments_t(lam)
    e, nu, g = [None] * 19, [None] * 19, [None] * 19
    for k in (0,) + tuple(range(4, 19)):
        e[k] = rate[k] * mu[k]
        nu[k] = jnp.where(solid, -mu[k] if k in ODD else mu[k], mu[k] - e[k])
        g[k] = mu[k] - 0.5 * e[k]

    def diagonal(v):
        out = []
        for a in AXES:
            b, c = OTHERS[a]
            out.append(2.0 * v[7 + a] + (2.0 / 3.0) * (v[quad(a, b)] + v[quad(a, c)]) - (1.0 / 3.0) * v[quad(b, c)])
        return out

    def thirds(v):
        return [(1.0 / 3.0) * (v[CUBIC[a, OTHERS[a][0]]] + v[CUBIC[a, OTHERS[a][1]]]) for a in AXES]

    level = (
        e[0]
        + (1.0 / 3.0) * (e[7] + e[8] + e[9])
        + (1.0 / 9.0) * (e[16] + e[17] + e[18])
    )
    lift = [mu[1 + a] + v for a, v in enumerate(thirds(g))]
    return [nu[0]] + nu[4:] + mu[1:4] + diagonal(e) + e[4:7] + diagonal(g) + g[4:7] + thirds(e) + lift + [level]


SETUP = 38


def adjoint_finish(setup, u, force, inv, solid):
    nu = [setup[0], None, None, None] + list(setup[1:16])
    mu, ed, ec, gd, gc, push, lift = (setup[n : n + 3] for n in range(16, 37, 3))
    level = setup[37]

    def times(diag, off, x):
        out = []
        for a in AXES:
            b, c = OTHERS[a]
            out.append(diag[a] * x[a] + off[cross(a, b) - 4] * x[b] + off[cross(a, c) - 4] * x[c])
        return out

    eu, gu, gf = times(ed, ec, u), times(gd, gc, u), times(gd, gc, force)
    fbar = []
    for a in AXES:
        jbar = push[a] + eu[a] + gf[a] * inv
        nu[1 + a] = jnp.where(solid, -mu[a], mu[a] + jbar)
        fbar.append(jnp.where(solid, 0.0, lift[a] + gu[a] + 0.5 * jbar))
    rho_bar = (
        level
        - 0.5 * (u[0] * eu[0] + u[1] * eu[1] + u[2] * eu[2])
        - (force[0] * gu[0] + force[1] * gu[1] + force[2] * gu[2]) * inv
    )
    return nu, fbar, jnp.where(solid, 0.0, rho_bar)


class Row:
    def __init__(self, x):
        self.x = x

    def near(self, ext, a=0, b=0):
        return ext[self.x + 1 + a, Y0 + b : Y1 + b, :]

    def put(self, ext, v):
        ext[self.x + 1, MID, :] = v

    def own(self, ref):
        return ref[self.x]

    def keep(self, ref, v):
        ref[self.x] = v


class Column:
    def __init__(self, y):
        self.y = y

    def near(self, ext, a=0, b=0):
        return flat(ext)[strip(Y0 + self.y + b, a), :]

    def put(self, ext, v):
        flat(ext)[strip(Y0 + self.y), :] = v

    def own(self, ref):
        return ref.reshape(H * B, Z)[pl.ds(self.y, H, stride=B), :]

    def keep(self, ref, v):
        ref.reshape(H * B, Z)[pl.ds(self.y, H, stride=B), :] = v


def neighbour_pull(ext, part):
    at = {(a, b): part.near(ext, a, b) for a, b in CLASSES}
    dx, dy = at[1, 0] - at[-1, 0], at[0, 1] - at[0, -1]
    main, other = at[1, 1] - at[-1, -1], at[1, -1] - at[-1, 1]
    total = FACE_W * at[0, 0] + EDGE_W * ((at[1, 0] + at[-1, 0]) + (at[0, 1] + at[0, -1]))
    gx = FACE_W * dx + EDGE_W * (main + other + (roll_z(dx, 1) + roll_z(dx, -1)))
    gy = FACE_W * dy + EDGE_W * (main - other + (roll_z(dy, 1) + roll_z(dy, -1)))
    return [gx, gy, roll_z(total, -1) - roll_z(total, 1)]


def spread_classes(p):
    px, py, pz = p
    up, down = roll_z(pz, 1), roll_z(pz, -1)
    turned = [EDGE_W * (roll_z(v, 1) + roll_z(v, -1)) + FACE_W * v for v in (px, py)]
    lift = EDGE_W * (up - down)
    both, apart = EDGE_W * (px + py), EDGE_W * (px - py)
    return {
        (0, 0): FACE_W * (up - down),
        (1, 0): turned[0] + lift, (-1, 0): lift - turned[0],
        (0, 1): turned[1] + lift, (0, -1): lift - turned[1],
        (1, 1): both, (-1, -1): -both, (1, -1): apart, (-1, 1): -apart,
    }


def chosen(d, orient):
    return [i for i, v in enumerate(VELOCITY) if all(d[n] == 0 or v[n] == orient * d[n] for n in (0, 1))]


def edge_of(d):
    return (1 if d[0] < 0 else H), (Y0 if d[1] < 0 else Y1 - 1)


def halo_of(d):
    return (0 if d[0] < 0 else H + 1), (Y0 - 1 if d[1] < 0 else Y1)


def strip(y, shift=0):
    return pl.ds((1 + shift) * 32 + y, H, stride=32)


def flat(ext):
    return ext.reshape((H + 2) * 32, Z)


def pack(sb, k, place, ext):
    d = DIRS[k]
    ex, ey = edge_of(d)
    if d[1] == 0:
        sb[k, place * B : (place + 1) * B, :] = ext[ex, MID, :]
    elif d[0] == 0:
        sb[k, place * H : (place + 1) * H, :] = flat(ext)[strip(ey), :]
    else:
        sb[k, place : place + 1, :] = ext[ex, ey : ey + 1, :]


def unpack(rb, k, place, ext):
    d = DIRS[k]
    hx, hy = halo_of((-d[0], -d[1]))
    if d[1] == 0:
        ext[hx, MID, :] = rb[k, place * B : (place + 1) * B, :]
    elif d[0] == 0:
        flat(ext)[strip(hy), :] = rb[k, place * H : (place + 1) * H, :]
    else:
        ext[hx, hy : hy + 1, :] = rb[k, place : place + 1, :]


def shifted(v, step):
    rows = v.shape[0]
    index = lax.broadcasted_iota(jnp.int32, v.shape, 0)
    return jnp.where(index == (0 if step > 0 else rows - 1), 0.0, pltpu.roll(v, step % rows, 0))


def line(t):
    size = t[0].shape[0]
    return t[0] + shifted(t[1], 1) + shifted(t[-1], -1), t[-1][0:1, :], t[1][size - 1 : size, :]


def size_of(d):
    return B if d[1] == 0 else H


def lines_towards(q, d):
    ex, ey = edge_of(d)
    if d[1] == 0:
        outer = {c: q[SLOT[d[0], c], ex, MID, :] for c in (-1, 0, 1)}
        behind = {c: q[SLOT[0, c], ex, MID, :] + q[SLOT[d[0], c], ex - d[0], MID, :] for c in (-1, 0, 1)}
    else:
        def column(c, y):
            return flat(q.at[SLOT[c]])[strip(y), :]

        outer = {c: column((c, d[1]), ey) for c in (-1, 0, 1)}
        behind = {c: column((c, 0), ey) + column((c, d[1]), ey - d[1]) for c in (-1, 0, 1)}
    return line(outer), line(behind)


def put_lines(sb, k, fields, lines, ends=True):
    s = size_of(DIRS[k])
    at = fields * s
    for n, (middle, low, high) in enumerate(lines):
        sb[k, at + n * s : at + (n + 1) * s, :] = middle
        if ends:
            e = at + len(lines) * s + 2 * n
            sb[k, e : e + 1, :] = low
            sb[k, e + 1 : e + 2, :] = high


def get_lines(rb, k, fields, count, ends=True):
    s = size_of(DIRS[k])
    at = fields * s
    out = []
    for n in range(count):
        e = at + count * s + 2 * n
        low, high = (rb[k, e : e + 1, :], rb[k, e + 1 : e + 2, :]) if ends else (None, None)
        out.append((rb[k, at + n * s : at + (n + 1) * s, :], low, high))
    return out


def put_corner(sb, k, place, q):
    dx, dy = DIRS[k]
    ex, ey = edge_of((dx, dy))

    def one(c, x, y):
        return q[SLOT[c], x, y : y + 1, :]

    across = (dx, dy)
    values = (
        one((0, 0), ex, ey) + one((dx, 0), ex - dx, ey) + one((0, dy), ex, ey - dy) + one(across, ex - dx, ey - dy),
        one((dx, 0), ex, ey) + one(across, ex, ey - dy),
        one((0, dy), ex, ey) + one(across, ex - dx, ey),
        one(across, ex, ey),
    )
    for n, v in enumerate(values):
        sb[k, place + n : place + n + 1, :] = v


def own_sum(q, out, border=True):
    for x in range(0 if border else 1, H + 2 if border else H + 1):
        total = None
        for c in CLASSES:
            if 1 <= x - c[0] <= H:
                v = q[SLOT[c], x - c[0], Y0 - c[1] : Y1 - c[1], :]
                total = v if total is None else total + v
        out[x, MID, :] = total
    if not border:
        return
    for d in DIRS:
        ex, ey = edge_of(d)
        hx, hy = halo_of(d)
        if d[0] == 0:
            total = None
            for c in (-1, 0, 1):
                v = flat(q.at[SLOT[c, d[1]]])[strip(ey, -c), :]
                total = v if total is None else total + v
            flat(out)[strip(hy), :] = total
        elif d[1] != 0:
            out[hx, hy : hy + 1, :] = q[SLOT[d], ex, ey : ey + 1, :]


def add_line(out, d, at, middle, low, high):
    if d[1] == 0:
        out[at, MID, :] += middle
        if low is not None:
            out[at, Y0 - 1 : Y0, :] += low
            out[at, Y1 : Y1 + 1, :] += high
    else:
        flat(out)[strip(at), :] += middle
        if low is not None:
            out[0, at : at + 1, :] += low
            out[H + 1, at : at + 1, :] += high


def add_arrived(rb, out, k, into, behind, fields):
    d = DIRS[k]
    back = (-d[0], -d[1])
    ex, ey = edge_of(back)
    hx, hy = halo_of(back)
    if d[0] == 0 or d[1] == 0:
        n = 1 if d[0] == 0 else 0
        add_line(out, d, (ex, ey)[n], *into)
        if behind is not None:
            add_line(out, d, (hx, hy)[n], *behind)
    elif behind is None:
        out[ex, ey : ey + 1, :] += into
    else:
        for n, (x, y) in enumerate(((hx, hy), (ex, hy), (hx, ey), (ex, ey))):
            out[x, y : y + 1, :] += rb[k, fields + n : fields + n + 1, :]


def kernel(
    nx, ny,
    table_hbm, rates_hbm, pops_hbm, mask_hbm, class_hbm, cot_hbm, base_out, extra,
    table, rates, pops, cot, mask, wall_class, state, setup,
    psi_ext, solid_ext, wall_ext, e2_ext, sum_ext, d_ext, q_ext, cot_ext, post_ext, base_ext,
    s0, s1, s2, s3, s4, r0, r1, r2, r3, r4,
    send_sem, recv_sem, local_sem,
):
    gx, gy = lax.axis_index("gx"), lax.axis_index("gy")
    sends, recvs = (s0, s1, s2, s3, s4), (r0, r1, r2, r3, r4)

    def device(d):
        return (lax.rem(gx + (d[0] + nx), nx), lax.rem(gy + (d[1] + ny), ny))

    barrier = pltpu.get_barrier_semaphore()
    for d in DIRS:
        pl.semaphore_signal(barrier, inc=1, device_id=device(d), device_id_type=MESH)

    loads = [
        pltpu.make_async_copy(src, dst, local_sem.at[n])
        for n, (src, dst) in enumerate(
            ((pops_hbm, pops), (mask_hbm, mask), (class_hbm, wall_class), (table_hbm, table), (rates_hbm, rates), (cot_hbm, cot))
        )
    ]
    for c in loads:
        c.start()

    def start(r, fields, ends=0):
        copies = []
        for k, d in enumerate(DIRS):
            rows = pl.ds(0, fields * size_of(d) + ends if d[0] == 0 or d[1] == 0 else 8)
            c = pltpu.make_async_remote_copy(
                src_ref=sends[r].at[k, rows], dst_ref=recvs[r].at[k, rows],
                send_sem=send_sem.at[r, k], recv_sem=recv_sem.at[r, k],
                device_id=device(d), device_id_type=MESH,
            )
            c.start()
            copies.append(c)
        return copies

    def finish(copies, which=range(8)):
        for k in which:
            copies[k].wait()

    def each_row(body, first=0, last=H):
        def step(x, carry):
            body(Row(x))
            return carry

        lax.fori_loop(first, last, step, 0, unroll=last - first)

    def clear(x, carry):
        for n in range(9):
            q_ext[n, x] = jnp.zeros((32, Z), jnp.float32)
        return carry

    lax.fori_loop(0, H + 2, clear, 0)

    for c in loads[:5]:
        c.wait()
    rate = [rates[k] for k in range(19)]

    def prepare(part):
        f = [part.own(pops.at[i]) for i in range(19)]
        rho = f[0]
        for i in range(1, 19):
            rho = rho + f[i]
        solid = part.own(mask) == 1
        kind = part.own(wall_class)
        wall = jnp.full(rho.shape, table[0], jnp.float32)
        for n in range(1, 8):
            wall = jnp.where(kind == n, table[n], wall)
        fade = jnp.exp(-rho)
        part.put(psi_ext, jnp.where(solid, wall, 1.0 - fade))
        part.put(solid_ext, jnp.where(solid, 1.0, 0.0))
        part.put(wall_ext, wall)
        part.keep(state.at[0], 1.0 / rho)
        part.keep(state.at[11], jnp.where(solid, 0.0, fade))

    each_row(prepare)
    for k in range(8):
        pack(s0, k, 0, psi_ext)
    pl.semaphore_wait(barrier, len(DIRS))
    first = start(0, 1)

    loads[5].wait()

    def turn(part):
        for i, c in enumerate(VELOCITY):
            part.put(cot_ext.at[i], roll_z(part.own(cot.at[i]), -c[2]))

    each_row(turn)
    for k, d in enumerate(DIRS):
        ids = chosen(d, -1)
        for n, i in enumerate(ids):
            pack(s1, k, n, cot_ext.at[i])
        pack(s1, k, len(ids), solid_ext)
        pack(s1, k, len(ids) + 1, wall_ext)
    early = start(1, 7)

    def forward(part):
        psi = part.near(psi_ext)
        pull = neighbour_pull(psi_ext, part)
        f = [part.own(pops.at[i]) for i in range(19)]
        post, u, force = collide(f, psi, pull, part.own(state.at[0]), part.own(mask) == 1, rate)
        post = [roll_z(v, c[2]) for v, c in zip(post, VELOCITY)]
        for i in range(19):
            part.put(post_ext.at[i], post[i])
        for c in CLASSES:
            total = post[MEMBERS[c][0]]
            for i in MEMBERS[c][1:]:
                total = total + post[i]
            part.put(q_ext.at[SLOT[c]], total)
        for a in AXES:
            part.keep(state.at[1 + a], u[a])
            part.keep(state.at[4 + a], force[a])
            part.keep(state.at[7 + a], pull[a])
        part.keep(state.at[10], psi)

    each_row(forward, 1, H - 1)
    finish(first, BESIDE)
    for k in BESIDE:
        unpack(r0, k, 0, psi_ext)
    for part in (Column(0), Column(B - 1)):
        forward(part)
    finish(first, ACROSS)
    for k in ACROSS:
        unpack(r0, k, 0, psi_ext)
    for part in (Row(0), Row(H - 1)):
        forward(part)
    for k, d in enumerate(DIRS):
        ids = chosen(d, 1)
        for n, i in enumerate(ids):
            pack(s2, k, n, post_ext.at[i])
        if len(ids) == 1:
            put_corner(s2, k, 1, q_ext)
        else:
            put_lines(s2, k, 5, lines_towards(q_ext, d)[1:])
    second = start(2, 6, 8)

    own_sum(q_ext, sum_ext)
    finish(early)
    for k, d in enumerate(DIRS):
        ids = chosen(d, -1)
        for n, i in enumerate(ids):
            unpack(r1, k, n, cot_ext.at[i])
        unpack(r1, k, len(ids), solid_ext)
        unpack(r1, k, len(ids) + 1, wall_ext)

    def prepare_adjoint(part):
        lam = [part.near(cot_ext.at[i], c[0], c[1]) for i, c in enumerate(VELOCITY)]
        for n, v in enumerate(adjoint_setup(lam, part.own(mask) == 1, rate)):
            part.keep(setup.at[n], v)

    each_row(prepare_adjoint)
    finish(second, BESIDE)

    for k in BESIDE:
        d = DIRS[k]
        ids = chosen(d, 1)
        for n, i in enumerate(ids):
            unpack(r2, k, n, post_ext.at[i])
        s = size_of(d)
        parts = {}
        for n, i in enumerate(ids):
            c = VELOCITY[i][1 if d[1] == 0 else 0]
            v = r2[k, n * s : (n + 1) * s, :]
            parts[c] = parts[c] + v if c in parts else v
        add_arrived(r2, sum_ext, k, line(parts), get_lines(r2, k, 5, 1)[0], 5)

    def potential(x):
        solid = solid_ext[x] > 0.5
        fade = jnp.exp(-sum_ext[x])
        psi_ext[x] = jnp.where(solid, wall_ext[x], 1.0 - fade)
        e2_ext[x] = jnp.where(solid, 0.0, fade)

    for x in range(2, H):
        potential(x)

    def spread_out(fbar, psi, part):
        p = [5.0 * psi * v for v in fbar]
        for c, v in spread_classes(p).items():
            part.put(q_ext.at[SLOT[c]], v)

    def backward_second(part):
        inv = 1.0 / part.near(sum_ext)
        psi = part.near(psi_ext)
        solid = part.own(mask) == 1
        pull = neighbour_pull(psi_ext, part)
        force = [5.0 * psi * g for g in pull]
        f = [part.near(post_ext.at[i], -c[0], -c[1]) for i, c in enumerate(VELOCITY)]
        u = []
        for a in AXES:
            m = None
            for i, c in enumerate(VELOCITY):
                if c[a] == 1:
                    m = f[i] if m is None else m + f[i]
            for i, c in enumerate(VELOCITY):
                if c[a] == -1:
                    m = m - f[i]
            u.append((m + 0.5 * force[a]) * inv)
        ready = [part.own(setup.at[n]) for n in range(SETUP)]
        nu, fbar, rho_bar = adjoint_finish(ready, u, force, inv, solid)
        local = rho_bar + part.near(e2_ext) * (
            5.0 * (pull[0] * fbar[0] + pull[1] * fbar[1] + pull[2] * fbar[2])
        )
        part.keep(extra.at[2], local)
        nu[0] = nu[0] + local
        for i, v in enumerate(moments_t(nu)):
            part.put(base_ext.at[i], roll_z(v, -VELOCITY[i][2]))
        spread_out(fbar, psi, part)

    each_row(backward_second, 2, H - 2)
    finish(second, ACROSS)
    for k in ACROSS:
        unpack(r2, k, 0, post_ext.at[chosen(DIRS[k], 1)[0]])
        add_arrived(r2, sum_ext, k, True, True, 1)
    for x in (0, 1, H, H + 1):
        potential(x)
    for x in (0, 1, H - 2, H - 1):
        backward_second(Row(x))
    for k, d in enumerate(DIRS):
        ids = chosen(d, -1)
        for n, i in enumerate(ids):
            pack(s3, k, n, base_ext.at[i])
        if len(ids) == 1:
            put_corner(s3, k, 1, q_ext)
        else:
            put_lines(s3, k, 5, lines_towards(q_ext, d))
    third = start(3, 7, 8)
    own_sum(q_ext, sum_ext)
    finish(third, BESIDE)
    for k in BESIDE:
        for n, i in enumerate(chosen(DIRS[k], -1)):
            unpack(r3, k, n, base_ext.at[i])
        add_arrived(r3, sum_ext, k, *get_lines(r3, k, 5, 2), 5)

    def shift_second(x):
        v = e2_ext[x] * sum_ext[x]
        for c in (-1, 0, 1):
            d_ext[c + 1, x] = roll_z(v, -c)

    for x in range(2, H):
        shift_second(x)
    finish(third, ACROSS)
    for k in ACROSS:
        unpack(r3, k, 0, base_ext.at[chosen(DIRS[k], -1)[0]])
        add_arrived(r3, sum_ext, k, True, True, 1)
    for x in (0, 1, H, H + 1):
        shift_second(x)

    def backward_first(part):
        solid = part.own(mask) == 1
        inv, psi = part.own(state.at[0]), part.own(state.at[10])
        u = [part.own(state.at[1 + a]) for a in AXES]
        force = [part.own(state.at[4 + a]) for a in AXES]
        lam = [
            part.near(base_ext.at[i], c[0], c[1]) + part.near(d_ext.at[c[2] + 1], c[0], c[1])
            for i, c in enumerate(VELOCITY)
        ]
        nu, fbar, rho_bar = adjoint_finish(adjoint_setup(lam, solid, rate), u, force, inv, solid)
        spread_out(fbar, psi, part)
        if isinstance(part, Column):
            return
        pull = [part.own(state.at[7 + a]) for a in AXES]
        local = rho_bar + part.own(state.at[11]) * (
            5.0 * (pull[0] * fbar[0] + pull[1] * fbar[1] + pull[2] * fbar[2])
        )
        part.keep(extra.at[1], local)
        nu[0] = nu[0] + local
        for i, v in enumerate(moments_t(nu)):
            part.keep(base_out.at[i], v)

    for part in (Row(0), Row(H - 1), Column(0), Column(B - 1)):
        backward_first(part)
    for k, d in enumerate(DIRS):
        if d[0] == 0 or d[1] == 0:
            put_lines(s4, k, 0, lines_towards(q_ext, d)[:1], False)
        else:
            pack(s4, k, 0, q_ext.at[SLOT[d]])
    last = start(4, 1)

    def spread_second(part):
        total = part.near(sum_ext)
        part.keep(extra.at[2], part.own(extra.at[2]) + part.near(d_ext.at[1]))
        part.keep(extra.at[3], jnp.where(part.own(mask) == 1, total, 0.0))

    each_row(spread_second)
    each_row(backward_first, 1, H - 1)
    own_sum(q_ext, sum_ext, False)
    finish(last, BESIDE)
    for k in BESIDE:
        add_arrived(r4, sum_ext, k, get_lines(r4, k, 0, 1, False)[0], None, 0)

    def spread_first(part):
        total = part.near(sum_ext)
        change = part.own(state.at[11]) * total
        part.keep(extra.at[0], change)
        part.keep(extra.at[1], part.own(extra.at[1]) + change)
        part.keep(extra.at[3], part.own(extra.at[3]) + jnp.where(part.own(mask) == 1, total, 0.0))

    each_row(spread_first, 1, H - 1)
    finish(last, ACROSS)
    for k in ACROSS:
        add_arrived(r4, sum_ext, k, r4[k, 0:1, :], None, 0)
    for x in (0, H - 1):
        spread_first(Row(x))


def closing(base, extra, adjoint_hbm, density_hbm, wet_hbm, adjoint, sems):
    copies = [
        pltpu.make_async_copy(extra.at[pl.ds(1, 2)], density_hbm, sems.at[19]),
        pltpu.make_async_copy(extra.at[3], wet_hbm, sems.at[20]),
    ]
    for c in copies:
        c.start()
    for i in range(19):
        adjoint[i] = base[i] + extra[0]
        c = pltpu.make_async_copy(adjoint.at[i], adjoint_hbm.at[i], sems.at[i])
        c.start()
        copies.append(c)
    for c in copies:
        c.wait()


def body(populations, solid_mask, wall_class, wall_table, relax_rates, pop_cotangent):
    f32 = jnp.float32
    nx, ny = lax.axis_size("gx"), lax.axis_size("gy")
    block = (H, B, Z)
    ext = (H + 2, 32, Z)
    anywhere = pl.BlockSpec(memory_space=pl.ANY)
    vmem = pltpu.VMEM
    far = [
        pltpu.with_memory_space_constraint(v, pltpu.HBM)
        for v in (wall_table, relax_rates, populations, solid_mask, wall_class, pop_cotangent)
    ]
    base, extra = pl.pallas_call(
        functools.partial(kernel, nx, ny),
        out_shape=(
            vmem((19,) + block, f32),
            vmem((4,) + block, f32),
        ),
        in_specs=[anywhere] * 6,
        out_specs=(pl.BlockSpec(memory_space=vmem),) * 2,
        scratch_shapes=[
            pltpu.SMEM((8,), f32),
            pltpu.SMEM((19,), f32),
            vmem((19,) + block, f32),
            vmem((19,) + block, f32),
            vmem(block, jnp.int32),
            vmem(block, jnp.int32),
            vmem((12,) + block, f32),
            vmem((SETUP,) + block, f32),
            vmem(ext, f32), vmem(ext, f32), vmem(ext, f32), vmem(ext, f32), vmem(ext, f32),
            vmem((3,) + ext, f32),
            vmem((9,) + ext, f32),
            vmem((19,) + ext, f32),
            vmem((19,) + ext, f32),
            vmem((19,) + ext, f32),
        ]
        + [vmem((8, n, Z), f32) for n in ROWS] * 2
        + [
            pltpu.SemaphoreType.DMA((5, 8)),
            pltpu.SemaphoreType.DMA((5, 8)),
            pltpu.SemaphoreType.DMA((6,)),
        ],
        compiler_params=pltpu.CompilerParams(
            collective_id=0, has_side_effects=True, vmem_limit_bytes=40 * 2**20
        ),
    )(*far)
    return pl.pallas_call(
        closing,
        out_shape=(
            jax.ShapeDtypeStruct((19,) + block, f32),
            jax.ShapeDtypeStruct((2,) + block, f32),
            jax.ShapeDtypeStruct(block, f32),
        ),
        in_specs=[pl.BlockSpec(memory_space=vmem)] * 2,
        out_specs=(anywhere,) * 3,
        scratch_shapes=[vmem((19,) + block, f32), pltpu.SemaphoreType.DMA((21,))],
        compiler_params=pltpu.CompilerParams(vmem_limit_bytes=8 * 2**20),
    )(base, extra)


def solution(mesh):
    in_specs = (
        P(None, "gx", "gy", None),
        P("gx", "gy", None),
        P("gx", "gy", None),
        P(),
        P(),
        P(None, "gx", "gy", None),
    )
    out_specs = (P(None, "gx", "gy", None), P(None, "gx", "gy", None), P("gx", "gy", None))
    return jax.shard_map(body, mesh=mesh, in_specs=in_specs, out_specs=out_specs, check_vma=False)
```

```python
import functools

import jax
import jax.numpy as jnp
from jax import lax
from jax.experimental import pallas as pl
from jax.experimental.pallas import tpu as pltpu
from jax.sharding import PartitionSpec as P

MESH = pl.DeviceIdType.MESH
VELOCITY = [
    (0, 0, 0),
    (1, 0, 0), (-1, 0, 0), (0, 1, 0), (0, -1, 0), (0, 0, 1), (0, 0, -1),
    (1, 1, 0), (-1, -1, 0), (1, -1, 0), (-1, 1, 0),
    (1, 0, 1), (-1, 0, -1), (1, 0, -1), (-1, 0, 1),
    (0, 1, 1), (0, -1, -1), (0, 1, -1), (0, -1, 1),
]
FACE_W, EDGE_W = 1.0 / 18.0, 1.0 / 36.0
AXES = (0, 1, 2)
PAIRS = ((0, 1), (0, 2), (1, 2))
H, B, Z = 8, 16, 128
CROSS = {(0, 1): 4, (0, 2): 5, (1, 2): 6}
QUAD = {(0, 1): 16, (0, 2): 17, (1, 2): 18}
CUBIC = {(0, 1): 10, (0, 2): 11, (1, 0): 12, (1, 2): 13, (2, 0): 14, (2, 1): 15}
EDGE = {(0, 1): 7, (0, 2): 11, (1, 2): 15}
ODD = (1, 2, 3, 10, 11, 12, 13, 14, 15)
OTHERS = {0: (1, 2), 1: (0, 2), 2: (0, 1)}
DIRS = ((-1, -1), (1, 1), (-1, 1), (1, -1), (-1, 0), (1, 0), (0, -1), (0, 1))
CLASSES = [(a, b) for a in (-1, 0, 1) for b in (-1, 0, 1)]
ACROSS, BESIDE = range(4), range(4, 8)
PAIR_A, PAIR_B = range(2), range(2, 4)
ENDS_A, ENDS_B = ((0, 0), (H - 1, B // 2)), ((0, B // 2), (H - 1, 0))
SLOT = {c: n for n, c in enumerate(CLASSES)}
MEMBERS = {c: [i for i, v in enumerate(VELOCITY) if v[:2] == c] for c in CLASSES}
Y0, Y1 = 8, 24
MID = slice(Y0, Y1)
ROWS = (16, 112, 104, 120, 16)


def quad(a, b):
    return QUAD[(min(a, b), max(a, b))]


def cross(a, b):
    return CROSS[(min(a, b), max(a, b))]


def roll_z(v, shift):
    return v if shift == 0 else pltpu.roll(v, shift % Z, v.ndim - 1)


def moments(f):
    m = [None] * 19
    s = [f[1 + 2 * a] + f[2 + 2 * a] for a in AXES]
    d = [f[1 + 2 * a] - f[2 + 2 * a] for a in AXES]
    for a, b in PAIRS:
        e = EDGE[a, b]
        al, ad = f[e] + f[e + 1], f[e] - f[e + 1]
        be, bd = f[e + 2] + f[e + 3], f[e + 2] - f[e + 3]
        m[CROSS[a, b]] = al - be
        m[QUAD[a, b]] = al + be
        m[CUBIC[a, b]] = ad + bd
        m[CUBIC[b, a]] = ad - bd
    for a in AXES:
        b, c = OTHERS[a]
        m[1 + a] = d[a] + (m[CUBIC[a, b]] + m[CUBIC[a, c]])
        m[7 + a] = s[a] + (m[quad(a, b)] + m[quad(a, c)])
    m[0] = (f[0] + s[0]) + (s[1] + s[2]) + (m[16] + m[17] + m[18])
    return m


def from_moments(p):
    f = [None] * 19
    for a in AXES:
        b, c = OTHERS[a]
        s = 0.5 * (p[7 + a] - (p[quad(a, b)] + p[quad(a, c)]))
        d = 0.5 * (p[1 + a] - (p[CUBIC[a, b]] + p[CUBIC[a, c]]))
        f[1 + 2 * a], f[2 + 2 * a] = s + d, s - d
    for a, b in PAIRS:
        e = EDGE[a, b]
        q, r = 0.25 * p[QUAD[a, b]], 0.25 * p[CROSS[a, b]]
        t, w = 0.25 * p[CUBIC[a, b]], 0.25 * p[CUBIC[b, a]]
        up, down, plus, minus = q + r, q - r, t + w, t - w
        f[e], f[e + 1], f[e + 2], f[e + 3] = up + plus, up - plus, down + minus, down - minus
    f[0] = p[0] - (p[7] + p[8] + p[9]) + (p[16] + p[17] + p[18])
    return f


def from_moments_t(lam):
    mu = [None] * 19
    mu[0] = lam[0]
    s = [0.5 * (lam[1 + 2 * a] + lam[2 + 2 * a]) for a in AXES]
    d = [0.5 * (lam[1 + 2 * a] - lam[2 + 2 * a]) for a in AXES]
    for a in AXES:
        mu[1 + a] = d[a]
        mu[7 + a] = s[a] - lam[0]
    for a, b in PAIRS:
        e = EDGE[a, b]
        al, ad = lam[e] + lam[e + 1], lam[e] - lam[e + 1]
        be, bd = lam[e + 2] + lam[e + 3], lam[e + 2] - lam[e + 3]
        mu[QUAD[a, b]] = 0.25 * (al + be) - s[a] - mu[7 + b]
        mu[CROSS[a, b]] = 0.25 * (al - be)
        mu[CUBIC[a, b]] = 0.25 * (ad + bd) - d[a]
        mu[CUBIC[b, a]] = 0.25 * (ad - bd) - d[b]
    return mu


def moments_t(nu):
    f = [None] * 19
    f[0] = nu[0]
    for a in AXES:
        s = nu[0] + nu[7 + a]
        f[1 + 2 * a], f[2 + 2 * a] = s + nu[1 + a], s - nu[1 + a]
    for a, b in PAIRS:
        e = EDGE[a, b]
        even = (nu[0] + nu[7 + a]) + (nu[7 + b] + nu[QUAD[a, b]])
        up, down = even + nu[CROSS[a, b]], even - nu[CROSS[a, b]]
        p, q = nu[1 + a] + nu[CUBIC[a, b]], nu[1 + b] + nu[CUBIC[b, a]]
        f[e], f[e + 1], f[e + 2], f[e + 3] = up + (p + q), up - (p + q), down + (p - q), down - (p - q)
    return f


def collide(f, psi, pull, inv, solid, rate):
    m = moments(f)
    rho = m[0]
    force = [5.0 * psi * g for g in pull]
    u = [(m[1 + a] + 0.5 * force[a]) * inv for a in AXES]
    n = [m[1 + a] - 0.5 * force[a] for a in AXES]
    p = [None] * 19
    p[0] = rho
    w = [u[a] * n[a] for a in AXES]
    t = [u[a] * force[a] for a in AXES]
    third = rho * (1.0 / 3.0)
    ninth = rho * (1.0 / 9.0)
    for a in AXES:
        p[1 + a] = m[1 + a] + force[a]
        k = 7 + a
        p[k] = m[k] + rate[k] * (third + w[a] - m[k]) + 2.0 * t[a]
    m3 = [m[1 + a] * (1.0 / 3.0) for a in AXES]
    f3 = [force[a] * (1.0 / 3.0) for a in AXES]
    for (a, b), k in CUBIC.items():
        p[k] = m[k] + rate[k] * (m3[a] - m[k]) + f3[a]
    w3 = [(1.0 / 3.0) * v for v in w]
    t3 = [(1.0 / 3.0) * v for v in t]
    for a, b in PAIRS:
        c = 3 - a - b
        k = CROSS[a, b]
        p[k] = m[k] + rate[k] * (0.5 * (u[b] * n[a] + u[a] * n[b]) - m[k]) + (u[a] * force[b] + u[b] * force[a])
        k = QUAD[a, b]
        p[k] = (
            m[k]
            + rate[k] * (ninth + (w3[a] + w3[b]) - 0.5 * w3[c] - m[k])
            + (2.0 * (t3[a] + t3[b]) - t3[c])
        )
    for k in range(1, 19):
        p[k] = jnp.where(solid, -m[k] if k in ODD else m[k], p[k])
    return from_moments(p), u, force


def adjoint_setup(lam, solid, rate):
    mu = from_moments_t(lam)
    e, nu, g = [None] * 19, [None] * 19, [None] * 19
    for k in (0,) + tuple(range(4, 19)):
        e[k] = rate[k] * mu[k]
        nu[k] = jnp.where(solid, -mu[k] if k in ODD else mu[k], mu[k] - e[k])
        g[k] = mu[k] - 0.5 * e[k]

    def diagonal(v):
        out = []
        for a in AXES:
            b, c = OTHERS[a]
            out.append(2.0 * v[7 + a] + (2.0 / 3.0) * (v[quad(a, b)] + v[quad(a, c)]) - (1.0 / 3.0) * v[quad(b, c)])
        return out

    def thirds(v):
        return [(1.0 / 3.0) * (v[CUBIC[a, OTHERS[a][0]]] + v[CUBIC[a, OTHERS[a][1]]]) for a in AXES]

    level = (
        e[0]
        + (1.0 / 3.0) * (e[7] + e[8] + e[9])
        + (1.0 / 9.0) * (e[16] + e[17] + e[18])
    )
    lift = [mu[1 + a] + v for a, v in enumerate(thirds(g))]
    return [nu[0]] + nu[4:] + mu[1:4] + diagonal(e) + e[4:7] + diagonal(g) + g[4:7] + thirds(e) + lift + [level]


SETUP = 38


def adjoint_finish(setup, u, force, inv, solid):
    nu = [setup[0], None, None, None] + list(setup[1:16])
    mu, ed, ec, gd, gc, push, lift = (setup[n : n + 3] for n in range(16, 37, 3))
    level = setup[37]

    def times(diag, off, x):
        out = []
        for a in AXES:
            b, c = OTHERS[a]
            out.append(diag[a] * x[a] + off[cross(a, b) - 4] * x[b] + off[cross(a, c) - 4] * x[c])
        return out

    eu, gu, gf = times(ed, ec, u), times(gd, gc, u), times(gd, gc, force)
    fbar = []
    for a in AXES:
        jbar = push[a] + eu[a] + gf[a] * inv
        nu[1 + a] = jnp.where(solid, -mu[a], mu[a] + jbar)
        fbar.append(jnp.where(solid, 0.0, lift[a] + gu[a] + 0.5 * jbar))
    rho_bar = (
        level
        - 0.5 * (u[0] * eu[0] + u[1] * eu[1] + u[2] * eu[2])
        - (force[0] * gu[0] + force[1] * gu[1] + force[2] * gu[2]) * inv
    )
    return nu, fbar, jnp.where(solid, 0.0, rho_bar)


class Row:
    def __init__(self, x, first=0, count=B):
        self.x, self.first, self.count = x, first, count

    def near(self, ext, a=0, b=0):
        y = Y0 + self.first + b
        return ext[self.x + 1 + a, y : y + self.count, :]

    def put(self, ext, v):
        y = Y0 + self.first
        ext[self.x + 1, y : y + self.count, :] = v

    def own(self, ref):
        return ref[self.x, self.first : self.first + self.count, :]

    def keep(self, ref, v):
        ref[self.x, self.first : self.first + self.count, :] = v


class Column:
    def __init__(self, y):
        self.y = y

    def near(self, ext, a=0, b=0):
        return flat(ext)[strip(Y0 + self.y + b, a), :]

    def put(self, ext, v):
        flat(ext)[strip(Y0 + self.y), :] = v

    def own(self, ref):
        return ref.reshape(H * B, Z)[pl.ds(self.y, H, stride=B), :]

    def keep(self, ref, v):
        ref.reshape(H * B, Z)[pl.ds(self.y, H, stride=B), :] = v


def neighbour_pull(ext, part):
    at = {(a, b): part.near(ext, a, b) for a, b in CLASSES}
    dx, dy = at[1, 0] - at[-1, 0], at[0, 1] - at[0, -1]
    main, other = at[1, 1] - at[-1, -1], at[1, -1] - at[-1, 1]
    total = FACE_W * at[0, 0] + EDGE_W * ((at[1, 0] + at[-1, 0]) + (at[0, 1] + at[0, -1]))
    gx = FACE_W * dx + EDGE_W * (main + other + (roll_z(dx, 1) + roll_z(dx, -1)))
    gy = FACE_W * dy + EDGE_W * (main - other + (roll_z(dy, 1) + roll_z(dy, -1)))
    return [gx, gy, roll_z(total, -1) - roll_z(total, 1)]


def spread_classes(p):
    px, py, pz = p
    up, down = roll_z(pz, 1), roll_z(pz, -1)
    turned = [EDGE_W * (roll_z(v, 1) + roll_z(v, -1)) + FACE_W * v for v in (px, py)]
    lift = EDGE_W * (up - down)
    both, apart = EDGE_W * (px + py), EDGE_W * (px - py)
    return {
        (0, 0): FACE_W * (up - down),
        (1, 0): turned[0] + lift, (-1, 0): lift - turned[0],
        (0, 1): turned[1] + lift, (0, -1): lift - turned[1],
        (1, 1): both, (-1, -1): -both, (1, -1): apart, (-1, 1): -apart,
    }


def chosen(d, orient):
    return [i for i, v in enumerate(VELOCITY) if all(d[n] == 0 or v[n] == orient * d[n] for n in (0, 1))]


def edge_of(d):
    return (1 if d[0] < 0 else H), (Y0 if d[1] < 0 else Y1 - 1)


def halo_of(d):
    return (0 if d[0] < 0 else H + 1), (Y0 - 1 if d[1] < 0 else Y1)


def strip(y, shift=0):
    return pl.ds((1 + shift) * 32 + y, H, stride=32)


def flat(ext):
    return ext.reshape((H + 2) * 32, Z)


def pack(sb, k, place, ext):
    d = DIRS[k]
    ex, ey = edge_of(d)
    if d[1] == 0:
        sb[k, place * B : (place + 1) * B, :] = ext[ex, MID, :]
    elif d[0] == 0:
        sb[k, place * H : (place + 1) * H, :] = flat(ext)[strip(ey), :]
    else:
        sb[k, place : place + 1, :] = ext[ex, ey : ey + 1, :]


def unpack(rb, k, place, ext):
    d = DIRS[k]
    hx, hy = halo_of((-d[0], -d[1]))
    if d[1] == 0:
        ext[hx, MID, :] = rb[k, place * B : (place + 1) * B, :]
    elif d[0] == 0:
        flat(ext)[strip(hy), :] = rb[k, place * H : (place + 1) * H, :]
    else:
        ext[hx, hy : hy + 1, :] = rb[k, place : place + 1, :]


def shifted(v, step):
    rows = v.shape[0]
    index = lax.broadcasted_iota(jnp.int32, v.shape, 0)
    return jnp.where(index == (0 if step > 0 else rows - 1), 0.0, pltpu.roll(v, step % rows, 0))


def line(t):
    size = t[0].shape[0]
    return t[0] + shifted(t[1], 1) + shifted(t[-1], -1), t[-1][0:1, :], t[1][size - 1 : size, :]


def size_of(d):
    return B if d[1] == 0 else H


def lines_towards(q, d):
    ex, ey = edge_of(d)
    if d[1] == 0:
        outer = {c: q[SLOT[d[0], c], ex, MID, :] for c in (-1, 0, 1)}
        behind = {c: q[SLOT[0, c], ex, MID, :] + q[SLOT[d[0], c], ex - d[0], MID, :] for c in (-1, 0, 1)}
    else:
        def column(c, y):
            return flat(q.at[SLOT[c]])[strip(y), :]

        outer = {c: column((c, d[1]), ey) for c in (-1, 0, 1)}
        behind = {c: column((c, 0), ey) + column((c, d[1]), ey - d[1]) for c in (-1, 0, 1)}
    return line(outer), line(behind)


def put_lines(sb, k, fields, lines, ends=True):
    s = size_of(DIRS[k])
    at = fields * s
    for n, (middle, low, high) in enumerate(lines):
        sb[k, at + n * s : at + (n + 1) * s, :] = middle
        if ends:
            e = at + len(lines) * s + 2 * n
            sb[k, e : e + 1, :] = low
            sb[k, e + 1 : e + 2, :] = high


def get_lines(rb, k, fields, count, ends=True):
    s = size_of(DIRS[k])
    at = fields * s
    out = []
    for n in range(count):
        e = at + count * s + 2 * n
        low, high = (rb[k, e : e + 1, :], rb[k, e + 1 : e + 2, :]) if ends else (None, None)
        out.append((rb[k, at + n * s : at + (n + 1) * s, :], low, high))
    return out


def put_corner(sb, k, place, q):
    dx, dy = DIRS[k]
    ex, ey = edge_of((dx, dy))

    def one(c, x, y):
        return q[SLOT[c], x, y : y + 1, :]

    across = (dx, dy)
    values = (
        one((0, 0), ex, ey) + one((dx, 0), ex - dx, ey) + one((0, dy), ex, ey - dy) + one(across, ex - dx, ey - dy),
        one((dx, 0), ex, ey) + one(across, ex, ey - dy),
        one((0, dy), ex, ey) + one(across, ex - dx, ey),
        one(across, ex, ey),
    )
    for n, v in enumerate(values):
        sb[k, place + n : place + n + 1, :] = v


def own_sum(q, out, border=True):
    for x in range(0 if border else 1, H + 2 if border else H + 1):
        total = None
        for c in CLASSES:
            if 1 <= x - c[0] <= H:
                v = q[SLOT[c], x - c[0], Y0 - c[1] : Y1 - c[1], :]
                total = v if total is None else total + v
        out[x, MID, :] = total
    if not border:
        return
    for d in DIRS:
        ex, ey = edge_of(d)
        hx, hy = halo_of(d)
        if d[0] == 0:
            total = None
            for c in (-1, 0, 1):
                v = flat(q.at[SLOT[c, d[1]]])[strip(ey, -c), :]
                total = v if total is None else total + v
            flat(out)[strip(hy), :] = total
        elif d[1] != 0:
            out[hx, hy : hy + 1, :] = q[SLOT[d], ex, ey : ey + 1, :]


def add_line(out, d, at, middle, low, high):
    if d[1] == 0:
        out[at, MID, :] += middle
        if low is not None:
            out[at, Y0 - 1 : Y0, :] += low
            out[at, Y1 : Y1 + 1, :] += high
    else:
        flat(out)[strip(at), :] += middle
        if low is not None:
            out[0, at : at + 1, :] += low
            out[H + 1, at : at + 1, :] += high


def add_arrived(rb, out, k, into, behind, fields):
    d = DIRS[k]
    back = (-d[0], -d[1])
    ex, ey = edge_of(back)
    hx, hy = halo_of(back)
    if d[0] == 0 or d[1] == 0:
        n = 1 if d[0] == 0 else 0
        add_line(out, d, (ex, ey)[n], *into)
        if behind is not None:
            add_line(out, d, (hx, hy)[n], *behind)
    elif behind is None:
        out[ex, ey : ey + 1, :] += into
    else:
        for n, (x, y) in enumerate(((hx, hy), (ex, hy), (hx, ey), (ex, ey))):
            out[x, y : y + 1, :] += rb[k, fields + n : fields + n + 1, :]


def kernel(
    nx, ny,
    table_hbm, rates_hbm, pops_hbm, mask_hbm, class_hbm, cot_hbm, base_out, density_out, wet_out,
    table, rates, pops, cot, mask, wall_class, state, setup,
    psi_ext, solid_ext, wall_ext, e2_ext, sum_ext, d_ext, q_ext, cot_ext, post_ext, base_ext,
    s0, s1, s2, s3, s4, r0, r1, r2, r3, r4,
    send_sem, recv_sem, local_sem,
):
    gx, gy = lax.axis_index("gx"), lax.axis_index("gy")
    sends, recvs = (s0, s1, s2, s3, s4), (r0, r1, r2, r3, r4)

    def device(d):
        return (lax.rem(gx + (d[0] + nx), nx), lax.rem(gy + (d[1] + ny), ny))

    barrier = pltpu.get_barrier_semaphore()
    for d in DIRS:
        pl.semaphore_signal(barrier, inc=1, device_id=device(d), device_id_type=MESH)

    loads = [
        pltpu.make_async_copy(src, dst, local_sem.at[n])
        for n, (src, dst) in enumerate(
            ((pops_hbm, pops), (mask_hbm, mask), (class_hbm, wall_class), (table_hbm, table), (rates_hbm, rates), (cot_hbm, cot))
        )
    ]
    for c in loads:
        c.start()

    def start(r, fields, ends=0, which=range(8)):
        copies = {}
        for k in which:
            d = DIRS[k]
            rows = pl.ds(0, fields * size_of(d) + ends if d[0] == 0 or d[1] == 0 else 8)
            c = pltpu.make_async_remote_copy(
                src_ref=sends[r].at[k, rows], dst_ref=recvs[r].at[k, rows],
                send_sem=send_sem.at[r, k], recv_sem=recv_sem.at[r, k],
                device_id=device(d), device_id_type=MESH,
            )
            c.start()
            copies[k] = c
        return copies

    def finish(copies, which=range(8)):
        for k in which:
            copies[k].wait()

    def each_row(body, first=0, last=H):
        def step(x, carry):
            body(Row(x))
            return carry

        lax.fori_loop(first, last, step, 0, unroll=last - first)

    def clear(x, carry):
        for n in range(9):
            q_ext[n, x] = jnp.zeros((32, Z), jnp.float32)
        return carry

    lax.fori_loop(0, H + 2, clear, 0)

    for c in loads[:5]:
        c.wait()
    rate = [rates[k] for k in range(19)]

    def prepare(part):
        f = [part.own(pops.at[i]) for i in range(19)]
        rho = f[0]
        for i in range(1, 19):
            rho = rho + f[i]
        solid = part.own(mask) == 1
        kind = part.own(wall_class)
        wall = jnp.full(rho.shape, table[0], jnp.float32)
        for n in range(1, 8):
            wall = jnp.where(kind == n, table[n], wall)
        fade = jnp.exp(-rho)
        part.put(psi_ext, jnp.where(solid, wall, 1.0 - fade))
        part.put(solid_ext, jnp.where(solid, 1.0, 0.0))
        part.put(wall_ext, wall)
        part.keep(state.at[0], 1.0 / rho)
        part.keep(state.at[11], jnp.where(solid, 0.0, fade))

    each_row(prepare)
    for k in range(8):
        pack(s0, k, 0, psi_ext)
    pl.semaphore_wait(barrier, len(DIRS))
    first = start(0, 1)

    loads[5].wait()

    def turn(part):
        for i, c in enumerate(VELOCITY):
            part.put(cot_ext.at[i], roll_z(part.own(cot.at[i]), -c[2]))

    each_row(turn)
    for k, d in enumerate(DIRS):
        ids = chosen(d, -1)
        for n, i in enumerate(ids):
            pack(s1, k, n, cot_ext.at[i])
        pack(s1, k, len(ids), solid_ext)
        pack(s1, k, len(ids) + 1, wall_ext)
    early = start(1, 7)

    def forward(part):
        psi = part.near(psi_ext)
        pull = neighbour_pull(psi_ext, part)
        f = [part.own(pops.at[i]) for i in range(19)]
        post, u, force = collide(f, psi, pull, part.own(state.at[0]), part.own(mask) == 1, rate)
        post = [roll_z(v, c[2]) for v, c in zip(post, VELOCITY)]
        for i in range(19):
            part.put(post_ext.at[i], post[i])
        for c in CLASSES:
            total = post[MEMBERS[c][0]]
            for i in MEMBERS[c][1:]:
                total = total + post[i]
            part.put(q_ext.at[SLOT[c]], total)
        for a in AXES:
            part.keep(state.at[1 + a], u[a])
            part.keep(state.at[4 + a], force[a])
            part.keep(state.at[7 + a], pull[a])
        part.keep(state.at[10], psi)

    each_row(forward, 1, H - 1)
    finish(first, BESIDE)
    for k in BESIDE:
        unpack(r0, k, 0, psi_ext)
    for part in (Column(0), Column(B - 1)):
        forward(part)
    finish(first, ACROSS)
    for k in ACROSS:
        unpack(r0, k, 0, psi_ext)
    second = {}
    for pair, ends in ((PAIR_A, ENDS_A), (PAIR_B, ENDS_B)):
        for x, y in ends:
            forward(Row(x, y, B // 2))
        for k in pair:
            pack(s2, k, 0, post_ext.at[chosen(DIRS[k], 1)[0]])
            put_corner(s2, k, 1, q_ext)
        second.update(start(2, 6, 8, pair))
    for k in BESIDE:
        d = DIRS[k]
        for n, i in enumerate(chosen(d, 1)):
            pack(s2, k, n, post_ext.at[i])
        put_lines(s2, k, 5, lines_towards(q_ext, d)[1:])
    second.update(start(2, 6, 8, BESIDE))

    own_sum(q_ext, sum_ext)
    finish(early)
    for k, d in enumerate(DIRS):
        ids = chosen(d, -1)
        for n, i in enumerate(ids):
            unpack(r1, k, n, cot_ext.at[i])
        unpack(r1, k, len(ids), solid_ext)
        unpack(r1, k, len(ids) + 1, wall_ext)

    def prepare_adjoint(part):
        lam = [part.near(cot_ext.at[i], c[0], c[1]) for i, c in enumerate(VELOCITY)]
        for n, v in enumerate(adjoint_setup(lam, part.own(mask) == 1, rate)):
            part.keep(setup.at[n], v)

    each_row(prepare_adjoint)
    finish(second, BESIDE)

    for k in BESIDE:
        d = DIRS[k]
        ids = chosen(d, 1)
        for n, i in enumerate(ids):
            unpack(r2, k, n, post_ext.at[i])
        s = size_of(d)
        parts = {}
        for n, i in enumerate(ids):
            c = VELOCITY[i][1 if d[1] == 0 else 0]
            v = r2[k, n * s : (n + 1) * s, :]
            parts[c] = parts[c] + v if c in parts else v
        add_arrived(r2, sum_ext, k, line(parts), get_lines(r2, k, 5, 1)[0], 5)

    def potential(x):
        solid = solid_ext[x] > 0.5
        fade = jnp.exp(-sum_ext[x])
        psi_ext[x] = jnp.where(solid, wall_ext[x], 1.0 - fade)
        e2_ext[x] = jnp.where(solid, 0.0, fade)

    for x in range(2, H):
        potential(x)

    def spread_out(fbar, psi, part):
        p = [5.0 * psi * v for v in fbar]
        for c, v in spread_classes(p).items():
            part.put(q_ext.at[SLOT[c]], v)

    def backward_second(part):
        inv = 1.0 / part.near(sum_ext)
        psi = part.near(psi_ext)
        solid = part.own(mask) == 1
        pull = neighbour_pull(psi_ext, part)
        force = [5.0 * psi * g for g in pull]
        f = [part.near(post_ext.at[i], -c[0], -c[1]) for i, c in enumerate(VELOCITY)]
        u = []
        for a in AXES:
            m = None
            for i, c in enumerate(VELOCITY):
                if c[a] == 1:
                    m = f[i] if m is None else m + f[i]
            for i, c in enumerate(VELOCITY):
                if c[a] == -1:
                    m = m - f[i]
            u.append((m + 0.5 * force[a]) * inv)
        ready = [part.own(setup.at[n]) for n in range(SETUP)]
        nu, fbar, rho_bar = adjoint_finish(ready, u, force, inv, solid)
        local = rho_bar + part.near(e2_ext) * (
            5.0 * (pull[0] * fbar[0] + pull[1] * fbar[1] + pull[2] * fbar[2])
        )
        part.keep(density_out.at[1], local)
        nu[0] = nu[0] + local
        for i, v in enumerate(moments_t(nu)):
            part.put(base_ext.at[i], roll_z(v, -VELOCITY[i][2]))
        spread_out(fbar, psi, part)

    each_row(backward_second, 2, H - 2)
    finish(second, ACROSS)
    for k in ACROSS:
        unpack(r2, k, 0, post_ext.at[chosen(DIRS[k], 1)[0]])
        add_arrived(r2, sum_ext, k, True, True, 1)
    for x in (0, 1, H, H + 1):
        potential(x)
    third = {}
    for pair, ends in ((PAIR_A, ENDS_A), (PAIR_B, ENDS_B)):
        for x, y in ends:
            backward_second(Row(x, y, B // 2))
            backward_second(Row(1 if x == 0 else H - 2, y, B // 2))
        for k in pair:
            pack(s3, k, 0, base_ext.at[chosen(DIRS[k], -1)[0]])
            put_corner(s3, k, 1, q_ext)
        third.update(start(3, 7, 8, pair))
    for k in BESIDE:
        d = DIRS[k]
        for n, i in enumerate(chosen(d, -1)):
            pack(s3, k, n, base_ext.at[i])
        put_lines(s3, k, 5, lines_towards(q_ext, d))
    third.update(start(3, 7, 8, BESIDE))
    own_sum(q_ext, sum_ext)
    finish(third, BESIDE)
    for k in BESIDE:
        for n, i in enumerate(chosen(DIRS[k], -1)):
            unpack(r3, k, n, base_ext.at[i])
        add_arrived(r3, sum_ext, k, *get_lines(r3, k, 5, 2), 5)

    def shift_second(x):
        v = e2_ext[x] * sum_ext[x]
        for c in (-1, 0, 1):
            d_ext[c + 1, x] = roll_z(v, -c)

    for x in range(2, H):
        shift_second(x)
    finish(third, ACROSS)
    for k in ACROSS:
        unpack(r3, k, 0, base_ext.at[chosen(DIRS[k], -1)[0]])
        add_arrived(r3, sum_ext, k, True, True, 1)
    for x in (0, 1, H, H + 1):
        shift_second(x)

    def backward_first(part):
        solid = part.own(mask) == 1
        inv, psi = part.own(state.at[0]), part.own(state.at[10])
        u = [part.own(state.at[1 + a]) for a in AXES]
        force = [part.own(state.at[4 + a]) for a in AXES]
        lam = [
            part.near(base_ext.at[i], c[0], c[1]) + part.near(d_ext.at[c[2] + 1], c[0], c[1])
            for i, c in enumerate(VELOCITY)
        ]
        nu, fbar, rho_bar = adjoint_finish(adjoint_setup(lam, solid, rate), u, force, inv, solid)
        spread_out(fbar, psi, part)
        if isinstance(part, Column):
            return
        pull = [part.own(state.at[7 + a]) for a in AXES]
        local = rho_bar + part.own(state.at[11]) * (
            5.0 * (pull[0] * fbar[0] + pull[1] * fbar[1] + pull[2] * fbar[2])
        )
        part.keep(density_out.at[0], local)
        nu[0] = nu[0] + local
        for i, v in enumerate(moments_t(nu)):
            part.keep(base_out.at[i], v)

    last = {}
    for pair, ends in ((PAIR_A, ENDS_A), (PAIR_B, ENDS_B)):
        for x, y in ends:
            backward_first(Row(x, y, B // 2))
        for k in pair:
            pack(s4, k, 0, q_ext.at[SLOT[DIRS[k]]])
        last.update(start(4, 1, 0, pair))
    for y in (0, B - 1):
        backward_first(Column(y))
    for k in BESIDE:
        put_lines(s4, k, 0, lines_towards(q_ext, DIRS[k])[:1], False)
    last.update(start(4, 1, 0, BESIDE))

    def spread_second(part):
        total = part.near(sum_ext)
        part.keep(density_out.at[1], part.own(density_out.at[1]) + part.near(d_ext.at[1]))
        part.keep(wet_out, jnp.where(part.own(mask) == 1, total, 0.0))

    each_row(spread_second)
    each_row(backward_first, 1, H - 1)
    own_sum(q_ext, sum_ext, False)
    finish(last, BESIDE)
    for k in BESIDE:
        add_arrived(r4, sum_ext, k, get_lines(r4, k, 0, 1, False)[0], None, 0)

    def spread_first(part):
        total = part.near(sum_ext)
        change = part.own(state.at[11]) * total
        part.keep(density_out.at[0], part.own(density_out.at[0]) + change)
        part.keep(wet_out, part.own(wet_out) + jnp.where(part.own(mask) == 1, total, 0.0))
        for i in range(19):
            part.keep(base_out.at[i], part.own(base_out.at[i]) + change)

    each_row(spread_first, 1, H - 1)
    finish(last, ACROSS)
    for k in ACROSS:
        add_arrived(r4, sum_ext, k, r4[k, 0:1, :], None, 0)
    for x in (0, H - 1):
        spread_first(Row(x))


def closing(adjoint, density, wet, adjoint_hbm, density_hbm, wet_hbm, sems):
    copies = [
        pltpu.make_async_copy(adjoint.at[pl.ds(n, 4 if n < 16 else 3)], adjoint_hbm.at[pl.ds(n, 4 if n < 16 else 3)], sems.at[n // 4])
        for n in range(0, 19, 4)
    ]
    copies.append(pltpu.make_async_copy(density, density_hbm, sems.at[10]))
    copies.append(pltpu.make_async_copy(wet, wet_hbm, sems.at[11]))
    for c in copies:
        c.start()
    for c in copies:
        c.wait()


def body(populations, solid_mask, wall_class, wall_table, relax_rates, pop_cotangent):
    f32 = jnp.float32
    nx, ny = lax.axis_size("gx"), lax.axis_size("gy")
    block = (H, B, Z)
    ext = (H + 2, 32, Z)
    anywhere = pl.BlockSpec(memory_space=pl.ANY)
    vmem = pltpu.VMEM
    far = [
        pltpu.with_memory_space_constraint(v, pltpu.HBM)
        for v in (wall_table, relax_rates, populations, solid_mask, wall_class, pop_cotangent)
    ]
    results = pl.pallas_call(
        functools.partial(kernel, nx, ny),
        out_shape=(
            vmem((19,) + block, f32),
            vmem((2,) + block, f32),
            vmem(block, f32),
        ),
        in_specs=[anywhere] * 6,
        out_specs=(pl.BlockSpec(memory_space=vmem),) * 3,
        scratch_shapes=[
            pltpu.SMEM((8,), f32),
            pltpu.SMEM((19,), f32),
            vmem((19,) + block, f32),
            vmem((19,) + block, f32),
            vmem(block, jnp.int32),
            vmem(block, jnp.int32),
            vmem((12,) + block, f32),
            vmem((SETUP,) + block, f32),
            vmem(ext, f32), vmem(ext, f32), vmem(ext, f32), vmem(ext, f32), vmem(ext, f32),
            vmem((3,) + ext, f32),
            vmem((9,) + ext, f32),
            vmem((19,) + ext, f32),
            vmem((19,) + ext, f32),
            vmem((19,) + ext, f32),
        ]
        + [vmem((8, n, Z), f32) for n in ROWS] * 2
        + [
            pltpu.SemaphoreType.DMA((5, 8)),
            pltpu.SemaphoreType.DMA((5, 8)),
            pltpu.SemaphoreType.DMA((6,)),
        ],
        compiler_params=pltpu.CompilerParams(
            collective_id=0, has_side_effects=True, vmem_limit_bytes=40 * 2**20
        ),
    )(*far)
    return pl.pallas_call(
        closing,
        out_shape=tuple(jax.ShapeDtypeStruct(v.shape, f32) for v in results),
        in_specs=[pl.BlockSpec(memory_space=vmem)] * 3,
        out_specs=(anywhere,) * 3,
        scratch_shapes=[pltpu.SemaphoreType.DMA((12,))],
        compiler_params=pltpu.CompilerParams(vmem_limit_bytes=8 * 2**20),
    )(*results)


def solution(mesh):
    in_specs = (
        P(None, "gx", "gy", None),
        P("gx", "gy", None),
        P("gx", "gy", None),
        P(),
        P(),
        P(None, "gx", "gy", None),
    )
    out_specs = (P(None, "gx", "gy", None), P(None, "gx", "gy", None), P("gx", "gy", None))
    return jax.shard_map(body, mesh=mesh, in_specs=in_specs, out_specs=out_specs, check_vma=False)
```

```python
import functools

import jax
import jax.numpy as jnp
from jax import lax
from jax.experimental import pallas as pl
from jax.experimental.pallas import tpu as pltpu
from jax.sharding import PartitionSpec as P

MESH = pl.DeviceIdType.MESH
VELOCITY = [
    (0, 0, 0),
    (1, 0, 0), (-1, 0, 0), (0, 1, 0), (0, -1, 0), (0, 0, 1), (0, 0, -1),
    (1, 1, 0), (-1, -1, 0), (1, -1, 0), (-1, 1, 0),
    (1, 0, 1), (-1, 0, -1), (1, 0, -1), (-1, 0, 1),
    (0, 1, 1), (0, -1, -1), (0, 1, -1), (0, -1, 1),
]
FACE_W, EDGE_W = 1.0 / 18.0, 1.0 / 36.0
AXES = (0, 1, 2)
PAIRS = ((0, 1), (0, 2), (1, 2))
H, B, Z = 8, 16, 128
CROSS = {(0, 1): 4, (0, 2): 5, (1, 2): 6}
QUAD = {(0, 1): 16, (0, 2): 17, (1, 2): 18}
CUBIC = {(0, 1): 10, (0, 2): 11, (1, 0): 12, (1, 2): 13, (2, 0): 14, (2, 1): 15}
EDGE = {(0, 1): 7, (0, 2): 11, (1, 2): 15}
ODD = (1, 2, 3, 10, 11, 12, 13, 14, 15)
OTHERS = {0: (1, 2), 1: (0, 2), 2: (0, 1)}
DIRS = ((-1, -1), (1, 1), (-1, 1), (1, -1), (-1, 0), (1, 0), (0, -1), (0, 1))
CLASSES = [(a, b) for a in (-1, 0, 1) for b in (-1, 0, 1)]
ACROSS, BESIDE = range(4), range(4, 8)
PAIR_A, PAIR_B = range(2), range(2, 4)
ENDS_A, ENDS_B = ((0, 0), (H - 1, B // 2)), ((0, B // 2), (H - 1, 0))
SLOT = {c: n for n, c in enumerate(CLASSES)}
MEMBERS = {c: [i for i, v in enumerate(VELOCITY) if v[:2] == c] for c in CLASSES}
WIDE, TALL = 40, 24
Y0, Y1 = 8, 24
MID = slice(Y0, Y1)
ROWS = (16, 112, 104, 120, 16)


def quad(a, b):
    return QUAD[(min(a, b), max(a, b))]


def cross(a, b):
    return CROSS[(min(a, b), max(a, b))]


def roll_z(v, shift):
    return v if shift == 0 else pltpu.roll(v, shift % Z, v.ndim - 1)


def moments(f):
    m = [None] * 19
    s = [f[1 + 2 * a] + f[2 + 2 * a] for a in AXES]
    d = [f[1 + 2 * a] - f[2 + 2 * a] for a in AXES]
    for a, b in PAIRS:
        e = EDGE[a, b]
        al, ad = f[e] + f[e + 1], f[e] - f[e + 1]
        be, bd = f[e + 2] + f[e + 3], f[e + 2] - f[e + 3]
        m[CROSS[a, b]] = al - be
        m[QUAD[a, b]] = al + be
        m[CUBIC[a, b]] = ad + bd
        m[CUBIC[b, a]] = ad - bd
    for a in AXES:
        b, c = OTHERS[a]
        m[1 + a] = d[a] + (m[CUBIC[a, b]] + m[CUBIC[a, c]])
        m[7 + a] = s[a] + (m[quad(a, b)] + m[quad(a, c)])
    m[0] = (f[0] + s[0]) + (s[1] + s[2]) + (m[16] + m[17] + m[18])
    return m


def from_moments(p):
    f = [None] * 19
    for a in AXES:
        b, c = OTHERS[a]
        s = 0.5 * (p[7 + a] - (p[quad(a, b)] + p[quad(a, c)]))
        d = 0.5 * (p[1 + a] - (p[CUBIC[a, b]] + p[CUBIC[a, c]]))
        f[1 + 2 * a], f[2 + 2 * a] = s + d, s - d
    for a, b in PAIRS:
        e = EDGE[a, b]
        q, r = 0.25 * p[QUAD[a, b]], 0.25 * p[CROSS[a, b]]
        t, w = 0.25 * p[CUBIC[a, b]], 0.25 * p[CUBIC[b, a]]
        up, down, plus, minus = q + r, q - r, t + w, t - w
        f[e], f[e + 1], f[e + 2], f[e + 3] = up + plus, up - plus, down + minus, down - minus
    f[0] = p[0] - (p[7] + p[8] + p[9]) + (p[16] + p[17] + p[18])
    return f


def from_moments_t(lam):
    mu = [None] * 19
    mu[0] = lam[0]
    s = [0.5 * (lam[1 + 2 * a] + lam[2 + 2 * a]) for a in AXES]
    d = [0.5 * (lam[1 + 2 * a] - lam[2 + 2 * a]) for a in AXES]
    for a in AXES:
        mu[1 + a] = d[a]
        mu[7 + a] = s[a] - lam[0]
    for a, b in PAIRS:
        e = EDGE[a, b]
        al, ad = lam[e] + lam[e + 1], lam[e] - lam[e + 1]
        be, bd = lam[e + 2] + lam[e + 3], lam[e + 2] - lam[e + 3]
        mu[QUAD[a, b]] = 0.25 * (al + be) - s[a] - mu[7 + b]
        mu[CROSS[a, b]] = 0.25 * (al - be)
        mu[CUBIC[a, b]] = 0.25 * (ad + bd) - d[a]
        mu[CUBIC[b, a]] = 0.25 * (ad - bd) - d[b]
    return mu


def moments_t(nu):
    f = [None] * 19
    f[0] = nu[0]
    for a in AXES:
        s = nu[0] + nu[7 + a]
        f[1 + 2 * a], f[2 + 2 * a] = s + nu[1 + a], s - nu[1 + a]
    for a, b in PAIRS:
        e = EDGE[a, b]
        even = (nu[0] + nu[7 + a]) + (nu[7 + b] + nu[QUAD[a, b]])
        up, down = even + nu[CROSS[a, b]], even - nu[CROSS[a, b]]
        p, q = nu[1 + a] + nu[CUBIC[a, b]], nu[1 + b] + nu[CUBIC[b, a]]
        f[e], f[e + 1], f[e + 2], f[e + 3] = up + (p + q), up - (p + q), down + (p - q), down - (p - q)
    return f


def collide(f, psi, pull, inv, solid, rate):
    m = moments(f)
    rho = m[0]
    force = [5.0 * psi * g for g in pull]
    u = [(m[1 + a] + 0.5 * force[a]) * inv for a in AXES]
    n = [m[1 + a] - 0.5 * force[a] for a in AXES]
    p = [None] * 19
    p[0] = rho
    w = [u[a] * n[a] for a in AXES]
    t = [u[a] * force[a] for a in AXES]
    third = rho * (1.0 / 3.0)
    ninth = rho * (1.0 / 9.0)
    for a in AXES:
        p[1 + a] = m[1 + a] + force[a]
        k = 7 + a
        p[k] = m[k] + rate[k] * (third + w[a] - m[k]) + 2.0 * t[a]
    m3 = [m[1 + a] * (1.0 / 3.0) for a in AXES]
    f3 = [force[a] * (1.0 / 3.0) for a in AXES]
    for (a, b), k in CUBIC.items():
        p[k] = m[k] + rate[k] * (m3[a] - m[k]) + f3[a]
    w3 = [(1.0 / 3.0) * v for v in w]
    t3 = [(1.0 / 3.0) * v for v in t]
    for a, b in PAIRS:
        c = 3 - a - b
        k = CROSS[a, b]
        p[k] = m[k] + rate[k] * (0.5 * (u[b] * n[a] + u[a] * n[b]) - m[k]) + (u[a] * force[b] + u[b] * force[a])
        k = QUAD[a, b]
        p[k] = (
            m[k]
            + rate[k] * (ninth + (w3[a] + w3[b]) - 0.5 * w3[c] - m[k])
            + (2.0 * (t3[a] + t3[b]) - t3[c])
        )
    for k in range(1, 19):
        p[k] = jnp.where(solid, -m[k] if k in ODD else m[k], p[k])
    return from_moments(p), u, force


def adjoint_setup(lam, solid, rate):
    mu = from_moments_t(lam)
    e, nu, g = [None] * 19, [None] * 19, [None] * 19
    for k in (0,) + tuple(range(4, 19)):
        e[k] = rate[k] * mu[k]
        nu[k] = jnp.where(solid, -mu[k] if k in ODD else mu[k], mu[k] - e[k])
        g[k] = mu[k] - 0.5 * e[k]

    def diagonal(v):
        out = []
        for a in AXES:
            b, c = OTHERS[a]
            out.append(2.0 * v[7 + a] + (2.0 / 3.0) * (v[quad(a, b)] + v[quad(a, c)]) - (1.0 / 3.0) * v[quad(b, c)])
        return out

    def thirds(v):
        return [(1.0 / 3.0) * (v[CUBIC[a, OTHERS[a][0]]] + v[CUBIC[a, OTHERS[a][1]]]) for a in AXES]

    level = (
        e[0]
        + (1.0 / 3.0) * (e[7] + e[8] + e[9])
        + (1.0 / 9.0) * (e[16] + e[17] + e[18])
    )
    lift = [mu[1 + a] + v for a, v in enumerate(thirds(g))]
    return [nu[0]] + nu[4:] + mu[1:4] + diagonal(e) + e[4:7] + diagonal(g) + g[4:7] + thirds(e) + lift + [level]


SETUP = 38


def adjoint_finish(setup, u, force, inv, solid):
    nu = [setup[0], None, None, None] + list(setup[1:16])
    mu, ed, ec, gd, gc, push, lift = (setup[n : n + 3] for n in range(16, 37, 3))
    level = setup[37]

    def times(diag, off, x):
        out = []
        for a in AXES:
            b, c = OTHERS[a]
            out.append(diag[a] * x[a] + off[cross(a, b) - 4] * x[b] + off[cross(a, c) - 4] * x[c])
        return out

    eu, gu, gf = times(ed, ec, u), times(gd, gc, u), times(gd, gc, force)
    fbar = []
    for a in AXES:
        jbar = push[a] + eu[a] + gf[a] * inv
        nu[1 + a] = jnp.where(solid, -mu[a], mu[a] + jbar)
        fbar.append(jnp.where(solid, 0.0, lift[a] + gu[a] + 0.5 * jbar))
    rho_bar = (
        level
        - 0.5 * (u[0] * eu[0] + u[1] * eu[1] + u[2] * eu[2])
        - (force[0] * gu[0] + force[1] * gu[1] + force[2] * gu[2]) * inv
    )
    return nu, fbar, jnp.where(solid, 0.0, rho_bar)


class Row:
    def __init__(self, x, first=0, count=B):
        self.x, self.first, self.count = x, first, count

    def near(self, ext, a=0, b=0):
        y = Y0 + self.first + b
        return ext[self.x + 1 + a, y : y + self.count, :]

    def put(self, ext, v):
        y = Y0 + self.first
        ext[self.x + 1, y : y + self.count, :] = v

    def own(self, ref):
        return ref[self.x, self.first : self.first + self.count, :]

    def keep(self, ref, v):
        ref[self.x, self.first : self.first + self.count, :] = v


class Column:
    def __init__(self, y):
        self.y = y

    def near(self, ext, a=0, b=0):
        return flat(ext)[strip(Y0 + self.y + b, a), :]

    def put(self, ext, v):
        flat(ext)[strip(Y0 + self.y), :] = v

    def own(self, ref):
        return ref.reshape(H * TALL, Z)[pl.ds(self.y, H, stride=TALL), :]

    def keep(self, ref, v):
        ref.reshape(H * TALL, Z)[pl.ds(self.y, H, stride=TALL), :] = v


def neighbour_pull(ext, part):
    at = {(a, b): part.near(ext, a, b) for a, b in CLASSES}
    dx, dy = at[1, 0] - at[-1, 0], at[0, 1] - at[0, -1]
    main, other = at[1, 1] - at[-1, -1], at[1, -1] - at[-1, 1]
    total = FACE_W * at[0, 0] + EDGE_W * ((at[1, 0] + at[-1, 0]) + (at[0, 1] + at[0, -1]))
    gx = FACE_W * dx + EDGE_W * (main + other + (roll_z(dx, 1) + roll_z(dx, -1)))
    gy = FACE_W * dy + EDGE_W * (main - other + (roll_z(dy, 1) + roll_z(dy, -1)))
    return [gx, gy, roll_z(total, -1) - roll_z(total, 1)]


def spread_classes(p):
    px, py, pz = p
    up, down = roll_z(pz, 1), roll_z(pz, -1)
    turned = [EDGE_W * (roll_z(v, 1) + roll_z(v, -1)) + FACE_W * v for v in (px, py)]
    lift = EDGE_W * (up - down)
    both, apart = EDGE_W * (px + py), EDGE_W * (px - py)
    return {
        (0, 0): FACE_W * (up - down),
        (1, 0): turned[0] + lift, (-1, 0): lift - turned[0],
        (0, 1): turned[1] + lift, (0, -1): lift - turned[1],
        (1, 1): both, (-1, -1): -both, (1, -1): apart, (-1, 1): -apart,
    }


def chosen(d, orient):
    return [i for i, v in enumerate(VELOCITY) if all(d[n] == 0 or v[n] == orient * d[n] for n in (0, 1))]


def edge_of(d):
    return (1 if d[0] < 0 else H), (Y0 if d[1] < 0 else Y1 - 1)


def halo_of(d):
    return (0 if d[0] < 0 else H + 1), (Y0 - 1 if d[1] < 0 else Y1)


def strip(y, shift=0):
    return pl.ds((1 + shift) * WIDE + y, H, stride=WIDE)


def flat(ext):
    return ext.reshape((H + 2) * WIDE, Z)


def pack(sb, k, place, ext):
    d = DIRS[k]
    ex, ey = edge_of(d)
    if d[1] == 0:
        sb[k, place * B : (place + 1) * B, :] = ext[ex, MID, :]
    elif d[0] == 0:
        sb[k, place * H : (place + 1) * H, :] = flat(ext)[strip(ey), :]
    else:
        sb[k, place : place + 1, :] = ext[ex, ey : ey + 1, :]


def unpack(rb, k, place, ext):
    d = DIRS[k]
    hx, hy = halo_of((-d[0], -d[1]))
    if d[1] == 0:
        ext[hx, MID, :] = rb[k, place * B : (place + 1) * B, :]
    elif d[0] == 0:
        flat(ext)[strip(hy), :] = rb[k, place * H : (place + 1) * H, :]
    else:
        ext[hx, hy : hy + 1, :] = rb[k, place : place + 1, :]


def shifted(v, step):
    rows = v.shape[0]
    index = lax.broadcasted_iota(jnp.int32, v.shape, 0)
    return jnp.where(index == (0 if step > 0 else rows - 1), 0.0, pltpu.roll(v, step % rows, 0))


def line(t):
    size = t[0].shape[0]
    return t[0] + shifted(t[1], 1) + shifted(t[-1], -1), t[-1][0:1, :], t[1][size - 1 : size, :]


def size_of(d):
    return B if d[1] == 0 else H


def lines_towards(q, d):
    ex, ey = edge_of(d)
    if d[1] == 0:
        outer = {c: q[SLOT[d[0], c], ex, MID, :] for c in (-1, 0, 1)}
        behind = {c: q[SLOT[0, c], ex, MID, :] + q[SLOT[d[0], c], ex - d[0], MID, :] for c in (-1, 0, 1)}
    else:
        def column(c, y):
            return flat(q.at[SLOT[c]])[strip(y), :]

        outer = {c: column((c, d[1]), ey) for c in (-1, 0, 1)}
        behind = {c: column((c, 0), ey) + column((c, d[1]), ey - d[1]) for c in (-1, 0, 1)}
    return line(outer), line(behind)


def put_lines(sb, k, fields, lines, ends=True):
    s = size_of(DIRS[k])
    at = fields * s
    for n, (middle, low, high) in enumerate(lines):
        sb[k, at + n * s : at + (n + 1) * s, :] = middle
        if ends:
            e = at + len(lines) * s + 2 * n
            sb[k, e : e + 1, :] = low
            sb[k, e + 1 : e + 2, :] = high


def get_lines(rb, k, fields, count, ends=True):
    s = size_of(DIRS[k])
    at = fields * s
    out = []
    for n in range(count):
        e = at + count * s + 2 * n
        low, high = (rb[k, e : e + 1, :], rb[k, e + 1 : e + 2, :]) if ends else (None, None)
        out.append((rb[k, at + n * s : at + (n + 1) * s, :], low, high))
    return out


def put_corner(sb, k, place, q):
    dx, dy = DIRS[k]
    ex, ey = edge_of((dx, dy))

    def one(c, x, y):
        return q[SLOT[c], x, y : y + 1, :]

    across = (dx, dy)
    values = (
        one((0, 0), ex, ey) + one((dx, 0), ex - dx, ey) + one((0, dy), ex, ey - dy) + one(across, ex - dx, ey - dy),
        one((dx, 0), ex, ey) + one(across, ex, ey - dy),
        one((0, dy), ex, ey) + one(across, ex - dx, ey),
        one(across, ex, ey),
    )
    for n, v in enumerate(values):
        sb[k, place + n : place + n + 1, :] = v


def own_sum(q, out, border=True):
    for x in range(0 if border else 1, H + 2 if border else H + 1):
        total = None
        for c in CLASSES:
            if 1 <= x - c[0] <= H:
                v = q[SLOT[c], x - c[0], Y0 - c[1] : Y1 - c[1], :]
                total = v if total is None else total + v
        out[x, MID, :] = total
    if not border:
        return
    for d in DIRS:
        ex, ey = edge_of(d)
        hx, hy = halo_of(d)
        if d[0] == 0:
            total = None
            for c in (-1, 0, 1):
                v = flat(q.at[SLOT[c, d[1]]])[strip(ey, -c), :]
                total = v if total is None else total + v
            flat(out)[strip(hy), :] = total
        elif d[1] != 0:
            out[hx, hy : hy + 1, :] = q[SLOT[d], ex, ey : ey + 1, :]


def add_line(out, d, at, middle, low, high):
    if d[1] == 0:
        out[at, MID, :] += middle
        if low is not None:
            out[at, Y0 - 1 : Y0, :] += low
            out[at, Y1 : Y1 + 1, :] += high
    else:
        flat(out)[strip(at), :] += middle
        if low is not None:
            out[0, at : at + 1, :] += low
            out[H + 1, at : at + 1, :] += high


def add_arrived(rb, out, k, into, behind, fields):
    d = DIRS[k]
    back = (-d[0], -d[1])
    ex, ey = edge_of(back)
    hx, hy = halo_of(back)
    if d[0] == 0 or d[1] == 0:
        n = 1 if d[0] == 0 else 0
        add_line(out, d, (ex, ey)[n], *into)
        if behind is not None:
            add_line(out, d, (hx, hy)[n], *behind)
    elif behind is None:
        out[ex, ey : ey + 1, :] += into
    else:
        for n, (x, y) in enumerate(((hx, hy), (ex, hy), (hx, ey), (ex, ey))):
            out[x, y : y + 1, :] += rb[k, fields + n : fields + n + 1, :]


def kernel(
    nx, ny,
    table_hbm, rates_hbm, pops_hbm, mask_hbm, class_hbm, cot_hbm, base_out, density_out, wet_out,
    table, rates, pops, cot, mask, wall_class, state, setup,
    psi_ext, solid_ext, wall_ext, e2_ext, sum_ext, d_ext, q_ext, cot_ext, post_ext, base_ext,
    s0, s1, s2, s3, s4, r0, r1, r2, r3, r4,
    send_sem, recv_sem, local_sem,
):
    gx, gy = lax.axis_index("gx"), lax.axis_index("gy")
    sends, recvs = (s0, s1, s2, s3, s4), (r0, r1, r2, r3, r4)

    def device(d):
        return (lax.rem(gx + (d[0] + nx), nx), lax.rem(gy + (d[1] + ny), ny))

    barrier = pltpu.get_barrier_semaphore()
    for d in DIRS:
        pl.semaphore_signal(barrier, inc=1, device_id=device(d), device_id_type=MESH)

    loads = [
        pltpu.make_async_copy(src, dst, local_sem.at[n])
        for n, (src, dst) in enumerate(
            ((pops_hbm, pops.at[:, :, pl.ds(0, B)]), (mask_hbm, mask.at[:, pl.ds(0, B)]), (class_hbm, wall_class), (table_hbm, table), (rates_hbm, rates), (cot_hbm, cot))
        )
    ]
    for c in loads:
        c.start()

    def start(r, fields, ends=0, which=range(8)):
        copies = {}
        for k in which:
            d = DIRS[k]
            rows = pl.ds(0, fields * size_of(d) + ends if d[0] == 0 or d[1] == 0 else 8)
            c = pltpu.make_async_remote_copy(
                src_ref=sends[r].at[k, rows], dst_ref=recvs[r].at[k, rows],
                send_sem=send_sem.at[r, k], recv_sem=recv_sem.at[r, k],
                device_id=device(d), device_id_type=MESH,
            )
            c.start()
            copies[k] = c
        return copies

    def finish(copies, which=range(8)):
        for k in which:
            copies[k].wait()

    def each_row(body, first=0, last=H):
        def step(x, carry):
            body(Row(x))
            return carry

        lax.fori_loop(first, last, step, 0, unroll=last - first)

    def clear(x, carry):
        for n in range(9):
            q_ext[n, x] = jnp.zeros((WIDE, Z), jnp.float32)
        return carry

    lax.fori_loop(0, H + 2, clear, 0)

    for c in loads[:5]:
        c.wait()
    rate = [rates[k] for k in range(19)]

    def prepare(part):
        f = [part.own(pops.at[i]) for i in range(19)]
        rho = f[0]
        for i in range(1, 19):
            rho = rho + f[i]
        solid = part.own(mask) == 1
        kind = part.own(wall_class)
        wall = jnp.full(rho.shape, table[0], jnp.float32)
        for n in range(1, 8):
            wall = jnp.where(kind == n, table[n], wall)
        fade = jnp.exp(-rho)
        part.put(psi_ext, jnp.where(solid, wall, 1.0 - fade))
        part.put(solid_ext, jnp.where(solid, 1.0, 0.0))
        part.put(wall_ext, wall)
        part.keep(state.at[0], 1.0 / rho)
        part.keep(state.at[11], jnp.where(solid, 0.0, fade))

    each_row(prepare)
    for k in range(8):
        pack(s0, k, 0, psi_ext)
    pl.semaphore_wait(barrier, len(DIRS))
    first = start(0, 1)

    loads[5].wait()

    def turn(part):
        for i, c in enumerate(VELOCITY):
            part.put(cot_ext.at[i], roll_z(part.own(cot.at[i]), -c[2]))

    each_row(turn)
    for k, d in enumerate(DIRS):
        ids = chosen(d, -1)
        for n, i in enumerate(ids):
            pack(s1, k, n, cot_ext.at[i])
        pack(s1, k, len(ids), solid_ext)
        pack(s1, k, len(ids) + 1, wall_ext)
    early = start(1, 7)

    def forward(part):
        psi = part.near(psi_ext)
        pull = neighbour_pull(psi_ext, part)
        f = [part.own(pops.at[i]) for i in range(19)]
        post, u, force = collide(f, psi, pull, part.own(state.at[0]), part.own(mask) == 1, rate)
        post = [roll_z(v, c[2]) for v, c in zip(post, VELOCITY)]
        for i in range(19):
            part.put(post_ext.at[i], post[i])
        for c in CLASSES:
            total = post[MEMBERS[c][0]]
            for i in MEMBERS[c][1:]:
                total = total + post[i]
            part.put(q_ext.at[SLOT[c]], total)
        for a in AXES:
            part.keep(state.at[1 + a], u[a])
            part.keep(state.at[4 + a], force[a])
            part.keep(state.at[7 + a], pull[a])
        part.keep(state.at[10], psi)

    each_row(forward, 1, H - 1)
    finish(first, BESIDE)
    for k in BESIDE:
        unpack(r0, k, 0, psi_ext)
    for part in (Column(0), Column(B - 1)):
        forward(part)
    finish(first, ACROSS)
    for k in ACROSS:
        unpack(r0, k, 0, psi_ext)
    second = {}
    for pair, ends in ((PAIR_A, ENDS_A), (PAIR_B, ENDS_B)):
        for x, y in ends:
            forward(Row(x, y, B // 2))
        for k in pair:
            pack(s2, k, 0, post_ext.at[chosen(DIRS[k], 1)[0]])
            put_corner(s2, k, 1, q_ext)
        second.update(start(2, 6, 8, pair))
    for k in BESIDE:
        d = DIRS[k]
        for n, i in enumerate(chosen(d, 1)):
            pack(s2, k, n, post_ext.at[i])
        put_lines(s2, k, 5, lines_towards(q_ext, d)[1:])
    second.update(start(2, 6, 8, BESIDE))

    own_sum(q_ext, sum_ext)
    finish(early)
    for k, d in enumerate(DIRS):
        ids = chosen(d, -1)
        for n, i in enumerate(ids):
            unpack(r1, k, n, cot_ext.at[i])
        unpack(r1, k, len(ids), solid_ext)
        unpack(r1, k, len(ids) + 1, wall_ext)

    def prepare_adjoint(part):
        lam = [part.near(cot_ext.at[i], c[0], c[1]) for i, c in enumerate(VELOCITY)]
        for n, v in enumerate(adjoint_setup(lam, part.own(mask) == 1, rate)):
            part.keep(setup.at[n], v)

    each_row(prepare_adjoint)
    finish(second, BESIDE)

    for k in BESIDE:
        d = DIRS[k]
        ids = chosen(d, 1)
        for n, i in enumerate(ids):
            unpack(r2, k, n, post_ext.at[i])
        s = size_of(d)
        parts = {}
        for n, i in enumerate(ids):
            c = VELOCITY[i][1 if d[1] == 0 else 0]
            v = r2[k, n * s : (n + 1) * s, :]
            parts[c] = parts[c] + v if c in parts else v
        add_arrived(r2, sum_ext, k, line(parts), get_lines(r2, k, 5, 1)[0], 5)

    used = slice(0, 32)

    def potential(x):
        solid = solid_ext[x, used, :] > 0.5
        fade = jnp.exp(-sum_ext[x, used, :])
        psi_ext[x, used, :] = jnp.where(solid, wall_ext[x, used, :], 1.0 - fade)
        e2_ext[x, used, :] = jnp.where(solid, 0.0, fade)

    for x in range(2, H):
        potential(x)

    def spread_out(fbar, psi, part):
        p = [5.0 * psi * v for v in fbar]
        for c, v in spread_classes(p).items():
            part.put(q_ext.at[SLOT[c]], v)

    def backward_second(part):
        inv = 1.0 / part.near(sum_ext)
        psi = part.near(psi_ext)
        solid = part.own(mask) == 1
        pull = neighbour_pull(psi_ext, part)
        force = [5.0 * psi * g for g in pull]
        f = [part.near(post_ext.at[i], -c[0], -c[1]) for i, c in enumerate(VELOCITY)]
        u = []
        for a in AXES:
            m = None
            for i, c in enumerate(VELOCITY):
                if c[a] == 1:
                    m = f[i] if m is None else m + f[i]
            for i, c in enumerate(VELOCITY):
                if c[a] == -1:
                    m = m - f[i]
            u.append((m + 0.5 * force[a]) * inv)
        ready = [part.own(setup.at[n]) for n in range(SETUP)]
        nu, fbar, rho_bar = adjoint_finish(ready, u, force, inv, solid)
        local = rho_bar + part.near(e2_ext) * (
            5.0 * (pull[0] * fbar[0] + pull[1] * fbar[1] + pull[2] * fbar[2])
        )
        part.keep(density_out.at[1], local)
        nu[0] = nu[0] + local
        for i, v in enumerate(moments_t(nu)):
            part.put(base_ext.at[i], roll_z(v, -VELOCITY[i][2]))
        spread_out(fbar, psi, part)

    each_row(backward_second, 2, H - 2)
    finish(second, ACROSS)
    for k in ACROSS:
        unpack(r2, k, 0, post_ext.at[chosen(DIRS[k], 1)[0]])
        add_arrived(r2, sum_ext, k, True, True, 1)
    for x in (0, 1, H, H + 1):
        potential(x)
    third = {}
    for pair, ends in ((PAIR_A, ENDS_A), (PAIR_B, ENDS_B)):
        for x, y in ends:
            backward_second(Row(x, y, B // 2))
            backward_second(Row(1 if x == 0 else H - 2, y, B // 2))
        for k in pair:
            pack(s3, k, 0, base_ext.at[chosen(DIRS[k], -1)[0]])
            put_corner(s3, k, 1, q_ext)
        third.update(start(3, 7, 8, pair))
    for k in BESIDE:
        d = DIRS[k]
        for n, i in enumerate(chosen(d, -1)):
            pack(s3, k, n, base_ext.at[i])
        put_lines(s3, k, 5, lines_towards(q_ext, d))
    third.update(start(3, 7, 8, BESIDE))
    own_sum(q_ext, sum_ext)
    finish(third, BESIDE)
    for k in BESIDE:
        for n, i in enumerate(chosen(DIRS[k], -1)):
            unpack(r3, k, n, base_ext.at[i])
        add_arrived(r3, sum_ext, k, *get_lines(r3, k, 5, 2), 5)

    def shift_second(x):
        v = e2_ext[x, used, :] * sum_ext[x, used, :]
        for c in (-1, 0, 1):
            d_ext[c + 1, x, used, :] = roll_z(v, -c)

    for x in range(2, H):
        shift_second(x)
    finish(third, ACROSS)
    for k in ACROSS:
        unpack(r3, k, 0, base_ext.at[chosen(DIRS[k], -1)[0]])
        add_arrived(r3, sum_ext, k, True, True, 1)
    for x in (0, 1, H, H + 1):
        shift_second(x)

    def backward_first(part):
        solid = part.own(mask) == 1
        inv, psi = part.own(state.at[0]), part.own(state.at[10])
        u = [part.own(state.at[1 + a]) for a in AXES]
        force = [part.own(state.at[4 + a]) for a in AXES]
        lam = [
            part.near(base_ext.at[i], c[0], c[1]) + part.near(d_ext.at[c[2] + 1], c[0], c[1])
            for i, c in enumerate(VELOCITY)
        ]
        nu, fbar, rho_bar = adjoint_finish(adjoint_setup(lam, solid, rate), u, force, inv, solid)
        spread_out(fbar, psi, part)
        if isinstance(part, Column):
            return
        pull = [part.own(state.at[7 + a]) for a in AXES]
        local = rho_bar + part.own(state.at[11]) * (
            5.0 * (pull[0] * fbar[0] + pull[1] * fbar[1] + pull[2] * fbar[2])
        )
        part.keep(density_out.at[0], local)
        nu[0] = nu[0] + local
        for i, v in enumerate(moments_t(nu)):
            part.keep(base_out.at[i], v)

    last = {}
    for pair, ends in ((PAIR_A, ENDS_A), (PAIR_B, ENDS_B)):
        for x, y in ends:
            backward_first(Row(x, y, B // 2))
        for k in pair:
            pack(s4, k, 0, q_ext.at[SLOT[DIRS[k]]])
        last.update(start(4, 1, 0, pair))
    for y in (0, B - 1):
        backward_first(Column(y))
    for k in BESIDE:
        put_lines(s4, k, 0, lines_towards(q_ext, DIRS[k])[:1], False)
    last.update(start(4, 1, 0, BESIDE))

    def spread_second(part):
        total = part.near(sum_ext)
        part.keep(density_out.at[1], part.own(density_out.at[1]) + part.near(d_ext.at[1]))
        part.keep(wet_out, jnp.where(part.own(mask) == 1, total, 0.0))

    each_row(spread_second)
    each_row(backward_first, 1, H - 1)
    own_sum(q_ext, sum_ext, False)
    finish(last, BESIDE)
    for k in BESIDE:
        add_arrived(r4, sum_ext, k, get_lines(r4, k, 0, 1, False)[0], None, 0)

    def spread_first(part):
        total = part.near(sum_ext)
        change = part.own(state.at[11]) * total
        part.keep(density_out.at[0], part.own(density_out.at[0]) + change)
        part.keep(wet_out, part.own(wet_out) + jnp.where(part.own(mask) == 1, total, 0.0))
        for i in range(19):
            part.keep(base_out.at[i], part.own(base_out.at[i]) + change)

    each_row(spread_first, 1, H - 1)
    finish(last, ACROSS)
    for k in ACROSS:
        add_arrived(r4, sum_ext, k, r4[k, 0:1, :], None, 0)
    for x in (0, H - 1):
        spread_first(Row(x))


def closing(adjoint, density, wet, adjoint_hbm, density_hbm, wet_hbm, sems):
    copies = [
        pltpu.make_async_copy(adjoint.at[pl.ds(n, 4 if n < 16 else 3)], adjoint_hbm.at[pl.ds(n, 4 if n < 16 else 3)], sems.at[n // 4])
        for n in range(0, 19, 4)
    ]
    copies.append(pltpu.make_async_copy(density, density_hbm, sems.at[10]))
    copies.append(pltpu.make_async_copy(wet, wet_hbm, sems.at[11]))
    for c in copies:
        c.start()
    for c in copies:
        c.wait()


def body(populations, solid_mask, wall_class, wall_table, relax_rates, pop_cotangent):
    f32 = jnp.float32
    nx, ny = lax.axis_size("gx"), lax.axis_size("gy")
    block = (H, B, Z)
    ext = (H + 2, WIDE, Z)
    anywhere = pl.BlockSpec(memory_space=pl.ANY)
    vmem = pltpu.VMEM
    far = [
        pltpu.with_memory_space_constraint(v, pltpu.HBM)
        for v in (wall_table, relax_rates, populations, solid_mask, wall_class, pop_cotangent)
    ]
    results = pl.pallas_call(
        functools.partial(kernel, nx, ny),
        out_shape=(
            vmem((19,) + block, f32),
            vmem((2,) + block, f32),
            vmem(block, f32),
        ),
        in_specs=[anywhere] * 6,
        out_specs=(pl.BlockSpec(memory_space=vmem),) * 3,
        scratch_shapes=[
            pltpu.SMEM((8,), f32),
            pltpu.SMEM((19,), f32),
            vmem((19, H, TALL, Z), f32),
            vmem((19,) + block, f32),
            vmem((H, TALL, Z), jnp.int32),
            vmem(block, jnp.int32),
            vmem((12, H, TALL, Z), f32),
            vmem((SETUP,) + block, f32),
            vmem(ext, f32), vmem(ext, f32), vmem(ext, f32), vmem(ext, f32), vmem(ext, f32),
            vmem((3,) + ext, f32),
            vmem((9,) + ext, f32),
            vmem((19,) + ext, f32),
            vmem((19,) + ext, f32),
            vmem((19,) + ext, f32),
        ]
        + [vmem((8, n, Z), f32) for n in ROWS] * 2
        + [
            pltpu.SemaphoreType.DMA((5, 8)),
            pltpu.SemaphoreType.DMA((5, 8)),
            pltpu.SemaphoreType.DMA((6,)),
        ],
        compiler_params=pltpu.CompilerParams(
            collective_id=0, has_side_effects=True, vmem_limit_bytes=40 * 2**20
        ),
    )(*far)
    return pl.pallas_call(
        closing,
        out_shape=tuple(jax.ShapeDtypeStruct(v.shape, f32) for v in results),
        in_specs=[pl.BlockSpec(memory_space=vmem)] * 3,
        out_specs=(anywhere,) * 3,
        scratch_shapes=[pltpu.SemaphoreType.DMA((12,))],
        compiler_params=pltpu.CompilerParams(vmem_limit_bytes=8 * 2**20),
    )(*results)


def solution(mesh):
    in_specs = (
        P(None, "gx", "gy", None),
        P("gx", "gy", None),
        P("gx", "gy", None),
        P(),
        P(),
        P(None, "gx", "gy", None),
    )
    out_specs = (P(None, "gx", "gy", None), P(None, "gx", "gy", None), P("gx", "gy", None))
    return jax.shard_map(body, mesh=mesh, in_specs=in_specs, out_specs=out_specs, check_vma=False)
```

```python
import functools

import jax
import jax.numpy as jnp
from jax import lax
from jax.experimental import pallas as pl
from jax.experimental.pallas import tpu as pltpu
from jax.sharding import PartitionSpec as P

MESH = pl.DeviceIdType.MESH
VELOCITY = [
    (0, 0, 0),
    (1, 0, 0), (-1, 0, 0), (0, 1, 0), (0, -1, 0), (0, 0, 1), (0, 0, -1),
    (1, 1, 0), (-1, -1, 0), (1, -1, 0), (-1, 1, 0),
    (1, 0, 1), (-1, 0, -1), (1, 0, -1), (-1, 0, 1),
    (0, 1, 1), (0, -1, -1), (0, 1, -1), (0, -1, 1),
]
FACE_W, EDGE_W = 1.0 / 18.0, 1.0 / 36.0
AXES = (0, 1, 2)
PAIRS = ((0, 1), (0, 2), (1, 2))
H, B, Z = 8, 16, 128
CROSS = {(0, 1): 4, (0, 2): 5, (1, 2): 6}
QUAD = {(0, 1): 16, (0, 2): 17, (1, 2): 18}
CUBIC = {(0, 1): 10, (0, 2): 11, (1, 0): 12, (1, 2): 13, (2, 0): 14, (2, 1): 15}
EDGE = {(0, 1): 7, (0, 2): 11, (1, 2): 15}
ODD = (1, 2, 3, 10, 11, 12, 13, 14, 15)
OTHERS = {0: (1, 2), 1: (0, 2), 2: (0, 1)}
DIRS = ((-1, -1), (1, 1), (-1, 1), (1, -1), (-1, 0), (1, 0), (0, -1), (0, 1))
CLASSES = [(a, b) for a in (-1, 0, 1) for b in (-1, 0, 1)]
ACROSS, BESIDE = range(4), range(4, 8)
PAIR_A, PAIR_B = range(2), range(2, 4)
ENDS_A, ENDS_B = ((0, 0), (H - 1, B // 2)), ((0, B // 2), (H - 1, 0))
SLOT = {c: n for n, c in enumerate(CLASSES)}
MEMBERS = {c: [i for i, v in enumerate(VELOCITY) if v[:2] == c] for c in CLASSES}
WIDE, TALL = 40, 24
Y0, Y1 = 8, 24
MID = slice(Y0, Y1)
ROWS = (16, 112, 104, 120, 16)


def quad(a, b):
    return QUAD[(min(a, b), max(a, b))]


def cross(a, b):
    return CROSS[(min(a, b), max(a, b))]


def roll_z(v, shift):
    return v if shift == 0 else pltpu.roll(v, shift % Z, v.ndim - 1)


def moments(f):
    m = [None] * 19
    s = [f[1 + 2 * a] + f[2 + 2 * a] for a in AXES]
    d = [f[1 + 2 * a] - f[2 + 2 * a] for a in AXES]
    for a, b in PAIRS:
        e = EDGE[a, b]
        al, ad = f[e] + f[e + 1], f[e] - f[e + 1]
        be, bd = f[e + 2] + f[e + 3], f[e + 2] - f[e + 3]
        m[CROSS[a, b]] = al - be
        m[QUAD[a, b]] = al + be
        m[CUBIC[a, b]] = ad + bd
        m[CUBIC[b, a]] = ad - bd
    for a in AXES:
        b, c = OTHERS[a]
        m[1 + a] = d[a] + (m[CUBIC[a, b]] + m[CUBIC[a, c]])
        m[7 + a] = s[a] + (m[quad(a, b)] + m[quad(a, c)])
    m[0] = (f[0] + s[0]) + (s[1] + s[2]) + (m[16] + m[17] + m[18])
    return m


def from_moments(p):
    f = [None] * 19
    for a in AXES:
        b, c = OTHERS[a]
        s = 0.5 * (p[7 + a] - (p[quad(a, b)] + p[quad(a, c)]))
        d = 0.5 * (p[1 + a] - (p[CUBIC[a, b]] + p[CUBIC[a, c]]))
        f[1 + 2 * a], f[2 + 2 * a] = s + d, s - d
    for a, b in PAIRS:
        e = EDGE[a, b]
        q, r = 0.25 * p[QUAD[a, b]], 0.25 * p[CROSS[a, b]]
        t, w = 0.25 * p[CUBIC[a, b]], 0.25 * p[CUBIC[b, a]]
        up, down, plus, minus = q + r, q - r, t + w, t - w
        f[e], f[e + 1], f[e + 2], f[e + 3] = up + plus, up - plus, down + minus, down - minus
    f[0] = p[0] - (p[7] + p[8] + p[9]) + (p[16] + p[17] + p[18])
    return f


def from_moments_t(lam):
    mu = [None] * 19
    mu[0] = lam[0]
    s = [0.5 * (lam[1 + 2 * a] + lam[2 + 2 * a]) for a in AXES]
    d = [0.5 * (lam[1 + 2 * a] - lam[2 + 2 * a]) for a in AXES]
    for a in AXES:
        mu[1 + a] = d[a]
        mu[7 + a] = s[a] - lam[0]
    for a, b in PAIRS:
        e = EDGE[a, b]
        al, ad = lam[e] + lam[e + 1], lam[e] - lam[e + 1]
        be, bd = lam[e + 2] + lam[e + 3], lam[e + 2] - lam[e + 3]
        mu[QUAD[a, b]] = 0.25 * (al + be) - s[a] - mu[7 + b]
        mu[CROSS[a, b]] = 0.25 * (al - be)
        mu[CUBIC[a, b]] = 0.25 * (ad + bd) - d[a]
        mu[CUBIC[b, a]] = 0.25 * (ad - bd) - d[b]
    return mu


def moments_t(nu):
    f = [None] * 19
    f[0] = nu[0]
    for a in AXES:
        s = nu[0] + nu[7 + a]
        f[1 + 2 * a], f[2 + 2 * a] = s + nu[1 + a], s - nu[1 + a]
    for a, b in PAIRS:
        e = EDGE[a, b]
        even = (nu[0] + nu[7 + a]) + (nu[7 + b] + nu[QUAD[a, b]])
        up, down = even + nu[CROSS[a, b]], even - nu[CROSS[a, b]]
        p, q = nu[1 + a] + nu[CUBIC[a, b]], nu[1 + b] + nu[CUBIC[b, a]]
        f[e], f[e + 1], f[e + 2], f[e + 3] = up + (p + q), up - (p + q), down + (p - q), down - (p - q)
    return f


def collide(f, psi, pull, inv, solid, rate):
    m = moments(f)
    rho = m[0]
    force = [5.0 * psi * g for g in pull]
    u = [(m[1 + a] + 0.5 * force[a]) * inv for a in AXES]
    n = [m[1 + a] - 0.5 * force[a] for a in AXES]
    p = [None] * 19
    p[0] = rho
    w = [u[a] * n[a] for a in AXES]
    t = [u[a] * force[a] for a in AXES]
    third = rho * (1.0 / 3.0)
    ninth = rho * (1.0 / 9.0)
    for a in AXES:
        p[1 + a] = m[1 + a] + force[a]
        k = 7 + a
        p[k] = m[k] + rate[k] * (third + w[a] - m[k]) + 2.0 * t[a]
    m3 = [m[1 + a] * (1.0 / 3.0) for a in AXES]
    f3 = [force[a] * (1.0 / 3.0) for a in AXES]
    for (a, b), k in CUBIC.items():
        p[k] = m[k] + rate[k] * (m3[a] - m[k]) + f3[a]
    w3 = [(1.0 / 3.0) * v for v in w]
    t3 = [(1.0 / 3.0) * v for v in t]
    for a, b in PAIRS:
        c = 3 - a - b
        k = CROSS[a, b]
        p[k] = m[k] + rate[k] * (0.5 * (u[b] * n[a] + u[a] * n[b]) - m[k]) + (u[a] * force[b] + u[b] * force[a])
        k = QUAD[a, b]
        p[k] = (
            m[k]
            + rate[k] * (ninth + (w3[a] + w3[b]) - 0.5 * w3[c] - m[k])
            + (2.0 * (t3[a] + t3[b]) - t3[c])
        )
    for k in range(1, 19):
        p[k] = jnp.where(solid, -m[k] if k in ODD else m[k], p[k])
    return from_moments(p), u, force


def adjoint_setup(lam, solid, rate):
    mu = from_moments_t(lam)
    e, nu, g = [None] * 19, [None] * 19, [None] * 19
    for k in (0,) + tuple(range(4, 19)):
        e[k] = rate[k] * mu[k]
        nu[k] = jnp.where(solid, -mu[k] if k in ODD else mu[k], mu[k] - e[k])
        g[k] = mu[k] - 0.5 * e[k]

    def diagonal(v):
        out = []
        for a in AXES:
            b, c = OTHERS[a]
            out.append(2.0 * v[7 + a] + (2.0 / 3.0) * (v[quad(a, b)] + v[quad(a, c)]) - (1.0 / 3.0) * v[quad(b, c)])
        return out

    def thirds(v):
        return [(1.0 / 3.0) * (v[CUBIC[a, OTHERS[a][0]]] + v[CUBIC[a, OTHERS[a][1]]]) for a in AXES]

    level = (
        e[0]
        + (1.0 / 3.0) * (e[7] + e[8] + e[9])
        + (1.0 / 9.0) * (e[16] + e[17] + e[18])
    )
    lift = [mu[1 + a] + v for a, v in enumerate(thirds(g))]
    return [nu[0]] + nu[4:] + mu[1:4] + diagonal(e) + e[4:7] + diagonal(g) + g[4:7] + thirds(e) + lift + [level]


SETUP = 38


def adjoint_finish(setup, u, force, inv, solid):
    nu = [setup[0], None, None, None] + list(setup[1:16])
    mu, ed, ec, gd, gc, push, lift = (setup[n : n + 3] for n in range(16, 37, 3))
    level = setup[37]

    def times(diag, off, x):
        out = []
        for a in AXES:
            b, c = OTHERS[a]
            out.append(diag[a] * x[a] + off[cross(a, b) - 4] * x[b] + off[cross(a, c) - 4] * x[c])
        return out

    eu, gu, gf = times(ed, ec, u), times(gd, gc, u), times(gd, gc, force)
    fbar = []
    for a in AXES:
        jbar = push[a] + eu[a] + gf[a] * inv
        nu[1 + a] = jnp.where(solid, -mu[a], mu[a] + jbar)
        fbar.append(jnp.where(solid, 0.0, lift[a] + gu[a] + 0.5 * jbar))
    rho_bar = (
        level
        - 0.5 * (u[0] * eu[0] + u[1] * eu[1] + u[2] * eu[2])
        - (force[0] * gu[0] + force[1] * gu[1] + force[2] * gu[2]) * inv
    )
    return nu, fbar, jnp.where(solid, 0.0, rho_bar)


class Row:
    def __init__(self, x, first=0, count=B):
        self.x, self.first, self.count = x, first, count

    def near(self, ext, a=0, b=0):
        y = Y0 + self.first + b
        return ext[self.x + 1 + a, y : y + self.count, :]

    def put(self, ext, v):
        y = Y0 + self.first
        ext[self.x + 1, y : y + self.count, :] = v

    def own(self, ref):
        return ref[self.x, self.first : self.first + self.count, :]

    def keep(self, ref, v):
        ref[self.x, self.first : self.first + self.count, :] = v


class Column:
    def __init__(self, y):
        self.y = y

    def near(self, ext, a=0, b=0):
        return flat(ext)[strip(Y0 + self.y + b, a), :]

    def put(self, ext, v):
        flat(ext)[strip(Y0 + self.y), :] = v

    def own(self, ref):
        return ref.reshape(H * TALL, Z)[pl.ds(self.y, H, stride=TALL), :]

    def keep(self, ref, v):
        ref.reshape(H * TALL, Z)[pl.ds(self.y, H, stride=TALL), :] = v


def neighbour_pull(ext, part):
    at = {(a, b): part.near(ext, a, b) for a, b in CLASSES}
    dx, dy = at[1, 0] - at[-1, 0], at[0, 1] - at[0, -1]
    main, other = at[1, 1] - at[-1, -1], at[1, -1] - at[-1, 1]
    total = FACE_W * at[0, 0] + EDGE_W * ((at[1, 0] + at[-1, 0]) + (at[0, 1] + at[0, -1]))
    gx = FACE_W * dx + EDGE_W * (main + other + (roll_z(dx, 1) + roll_z(dx, -1)))
    gy = FACE_W * dy + EDGE_W * (main - other + (roll_z(dy, 1) + roll_z(dy, -1)))
    return [gx, gy, roll_z(total, -1) - roll_z(total, 1)]


def spread_classes(p):
    px, py, pz = p
    up, down = roll_z(pz, 1), roll_z(pz, -1)
    turned = [EDGE_W * (roll_z(v, 1) + roll_z(v, -1)) + FACE_W * v for v in (px, py)]
    lift = EDGE_W * (up - down)
    both, apart = EDGE_W * (px + py), EDGE_W * (px - py)
    return {
        (0, 0): FACE_W * (up - down),
        (1, 0): turned[0] + lift, (-1, 0): lift - turned[0],
        (0, 1): turned[1] + lift, (0, -1): lift - turned[1],
        (1, 1): both, (-1, -1): -both, (1, -1): apart, (-1, 1): -apart,
    }


def chosen(d, orient):
    return [i for i, v in enumerate(VELOCITY) if all(d[n] == 0 or v[n] == orient * d[n] for n in (0, 1))]


def edge_of(d):
    return (1 if d[0] < 0 else H), (Y0 if d[1] < 0 else Y1 - 1)


def halo_of(d):
    return (0 if d[0] < 0 else H + 1), (Y0 - 1 if d[1] < 0 else Y1)


def strip(y, shift=0):
    return pl.ds((1 + shift) * WIDE + y, H, stride=WIDE)


def flat(ext):
    return ext.reshape((H + 2) * WIDE, Z)


def pack(sb, k, place, ext):
    d = DIRS[k]
    ex, ey = edge_of(d)
    if d[1] == 0:
        sb[k, place * B : (place + 1) * B, :] = ext[ex, MID, :]
    elif d[0] == 0:
        sb[k, place * H : (place + 1) * H, :] = flat(ext)[strip(ey), :]
    else:
        sb[k, place : place + 1, :] = ext[ex, ey : ey + 1, :]


def unpack(rb, k, place, ext):
    d = DIRS[k]
    hx, hy = halo_of((-d[0], -d[1]))
    if d[1] == 0:
        ext[hx, MID, :] = rb[k, place * B : (place + 1) * B, :]
    elif d[0] == 0:
        flat(ext)[strip(hy), :] = rb[k, place * H : (place + 1) * H, :]
    else:
        ext[hx, hy : hy + 1, :] = rb[k, place : place + 1, :]


def shifted(v, step):
    rows = v.shape[0]
    index = lax.broadcasted_iota(jnp.int32, v.shape, 0)
    return jnp.where(index == (0 if step > 0 else rows - 1), 0.0, pltpu.roll(v, step % rows, 0))


def line(t):
    size = t[0].shape[0]
    return t[0] + shifted(t[1], 1) + shifted(t[-1], -1), t[-1][0:1, :], t[1][size - 1 : size, :]


def size_of(d):
    return B if d[1] == 0 else H


def lines_towards(q, d):
    ex, ey = edge_of(d)
    if d[1] == 0:
        outer = {c: q[SLOT[d[0], c], ex, MID, :] for c in (-1, 0, 1)}
        behind = {c: q[SLOT[0, c], ex, MID, :] + q[SLOT[d[0], c], ex - d[0], MID, :] for c in (-1, 0, 1)}
    else:
        def column(c, y):
            return flat(q.at[SLOT[c]])[strip(y), :]

        outer = {c: column((c, d[1]), ey) for c in (-1, 0, 1)}
        behind = {c: column((c, 0), ey) + column((c, d[1]), ey - d[1]) for c in (-1, 0, 1)}
    return line(outer), line(behind)


def put_lines(sb, k, fields, lines, ends=True):
    s = size_of(DIRS[k])
    at = fields * s
    for n, (middle, low, high) in enumerate(lines):
        sb[k, at + n * s : at + (n + 1) * s, :] = middle
        if ends:
            e = at + len(lines) * s + 2 * n
            sb[k, e : e + 1, :] = low
            sb[k, e + 1 : e + 2, :] = high


def get_lines(rb, k, fields, count, ends=True):
    s = size_of(DIRS[k])
    at = fields * s
    out = []
    for n in range(count):
        e = at + count * s + 2 * n
        low, high = (rb[k, e : e + 1, :], rb[k, e + 1 : e + 2, :]) if ends else (None, None)
        out.append((rb[k, at + n * s : at + (n + 1) * s, :], low, high))
    return out


def put_corner(sb, k, place, q):
    dx, dy = DIRS[k]
    ex, ey = edge_of((dx, dy))

    def one(c, x, y):
        return q[SLOT[c], x, y : y + 1, :]

    across = (dx, dy)
    values = (
        one((0, 0), ex, ey) + one((dx, 0), ex - dx, ey) + one((0, dy), ex, ey - dy) + one(across, ex - dx, ey - dy),
        one((dx, 0), ex, ey) + one(across, ex, ey - dy),
        one((0, dy), ex, ey) + one(across, ex - dx, ey),
        one(across, ex, ey),
    )
    for n, v in enumerate(values):
        sb[k, place + n : place + n + 1, :] = v


def own_sum(q, out, border=True):
    for x in range(0 if border else 1, H + 2 if border else H + 1):
        total = None
        for c in CLASSES:
            if 1 <= x - c[0] <= H:
                v = q[SLOT[c], x - c[0], Y0 - c[1] : Y1 - c[1], :]
                total = v if total is None else total + v
        out[x, MID, :] = total
    if not border:
        return
    for d in DIRS:
        ex, ey = edge_of(d)
        hx, hy = halo_of(d)
        if d[0] == 0:
            total = None
            for c in (-1, 0, 1):
                v = flat(q.at[SLOT[c, d[1]]])[strip(ey, -c), :]
                total = v if total is None else total + v
            flat(out)[strip(hy), :] = total
        elif d[1] != 0:
            out[hx, hy : hy + 1, :] = q[SLOT[d], ex, ey : ey + 1, :]


def add_line(out, d, at, middle, low, high):
    if d[1] == 0:
        out[at, MID, :] += middle
        if low is not None:
            out[at, Y0 - 1 : Y0, :] += low
            out[at, Y1 : Y1 + 1, :] += high
    else:
        flat(out)[strip(at), :] += middle
        if low is not None:
            out[0, at : at + 1, :] += low
            out[H + 1, at : at + 1, :] += high


def add_arrived(rb, out, k, into, behind, fields):
    d = DIRS[k]
    back = (-d[0], -d[1])
    ex, ey = edge_of(back)
    hx, hy = halo_of(back)
    if d[0] == 0 or d[1] == 0:
        n = 1 if d[0] == 0 else 0
        add_line(out, d, (ex, ey)[n], *into)
        if behind is not None:
            add_line(out, d, (hx, hy)[n], *behind)
    elif behind is None:
        out[ex, ey : ey + 1, :] += into
    else:
        for n, (x, y) in enumerate(((hx, hy), (ex, hy), (hx, ey), (ex, ey))):
            out[x, y : y + 1, :] += rb[k, fields + n : fields + n + 1, :]


def kernel(
    nx, ny,
    table_hbm, rates_hbm, pops_hbm, mask_hbm, class_hbm, cot_hbm, base_out, density_out, wet_out,
    table, rates, pops, cot, mask, wall_class, state, setup,
    psi_ext, solid_ext, wall_ext, e2_ext, sum_ext, d_ext, q_ext, cot_ext, post_ext, base_ext,
    s0, s1, s2, s3, s4, r0, r1, r2, r3, r4,
    send_sem, recv_sem, local_sem,
):
    gx, gy = lax.axis_index("gx"), lax.axis_index("gy")
    sends, recvs = (s0, s1, s2, s3, s4), (r0, r1, r2, r3, r4)

    def device(d):
        return (lax.rem(gx + (d[0] + nx), nx), lax.rem(gy + (d[1] + ny), ny))

    barrier = pltpu.get_barrier_semaphore()
    for d in DIRS:
        pl.semaphore_signal(barrier, inc=1, device_id=device(d), device_id_type=MESH)

    loads = [
        pltpu.make_async_copy(src, dst, local_sem.at[n])
        for n, (src, dst) in enumerate(
            ((pops_hbm, pops.at[:, :, pl.ds(0, B)]), (mask_hbm, mask.at[:, pl.ds(0, B)]), (class_hbm, wall_class), (table_hbm, table), (rates_hbm, rates), (cot_hbm, cot))
        )
    ]
    for c in loads:
        c.start()

    def start(r, fields, ends=0, which=range(8)):
        copies = {}
        for k in which:
            d = DIRS[k]
            rows = pl.ds(0, fields * size_of(d) + ends if d[0] == 0 or d[1] == 0 else 8)
            c = pltpu.make_async_remote_copy(
                src_ref=sends[r].at[k, rows], dst_ref=recvs[r].at[k, rows],
                send_sem=send_sem.at[r, k], recv_sem=recv_sem.at[r, k],
                device_id=device(d), device_id_type=MESH,
            )
            c.start()
            copies[k] = c
        return copies

    def finish(copies, which=range(8)):
        for k in which:
            copies[k].wait()

    def each_row(body, first=0, last=H):
        def step(x, carry):
            body(Row(x))
            return carry

        lax.fori_loop(first, last, step, 0, unroll=last - first)

    def clear(x, carry):
        for n in range(9):
            q_ext[n, x] = jnp.zeros((WIDE, Z), jnp.float32)
        return carry

    lax.fori_loop(0, H + 2, clear, 0)

    for c in loads[:5]:
        c.wait()
    rate = [rates[k] for k in range(19)]

    def prepare(part):
        f = [part.own(pops.at[i]) for i in range(19)]
        rho = f[0]
        for i in range(1, 19):
            rho = rho + f[i]
        solid = part.own(mask) == 1
        kind = part.own(wall_class)
        wall = jnp.full(rho.shape, table[0], jnp.float32)
        for n in range(1, 8):
            wall = jnp.where(kind == n, table[n], wall)
        fade = jnp.exp(-rho)
        part.put(psi_ext, jnp.where(solid, wall, 1.0 - fade))
        part.put(solid_ext, jnp.where(solid, 1.0, 0.0))
        part.put(wall_ext, wall)
        part.keep(state.at[0], 1.0 / rho)
        part.keep(state.at[11], jnp.where(solid, 0.0, fade))

    each_row(prepare)
    for k in range(8):
        pack(s0, k, 0, psi_ext)
    pl.semaphore_wait(barrier, len(DIRS))
    first = start(0, 1)

    loads[5].wait()

    def turn(part):
        for i, c in enumerate(VELOCITY):
            part.put(cot_ext.at[i], roll_z(part.own(cot.at[i]), -c[2]))

    each_row(turn)
    for k, d in enumerate(DIRS):
        ids = chosen(d, -1)
        for n, i in enumerate(ids):
            pack(s1, k, n, cot_ext.at[i])
        pack(s1, k, len(ids), solid_ext)
        pack(s1, k, len(ids) + 1, wall_ext)
    early = start(1, 7)

    def forward(part):
        psi = part.near(psi_ext)
        pull = neighbour_pull(psi_ext, part)
        f = [part.own(pops.at[i]) for i in range(19)]
        post, u, force = collide(f, psi, pull, part.own(state.at[0]), part.own(mask) == 1, rate)
        post = [roll_z(v, c[2]) for v, c in zip(post, VELOCITY)]
        for i in range(19):
            part.put(post_ext.at[i], post[i])
        for c in CLASSES:
            total = post[MEMBERS[c][0]]
            for i in MEMBERS[c][1:]:
                total = total + post[i]
            part.put(q_ext.at[SLOT[c]], total)
        for a in AXES:
            part.keep(state.at[1 + a], u[a])
            part.keep(state.at[4 + a], force[a])
            part.keep(state.at[7 + a], pull[a])
        part.keep(state.at[10], psi)

    each_row(forward, 1, H - 1)
    finish(first, BESIDE)
    for k in BESIDE:
        unpack(r0, k, 0, psi_ext)
    for part in (Column(0), Column(B - 1)):
        forward(part)
    second = {}
    for pair, ends in ((PAIR_A, ENDS_A), (PAIR_B, ENDS_B)):
        finish(first, pair)
        for k in pair:
            unpack(r0, k, 0, psi_ext)
        for x, y in ends:
            forward(Row(x, y, B // 2))
        for k in pair:
            pack(s2, k, 0, post_ext.at[chosen(DIRS[k], 1)[0]])
            put_corner(s2, k, 1, q_ext)
        second.update(start(2, 6, 8, pair))
    for k in BESIDE:
        d = DIRS[k]
        for n, i in enumerate(chosen(d, 1)):
            pack(s2, k, n, post_ext.at[i])
        put_lines(s2, k, 5, lines_towards(q_ext, d)[1:])
    second.update(start(2, 6, 8, BESIDE))

    own_sum(q_ext, sum_ext)
    finish(early)
    for k, d in enumerate(DIRS):
        ids = chosen(d, -1)
        for n, i in enumerate(ids):
            unpack(r1, k, n, cot_ext.at[i])
        unpack(r1, k, len(ids), solid_ext)
        unpack(r1, k, len(ids) + 1, wall_ext)

    def prepare_adjoint(part):
        lam = [part.near(cot_ext.at[i], c[0], c[1]) for i, c in enumerate(VELOCITY)]
        for n, v in enumerate(adjoint_setup(lam, part.own(mask) == 1, rate)):
            part.keep(setup.at[n], v)

    each_row(prepare_adjoint)
    finish(second, BESIDE)

    for k in BESIDE:
        d = DIRS[k]
        ids = chosen(d, 1)
        for n, i in enumerate(ids):
            unpack(r2, k, n, post_ext.at[i])
        s = size_of(d)
        parts = {}
        for n, i in enumerate(ids):
            c = VELOCITY[i][1 if d[1] == 0 else 0]
            v = r2[k, n * s : (n + 1) * s, :]
            parts[c] = parts[c] + v if c in parts else v
        add_arrived(r2, sum_ext, k, line(parts), get_lines(r2, k, 5, 1)[0], 5)

    used = slice(0, 32)

    def potential(x):
        solid = solid_ext[x, used, :] > 0.5
        fade = jnp.exp(-sum_ext[x, used, :])
        psi_ext[x, used, :] = jnp.where(solid, wall_ext[x, used, :], 1.0 - fade)
        e2_ext[x, used, :] = jnp.where(solid, 0.0, fade)

    for x in range(2, H):
        potential(x)

    def spread_out(fbar, psi, part):
        p = [5.0 * psi * v for v in fbar]
        for c, v in spread_classes(p).items():
            part.put(q_ext.at[SLOT[c]], v)

    def backward_second(part):
        inv = 1.0 / part.near(sum_ext)
        psi = part.near(psi_ext)
        solid = part.own(mask) == 1
        pull = neighbour_pull(psi_ext, part)
        force = [5.0 * psi * g for g in pull]
        f = [part.near(post_ext.at[i], -c[0], -c[1]) for i, c in enumerate(VELOCITY)]
        u = []
        for a in AXES:
            m = None
            for i, c in enumerate(VELOCITY):
                if c[a] == 1:
                    m = f[i] if m is None else m + f[i]
            for i, c in enumerate(VELOCITY):
                if c[a] == -1:
                    m = m - f[i]
            u.append((m + 0.5 * force[a]) * inv)
        ready = [part.own(setup.at[n]) for n in range(SETUP)]
        nu, fbar, rho_bar = adjoint_finish(ready, u, force, inv, solid)
        local = rho_bar + part.near(e2_ext) * (
            5.0 * (pull[0] * fbar[0] + pull[1] * fbar[1] + pull[2] * fbar[2])
        )
        part.keep(density_out.at[1], local)
        nu[0] = nu[0] + local
        for i, v in enumerate(moments_t(nu)):
            part.put(base_ext.at[i], roll_z(v, -VELOCITY[i][2]))
        spread_out(fbar, psi, part)

    each_row(backward_second, 2, H - 2)
    finish(second, ACROSS)
    for k in ACROSS:
        unpack(r2, k, 0, post_ext.at[chosen(DIRS[k], 1)[0]])
        add_arrived(r2, sum_ext, k, True, True, 1)
    for x in (0, 1, H, H + 1):
        potential(x)
    third = {}
    for pair, ends in ((PAIR_A, ENDS_A), (PAIR_B, ENDS_B)):
        for x, y in ends:
            backward_second(Row(x, y, B // 2))
            backward_second(Row(1 if x == 0 else H - 2, y, B // 2))
        for k in pair:
            pack(s3, k, 0, base_ext.at[chosen(DIRS[k], -1)[0]])
            put_corner(s3, k, 1, q_ext)
        third.update(start(3, 7, 8, pair))
    for k in BESIDE:
        d = DIRS[k]
        for n, i in enumerate(chosen(d, -1)):
            pack(s3, k, n, base_ext.at[i])
        put_lines(s3, k, 5, lines_towards(q_ext, d))
    third.update(start(3, 7, 8, BESIDE))
    own_sum(q_ext, sum_ext)
    finish(third, BESIDE)
    for k in BESIDE:
        for n, i in enumerate(chosen(DIRS[k], -1)):
            unpack(r3, k, n, base_ext.at[i])
        add_arrived(r3, sum_ext, k, *get_lines(r3, k, 5, 2), 5)

    def shift_second(x):
        v = e2_ext[x, used, :] * sum_ext[x, used, :]
        for c in (-1, 0, 1):
            d_ext[c + 1, x, used, :] = roll_z(v, -c)

    for x in range(2, H):
        shift_second(x)
    finish(third, ACROSS)
    for k in ACROSS:
        unpack(r3, k, 0, base_ext.at[chosen(DIRS[k], -1)[0]])
        add_arrived(r3, sum_ext, k, True, True, 1)
    for x in (0, 1, H, H + 1):
        shift_second(x)

    def backward_first(part):
        solid = part.own(mask) == 1
        inv, psi = part.own(state.at[0]), part.own(state.at[10])
        u = [part.own(state.at[1 + a]) for a in AXES]
        force = [part.own(state.at[4 + a]) for a in AXES]
        lam = [
            part.near(base_ext.at[i], c[0], c[1]) + part.near(d_ext.at[c[2] + 1], c[0], c[1])
            for i, c in enumerate(VELOCITY)
        ]
        nu, fbar, rho_bar = adjoint_finish(adjoint_setup(lam, solid, rate), u, force, inv, solid)
        spread_out(fbar, psi, part)
        if isinstance(part, Column):
            return
        pull = [part.own(state.at[7 + a]) for a in AXES]
        local = rho_bar + part.own(state.at[11]) * (
            5.0 * (pull[0] * fbar[0] + pull[1] * fbar[1] + pull[2] * fbar[2])
        )
        part.keep(density_out.at[0], local)
        nu[0] = nu[0] + local
        for i, v in enumerate(moments_t(nu)):
            part.keep(base_out.at[i], v)

    last = {}
    for pair, ends in ((PAIR_A, ENDS_A), (PAIR_B, ENDS_B)):
        for x, y in ends:
            backward_first(Row(x, y, B // 2))
        for k in pair:
            pack(s4, k, 0, q_ext.at[SLOT[DIRS[k]]])
        last.update(start(4, 1, 0, pair))
    for y in (0, B - 1):
        backward_first(Column(y))
    for k in BESIDE:
        put_lines(s4, k, 0, lines_towards(q_ext, DIRS[k])[:1], False)
    last.update(start(4, 1, 0, BESIDE))

    def spread_second(part):
        total = part.near(sum_ext)
        part.keep(density_out.at[1], part.own(density_out.at[1]) + part.near(d_ext.at[1]))
        part.keep(wet_out, jnp.where(part.own(mask) == 1, total, 0.0))

    each_row(spread_second)
    each_row(backward_first, 1, H - 1)
    own_sum(q_ext, sum_ext, False)
    finish(last, BESIDE)
    for k in BESIDE:
        add_arrived(r4, sum_ext, k, get_lines(r4, k, 0, 1, False)[0], None, 0)

    def spread_first(part):
        total = part.near(sum_ext)
        change = part.own(state.at[11]) * total
        part.keep(density_out.at[0], part.own(density_out.at[0]) + change)
        part.keep(wet_out, part.own(wet_out) + jnp.where(part.own(mask) == 1, total, 0.0))
        for i in range(19):
            part.keep(base_out.at[i], part.own(base_out.at[i]) + change)

    each_row(spread_first, 1, H - 1)
    finish(last, ACROSS)
    for k in ACROSS:
        add_arrived(r4, sum_ext, k, r4[k, 0:1, :], None, 0)
    for x in (0, H - 1):
        spread_first(Row(x))


def closing(adjoint, density, wet, adjoint_hbm, density_hbm, wet_hbm, sems):
    copies = [
        pltpu.make_async_copy(adjoint.at[pl.ds(n, 4 if n < 16 else 3)], adjoint_hbm.at[pl.ds(n, 4 if n < 16 else 3)], sems.at[n // 4])
        for n in range(0, 19, 4)
    ]
    copies.append(pltpu.make_async_copy(density, density_hbm, sems.at[10]))
    copies.append(pltpu.make_async_copy(wet, wet_hbm, sems.at[11]))
    for c in copies:
        c.start()
    for c in copies:
        c.wait()


def body(populations, solid_mask, wall_class, wall_table, relax_rates, pop_cotangent):
    f32 = jnp.float32
    nx, ny = lax.axis_size("gx"), lax.axis_size("gy")
    block = (H, B, Z)
    ext = (H + 2, WIDE, Z)
    anywhere = pl.BlockSpec(memory_space=pl.ANY)
    vmem = pltpu.VMEM
    far = [
        pltpu.with_memory_space_constraint(v, pltpu.HBM)
        for v in (wall_table, relax_rates, populations, solid_mask, wall_class, pop_cotangent)
    ]
    results = pl.pallas_call(
        functools.partial(kernel, nx, ny),
        out_shape=(
            vmem((19,) + block, f32),
            vmem((2,) + block, f32),
            vmem(block, f32),
        ),
        in_specs=[anywhere] * 6,
        out_specs=(pl.BlockSpec(memory_space=vmem),) * 3,
        scratch_shapes=[
            pltpu.SMEM((8,), f32),
            pltpu.SMEM((19,), f32),
            vmem((19, H, TALL, Z), f32),
            vmem((19,) + block, f32),
            vmem((H, TALL, Z), jnp.int32),
            vmem(block, jnp.int32),
            vmem((12, H, TALL, Z), f32),
            vmem((SETUP,) + block, f32),
            vmem(ext, f32), vmem(ext, f32), vmem(ext, f32), vmem(ext, f32), vmem(ext, f32),
            vmem((3,) + ext, f32),
            vmem((9,) + ext, f32),
            vmem((19,) + ext, f32),
            vmem((19,) + ext, f32),
            vmem((19,) + ext, f32),
        ]
        + [vmem((8, n, Z), f32) for n in ROWS] * 2
        + [
            pltpu.SemaphoreType.DMA((5, 8)),
            pltpu.SemaphoreType.DMA((5, 8)),
            pltpu.SemaphoreType.DMA((6,)),
        ],
        compiler_params=pltpu.CompilerParams(
            collective_id=0, has_side_effects=True, vmem_limit_bytes=40 * 2**20
        ),
    )(*far)
    return pl.pallas_call(
        closing,
        out_shape=tuple(jax.ShapeDtypeStruct(v.shape, f32) for v in results),
        in_specs=[pl.BlockSpec(memory_space=vmem)] * 3,
        out_specs=(anywhere,) * 3,
        scratch_shapes=[pltpu.SemaphoreType.DMA((12,))],
        compiler_params=pltpu.CompilerParams(vmem_limit_bytes=8 * 2**20),
    )(*results)


def solution(mesh):
    in_specs = (
        P(None, "gx", "gy", None),
        P("gx", "gy", None),
        P("gx", "gy", None),
        P(),
        P(),
        P(None, "gx", "gy", None),
    )
    out_specs = (P(None, "gx", "gy", None), P(None, "gx", "gy", None), P("gx", "gy", None))
    return jax.shard_map(body, mesh=mesh, in_specs=in_specs, out_specs=out_specs, check_vma=False)
```
